32 devices in a mesh: batch: 8 (over z, core), seq: 4 (over y, x).
Axes of the slice: x: 2, y: 2, z: 4, core: 2. Of those that a mesh axis runs over, the one named last changes fastest.
Arguments:
- tokens: bfloat16 [16, 2048, 768], P('batch', 'seq'), may hold values from -6 to 6
- history: bfloat16 [8, 16, 2048, 768], P(None, 'batch', 'seq'), may hold values from -6 to 6
- cotangent: bfloat16 [16, 2048, 768], P('batch', 'seq'), may hold values from -6 to 6
- qkv_weight: bfloat16 [768, 2304], replicated, may hold values from -0.21875 to 0.21875
- out_weight: bfloat16 [768, 768], replicated, may hold values from -3.5 to 3.5
- up_weight: bfloat16 [768, 3072], replicated, may hold values from -0.21875 to 0.21875
- down_weight: bfloat16 [3072, 768], replicated, may hold values from -0.109375 to 0.109375
- attn_gain: float32 [768], replicated, may hold values from 0.5 to 1.5
- mlp_gain: float32 [768], replicated, may hold values from 0.5 to 1.5
- depth_mix: float32 [9], replicated, may hold values from 0.1 to 0.6
- lengths: int32 [16], P('batch'), may hold values from 1 to 2048, as said below
- positions: int32 [16, 2048], P('batch', 'seq'), may hold values from 0 to 8189, as said below
Outputs:
- mixed_out: bfloat16 [16, 2048, 768], P('batch', 'seq')
- input_grad: bfloat16 [16, 2048, 768], P('batch', 'seq')
- history_grad: bfloat16 [8, 16, 2048, 768], P(None, 'batch', 'seq')
- qkv_grad: float32 [768, 2304], replicated
- out_grad: float32 [768, 768], replicated
- up_grad: float32 [768, 3072], replicated
- down_grad: float32 [3072, 768], replicated
- attn_gain_grad: float32 [768], replicated
- mlp_gain_grad: float32 [768], replicated
- mix_grad: float32 [9], replicated
The draws below stay inside these ranges and needn't reach their ends.
Inputs may be any that keep to these rules, and one draw needn't show every extreme that they name: `lengths`: each group of 2 sequences on one index of batch holds one sequence of full length. `positions`: within a sequence, each token's position exceeds the previous token's by 1 or 2; some sequence starts at 0 and some starts at 4095 and steps by 2 throughout.
All inputs are finite; a program needn't handle non-finite values.
Results may differ from the reference program's by a relative error of at most 0.015.
Values may be sent and summed in bfloat16 or wider, within the bound.
A program may use at most 384 MiB of HBM per device.

```python
import jax
import jax.numpy as jnp
from jax import lax

D = 768
H = 12
HD = 64
FF = 3072
SEQ_LEN = 2048
SEQS = 2
NHIST = 8
NSEQ = 16


def draw_lengths(key, part):
    key = jax.random.fold_in(key, 11)
    first_key, second_key = jax.random.split(key)
    seq_index = jnp.arange(NSEQ, dtype=jnp.int32)
    group_index = seq_index // SEQS
    group_total = NSEQ // SEQS
    lowest = 1 + SEQ_LEN // 2 * group_index // max(group_total - 1, 1)
    random_bits = jax.random.randint(first_key, (NSEQ,), 0, 1 << 20)
    drawn = lowest + random_bits % (SEQ_LEN + 1 - lowest)
    full_pick = jax.random.randint(second_key, (group_total,), 0, SEQS)
    is_full = seq_index % SEQS == full_pick[group_index]
    return jnp.where(is_full, SEQ_LEN, drawn).astype(jnp.int32)


def draw_positions(key, part):
    key = jax.random.fold_in(key, 12)
    start_key, order_key, step_key = jax.random.split(key, 3)
    starts = jax.random.randint(start_key, (NSEQ,), 0, 4096)
    order = jax.random.permutation(order_key, NSEQ)
    seq_index = jnp.arange(NSEQ, dtype=jnp.int32)
    starts = jnp.where(seq_index == order[0], 0, starts)
    starts = jnp.where(seq_index == order[1], 4095, starts)
    steps = jax.random.randint(step_key, (NSEQ, SEQ_LEN), 1, 3)
    steps = jnp.where((seq_index == order[1])[:, None], 2, steps)
    before = jnp.cumsum(steps, axis=1) - steps
    return (starts[:, None] + before).astype(jnp.int32)


def levels(own_key, shape, cuts, smallest, largest):
    def one(axis_at, blocks):
        steps = jax.random.uniform(jax.random.fold_in(jax.random.fold_in(own_key, 6), axis_at), (blocks,), jnp.float32, smallest / len(cuts), largest / len(cuts))
        return jnp.repeat(jnp.exp(steps), shape[axis_at] // blocks).reshape((-1,) + (1,) * (len(shape) - axis_at - 1))

    factor_of = one(*cuts[0])
    for cut in cuts[1:]:
        factor_of = factor_of * one(*cut)
    return factor_of


def noise(own_key, shape, scale, limit, cuts=(), kind=jnp.bfloat16):
    gain = levels(own_key, shape, cuts, -0.22, 0.18) if cuts else 1.0
    result = jax.random.normal(own_key, shape, jnp.float32) * scale * gain
    return jnp.minimum(jnp.maximum(result, -limit), limit).astype(kind)


def setup_inputs(seed: int = 0) -> dict:
    seeds = jax.random.split(jax.random.key(seed), 13)
    tokens = noise(seeds[0], (NSEQ, SEQ_LEN, D), 1.0, 6.0, ((0, 8), (1, 4)))
    history = noise(seeds[1], (NHIST, NSEQ, SEQ_LEN, D), 1.0, 6.0, ((1, 8), (2, 4)))
    cotangent = noise(seeds[2], (NSEQ, SEQ_LEN, D), 1.0, 6.0, ((0, 8), (1, 4)))
    qkv_weight = noise(seeds[3], (D, 3 * D), D ** -0.5, 0.21875)
    out_weight = noise(seeds[4], (D, D), (max(D // 256, 1)) ** -0.5, 3.5)
    up_weight = noise(seeds[5], (D, FF), D ** -0.5, 0.21875)
    down_weight = noise(seeds[6], (FF, D), FF ** -0.5, 0.109375)
    attn_gain = jnp.clip(1.0 + 0.1 * jax.random.normal(seeds[7], (D,), jnp.float32), 0.5, 1.5)
    mlp_gain = jnp.clip(1.0 + 0.1 * jax.random.normal(seeds[8], (D,), jnp.float32), 0.5, 1.5)
    depth_mix = jnp.clip(jax.random.uniform(seeds[9], (NHIST + 1,), jnp.float32, 0.1, 0.6), 0.1, 0.6)
    lengths = draw_lengths(jax.random.fold_in(seeds[12], 71), 0)
    positions = draw_positions(jax.random.fold_in(seeds[12], 71), 0)
    return {"tokens": tokens, "history": history, "cotangent": cotangent, "qkv_weight": qkv_weight, "out_weight": out_weight, "up_weight": up_weight, "down_weight": down_weight, "attn_gain": attn_gain, "mlp_gain": mlp_gain, "depth_mix": depth_mix, "lengths": lengths, "positions": positions}


@jax.custom_vjp
def low(v):
    return lax.optimization_barrier(v.astype(jnp.bfloat16)).astype(jnp.float32)

@jax.custom_vjp
def low_back(v):
    return v

def low_keep(v):
    return (low(v), None)

def low_pass(kept, grad):
    return (grad,)

def back_keep(v):
    return (v, None)

def back_low(kept, grad):
    return (low(grad),)
low.defvjp(low_keep, low_pass)
low_back.defvjp(back_keep, back_low)
epsilon = 1e-05
highest = lax.Precision.HIGHEST

def layer_norm(values, gain_vec):
    center = values - lax.optimization_barrier(jnp.mean(values, -1, keepdims=True))
    spread = lax.optimization_barrier(jnp.mean(center * center, -1, keepdims=True))
    return center * lax.rsqrt(spread + epsilon) * gain_vec

def smooth_gelu(values):
    return jax.nn.gelu(values, approximate=True)

def angles(position_rows, head_size):
    half_size = head_size // 2
    frequency = 1.0 / 10000.0 ** (jnp.arange(half_size, dtype=jnp.float32) * 2.0 / head_size)
    turned = position_rows.astype(jnp.float32)[..., None] * frequency
    return (jnp.cos(turned)[..., None, :], jnp.sin(turned)[..., None, :])

def rotate(values, cosine, sine_part):
    half_size = values.shape[-1] // 2
    lower_half = values[..., :half_size]
    upper_half = values[..., half_size:]
    return jnp.concatenate([lower_half * cosine - upper_half * sine_part, upper_half * cosine + lower_half * sine_part], -1)

def sequence_forward(inputs, stored, qkv_weight, out_weight, up_weight, down_weight, attn_gain, mlp_gain, depth_mix, length_one, position_row):
    seq_len = inputs.shape[0]
    model_width = inputs.shape[1]
    normed = low(layer_norm(inputs, attn_gain))
    projected = low_back(jnp.dot(normed, qkv_weight, precision=highest)).reshape(seq_len, 3, H, HD)
    cosine, sine_part = angles(position_row, HD)
    queries = low(rotate(projected[:, 0], cosine, sine_part))
    key_rows = low(rotate(projected[:, 1], cosine, sine_part))
    value_rows = low(projected[:, 2])
    raw_scores = low_back(jnp.einsum('qhd,khd->hqk', queries, key_rows, precision=highest) * HD ** (-0.5))
    slot_index = jnp.arange(seq_len, dtype=jnp.int32)
    allowed = (slot_index[None, :] <= slot_index[:, None]) & (slot_index[None, :] < length_one)
    masked = jnp.where(allowed[None], raw_scores, -1e+30)
    row_max = lax.optimization_barrier(jnp.max(masked, -1, keepdims=True))
    weights = jnp.exp(masked - row_max)
    row_sum = lax.optimization_barrier(jnp.sum(weights, -1, keepdims=True))
    attended = jnp.einsum('hqk,khd->qhd', low(weights), value_rows, precision=highest) / jnp.transpose(row_sum, (1, 0, 2))
    attended = low(low_back(attended.reshape(seq_len, model_width)))
    middle = inputs + low_back(jnp.dot(attended, out_weight, precision=highest))
    normed_two = low(layer_norm(middle, mlp_gain))
    hidden_pre = low_back(jnp.dot(normed_two, up_weight, precision=highest))
    activated = low(smooth_gelu(hidden_pre))
    block_out = middle + low_back(jnp.dot(activated, down_weight, precision=highest))
    return jnp.einsum('j,jtd->td', depth_mix[:-1], stored, precision=highest) + depth_mix[-1] * block_out

def reference(tokens, history, cotangent, qkv_weight, out_weight, up_weight, down_weight, attn_gain, mlp_gain, depth_mix, lengths, positions):
    qkv_full = qkv_weight.astype(jnp.float32)
    out_full = out_weight.astype(jnp.float32)
    up_full = up_weight.astype(jnp.float32)
    down_full = down_weight.astype(jnp.float32)
    counted = jnp.sum(lengths).astype(jnp.float32)
    factor = NSEQ * SEQ_LEN / counted

    def one_sequence(running, sequence_item):
        inputs, stored, cot_row, length_one, position_row = sequence_item

        def forward(input_full, stored_full, qkv_arg, out_arg, up_arg, down_arg, gain_one, gain_two, mix_arg):
            return sequence_forward(input_full, stored_full, qkv_arg, out_arg, up_arg, down_arg, gain_one, gain_two, mix_arg, length_one, position_row)
        mixed_out, pullback = jax.vjp(forward, inputs.astype(jnp.float32), stored.astype(jnp.float32), qkv_full, out_full, up_full, down_full, attn_gain, mlp_gain, depth_mix)
        live_mask = (jnp.arange(SEQ_LEN, dtype=jnp.int32) < length_one).astype(jnp.float32)
        grads = pullback(cot_row.astype(jnp.float32) * live_mask[:, None] * factor)
        running = tuple((summed + grad for summed, grad in zip(running, grads[2:])))
        return (running, (mixed_out.astype(jnp.bfloat16), grads[0].astype(jnp.bfloat16), grads[1].astype(jnp.bfloat16)))
    start = (jnp.zeros_like(qkv_full), jnp.zeros_like(out_full), jnp.zeros_like(up_full), jnp.zeros_like(down_full), jnp.zeros_like(attn_gain), jnp.zeros_like(mlp_gain), jnp.zeros_like(depth_mix))
    final, stacked = lax.scan(one_sequence, start, (tokens, jnp.moveaxis(history, 1, 0), cotangent, lengths, positions))
    outputs, input_grads, stored_grads = stacked
    return (outputs, input_grads, jnp.moveaxis(stored_grads, 0, 1), final[0], final[1], final[2], final[3], final[4], final[5], final[6])
```

```python
import functools
import math

import jax
import jax.numpy as jnp
import numpy as np
from jax import lax
from jax.experimental import pallas as pl
from jax.experimental.pallas import tpu as pltpu
from jax.sharding import PartitionSpec as P

H = 12
HD = 64
LANES = 128
TILE = 256
PIECE = 512
QUERIES = 256
ROWS = 512
NEGATIVE = -1e30
epsilon = 1e-05
MESH = pl.DeviceIdType.MESH
F32 = jnp.float32
B16 = jnp.bfloat16
VMEM = pl.BlockSpec(memory_space=pltpu.VMEM)
SMEM = pl.BlockSpec(memory_space=pltpu.SMEM)
ANY = pl.BlockSpec(memory_space=pl.ANY)


def dot(a, b):
    return jnp.dot(a, b, preferred_element_type=F32)


def dot_nt(a, b):
    return lax.dot_general(a, b, (((1,), (1,)), ((), ())), preferred_element_type=F32)


def dot_tn(a, b):
    return lax.dot_general(a, b, (((0,), (0,)), ((), ())), preferred_element_type=F32)


def lane_of(shape):
    return lax.broadcasted_iota(jnp.int32, shape, 1)


def three(values):
    high = values.astype(B16).astype(F32)
    rest = values - high
    middle = rest.astype(B16).astype(F32)
    return high, middle, rest - middle


class Place:
    def __init__(self):
        self.count = lax.axis_size("seq")
        self.each = self.count // 4
        self.share = 2 * self.each
        self.batches = lax.axis_size("batch")
        self.b = lax.axis_index("batch")
        self.k = lax.axis_index("seq")
        self.core = lax.rem(self.b, 2)
        self.base = self.b - self.core
        self.q = lax.div(self.k, self.each)
        self.u = lax.rem(self.k, self.each) * 2 + self.core

    def worker(self, q, u):
        return (self.base + u % 2, q * self.each + u // 2)

    def owner(self, q, j):
        return (self.base + lax.div(q, 2), j)

    def is_me(self, device):
        return jnp.logical_and(device[0] == self.b, device[1] == self.k)


def greet(place, other_planes=()):
    barrier = pltpu.get_barrier_semaphore()
    met = 0
    for other in (0, 1):
        for step in range(place.count):
            if other == 0 and step == 0:
                continue
            core = lax.rem(place.core + other, 2)
            k = lax.rem(place.k + step, place.count)
            pl.semaphore_signal(barrier, inc=1, device_id=(place.base + core, k), device_id_type=MESH)
            met += 1
    for step in range(place.batches // 2 - 1):
        base = lax.rem(place.base + 2 * (step + 1), place.batches)
        for core in other_planes:
            pl.semaphore_signal(barrier, inc=1, device_id=(base + core, place.k), device_id_type=MESH)
            met += 1
    pl.semaphore_wait(barrier, met)


class Copies:
    def __init__(self, place):
        self.place = place
        self.sent = []

    def post(self, src, dst, send_sem, recv_sem, device):
        mine = self.place.is_me(device)
        far = pltpu.make_async_remote_copy(
            src_ref=src, dst_ref=dst, send_sem=send_sem, recv_sem=recv_sem,
            device_id=device, device_id_type=MESH,
        )

        @pl.when(jnp.logical_not(mine))
        def _():
            far.start()

        @pl.when(mine)
        def _():
            pltpu.make_async_copy(src, dst, recv_sem).start()

        self.sent.append((mine, far))

    def drain(self):
        for mine, far in self.sent:
            @pl.when(jnp.logical_not(mine))
            def _():
                far.wait_send()


def remote(src, dst, send_sem, recv_sem, device):
    return pltpu.make_async_remote_copy(
        src_ref=src, dst_ref=dst, send_sem=send_sem, recv_sem=recv_sem, device_id=device, device_id_type=MESH
    )


def arrived(slot, sem):
    pltpu.make_async_copy(slot, slot, sem).wait()


def to_owners_kernel(src_ref, dst_ref, send, recv):
    place = Place()
    greet(place)
    copies = Copies(place)
    for step in range(place.count):
        j = lax.rem(place.k + step, place.count)
        s = lax.rem(place.q, 2)
        copies.post(src_ref.at[j], dst_ref.at[s, place.u], send.at[step], recv.at[s, place.u], place.owner(place.q, j))
    for s in (0, 1):
        for u in range(place.share):
            arrived(dst_ref.at[s, u], recv.at[s, u])
    copies.drain()


def to_owners(values, name, number):
    n = lax.axis_size("seq")
    dma = pltpu.SemaphoreType.DMA
    return pl.pallas_call(
        to_owners_kernel,
        out_shape=jax.ShapeDtypeStruct((2, n // 2) + values.shape[1:], values.dtype),
        in_specs=[ANY],
        out_specs=ANY,
        scratch_shapes=[dma((n,)), dma((2, n // 2))],
        compiler_params=pltpu.CompilerParams(collective_id=number, has_side_effects=True),
        name=name,
    )(values)


class Sum:
    def __init__(self, place, order, rows, source, bufs, result, first, sems):
        groups = {
            "z": (lax.div(place.base, 2), 4, lambda i: (2 * i + place.core, place.k)),
            "seq": (place.k, 4, lambda i: (place.b, i)),
            "all": (2 * place.base + place.k, 16, lambda i: (2 * lax.div(i, 4) + place.core, lax.rem(i, 4))),
        }
        self.levels = [groups[name] for name in order]
        self.rows = []
        for _, size, _ in self.levels:
            rows = rows // size
            self.rows.append(rows)
        count = len(order)
        self.core = place.core
        self.partner = (place.base + 1 - place.core, place.k)
        self.source, self.result, self.first = source, result, first
        self.recvs, self.helds = bufs[0::2], bufs[1::2]
        self.out_sems = [sems[2 * i : 2 * i + 2] for i in range(count)]
        self.back_sems = [sems[2 * count + 2 * i : 2 * count + 2 * i + 2] for i in range(count)]
        self.here, self.swap_send, self.swap_recv = sems[4 * count :]

    def others(self, level):
        me, size, _ = self.levels[level]
        return [lax.rem(me + d, size) for d in range(1, size)]

    def shard(self, unit, level, i):
        held = self.source(unit) if level == 0 else self.helds[level - 1].at[unit]
        return held.at[pl.ds(pl.multiple_of(i * self.rows[level], 16), self.rows[level])]

    def region(self, unit, level, i):
        start = i * self.rows[level]
        for before in range(level):
            start = start + self.levels[before][0] * self.rows[before]
        return self.result.at[self.first + unit, self.core, pl.ds(pl.multiple_of(start, 16), self.rows[level])]

    def outward(self, unit, level):
        me, _, device = self.levels[level]
        send, recv = self.out_sems[level]
        for d, i in enumerate(self.others(level)):
            yield remote(
                self.shard(unit, level, i), self.recvs[level].at[unit, me], send.at[unit, d], recv.at[unit, me], device(i)
            )

    def back(self, unit, level):
        me, _, device = self.levels[level]
        send, recv = self.back_sems[level]
        last = level == len(self.levels) - 1
        region = self.region(unit, level, me)
        for d, i in enumerate(self.others(level)):
            src = self.helds[level].at[unit] if last else region
            yield remote(src, region, send.at[unit, d], recv.at[unit, me], device(i))

    def keep(self, unit):
        last = len(self.levels) - 1
        return pltpu.make_async_copy(
            self.helds[last].at[unit], self.region(unit, last, self.levels[last][0]), self.here.at[unit]
        )

    def cross(self, unit):
        region = self.result.at[self.first + unit, self.core]
        return remote(region, region, self.swap_send.at[unit], self.swap_recv.at[unit], self.partner)

    def scatter(self, unit):
        self.send(unit, 0)

    def sum(self, unit, level, onward=True):
        others = self.others(level)
        recv = self.recvs[level]
        for i in others:
            arrived(recv.at[unit, i], self.out_sems[level][1].at[unit, i])
        own = self.shard(unit, level, self.levels[level][0])
        pieces = 4 if self.rows[level] % 64 == 0 else 1
        size = self.rows[level] // pieces
        for piece in range(pieces):
            rows = slice(piece * size, (piece + 1) * size)
            total = own[rows, :].astype(F32)
            for i in others:
                total = total + recv[unit, i, rows, :].astype(F32)
            self.helds[level][unit, rows, :] = total.astype(B16)
        if onward and level + 1 < len(self.levels):
            self.send(unit, level + 1)

    def send(self, unit, level):
        for copy in self.outward(unit, level):
            copy.start()

    def share(self, unit):
        self.keep(unit).start()
        for copy in self.back(unit, len(self.levels) - 1):
            copy.start()

    def collect(self, unit, level):
        if level == len(self.levels) - 1:
            self.keep(unit).wait()
        for i in self.others(level):
            arrived(self.region(unit, level, i), self.back_sems[level][1].at[unit, i])

    def gather(self, unit, level, collected=False):
        if not collected:
            self.collect(unit, level + 1)
        for copy in self.back(unit, level):
            copy.start()

    def swap(self, unit):
        self.collect(unit, 0)
        self.cross(unit).start()

    def close(self, unit, out=(), back=()):
        for level in range(len(self.levels)):
            for copy in self.outward(unit, level) if level in out else ():
                copy.wait_send()
            for copy in self.back(unit, level) if level in back else ():
                copy.wait_send()

    def end(self, unit):
        self.cross(unit).wait_send()
        arrived(self.result.at[self.first + unit, 1 - self.core], self.swap_recv.at[unit])


SIZES = {"z": 4, "seq": 4, "all": 16}


def sum_buffers(order, units, rows):
    bufs = []
    for name in order:
        rows //= SIZES[name]
        bufs += [pltpu.VMEM((units, SIZES[name], rows, LANES), B16), pltpu.VMEM((units, rows, LANES), B16)]
    return bufs


def sum_sems(order, units):
    dma = pltpu.SemaphoreType.DMA
    each = [dma((units, count)) for name in order for count in (SIZES[name] - 1, SIZES[name])]
    return each + each + [dma((units,))] * 3


def center_of(values):
    center = values - jnp.mean(values, -1, keepdims=True)
    spread = lax.rsqrt(jnp.mean(center * center, -1, keepdims=True) + epsilon)
    return center * spread, spread


def partner_of(values, lane):
    return jnp.where(lax.rem(lane, HD) < HD // 2, pltpu.roll(values, LANES - HD // 2, 1), pltpu.roll(values, HD // 2, 1))


def own_columns(place, all_ref, w_ref, sems):
    wide = w_ref.shape[1] // 3
    return [
        pltpu.make_async_copy(
            all_ref.at[:, pl.ds(pl.multiple_of((part * place.share + place.u) * wide, LANES), wide)],
            w_ref.at[:, pl.ds(part * wide, wide)],
            sems.at[part],
        )
        for part in range(3)
    ]


def turn_tables(position_row, freq_ref):
    turned = freq_ref[...] * position_row.astype(F32)
    cosine, sine = jnp.cos(turned), jnp.sin(turned)
    return (
        jnp.transpose(jnp.concatenate([cosine] * 4, axis=0)),
        jnp.transpose(jnp.concatenate([-sine, sine, -sine, sine], axis=0)),
    )


def attend_kernel(
    pairs, len_in, tok_ref, wall_ref, pos_in, gain_in, freq_ref,
    o_ref, att_out, normed_out, qp_out, kp_out, vp_out, cos_out, sin_out, alllen_ref,
    seq_ref, allpos_ref, w_ref, att_ref, normed_ref, qp_ref, kp_ref, vp_ref, cos_ref, sin_ref, out_ref, pos_ref, len_ref,
    wsem, send, recv, tsend, trecv, fsend, frecv, psend, precv, lsend, lrecv, osem, psem,
):
    place = Place()
    n, share = place.count, place.share
    for copy in own_columns(place, wall_ref, w_ref, wsem):
        copy.start()
    blocks, _, block, _ = out_ref.shape
    for s in (0, 1):
        len_ref[s] = jnp.full(len_ref.shape[1:], len_in[s], jnp.int32)
        for i in range(block // LANES):
            pos_ref[s, i : i + 1, :] = pos_in[s : s + 1, i * LANES : (i + 1) * LANES]
    gain = gain_in[...].reshape(1, gain_in.shape[0])
    greet(place, (0, 1))
    total = blocks * block
    tiles = total // TILE
    copies = Copies(place)
    for s in (0, 1):
        q = 2 * place.core + s
        for u in range(share):
            device = place.worker(q, u)
            copies.post(pos_ref.at[s], allpos_ref.at[place.k], psend.at[s, u], precv.at[place.k], device)
    for step in range(place.batches):
        b = lax.rem(place.b + step, place.batches)
        copies.post(len_ref, alllen_ref.at[place.b], lsend.at[step], lrecv.at[place.b], (b, place.k))
    first = lax.rem(place.k, 2)
    if n == 4:
        far_corner = lax.div(place.k, 2) != place.core
        order = lambda step: (
            place.k
            + jnp.where(step == 1, 1 - 2 * lax.rem(place.k, 2), 0)
            + jnp.where(step == 2, 2 - 4 * lax.div(place.k, 2), 0)
            + jnp.where(step == 3, 3 - 2 * place.k, 0)
        )
    else:
        far_corner = place.k < 0
        order = lambda step: lax.rem(place.k + step, n)

    def token_copies(turn):
        s = first if turn == 0 else 1 - first
        for u in range(share):
            device = place.worker(2 * place.core + s, u)
            src, dst, arrival = tok_ref.at[s, u], seq_ref.at[place.k, u], trecv.at[place.k]
            yield place.is_me(device), remote(src, dst, tsend.at[turn, u], arrival, device), pltpu.make_async_copy(
                src, dst, arrival
            )

    def post_tokens(turn):
        for mine, far_copy, near_copy in token_copies(turn):

            @pl.when(jnp.logical_not(mine))
            def _():
                far_copy.start()

            @pl.when(mine)
            def _():
                near_copy.start()

    def tokens_left(turn):
        for mine, far_copy, _ in token_copies(turn):

            @pl.when(jnp.logical_not(mine))
            def _():
                far_copy.wait_send()

    post_tokens(0)

    @pl.when(jnp.logical_not(far_corner))
    def _():
        post_tokens(1)

    def forward(j, other):
        u = lax.rem(place.u + other, share)
        device = (place.base + lax.rem(u, 2), place.q * place.each + lax.div(u, 2))
        piece = seq_ref.at[j, place.u]
        return remote(piece, piece, fsend.at[j, other - 1], frecv.at[j, other - 1], device)

    def leave(p, j):
        src, dst = out_ref.at[j, p], o_ref.at[lax.rem(place.q, 2), place.u, p]
        arrival = recv.at[lax.rem(place.q, 2), place.u, p]
        device = place.owner(place.q, j)
        return place.is_me(device), remote(src, dst, send.at[p, j], arrival, device), pltpu.make_async_copy(src, dst, arrival)

    for copy in own_columns(place, wall_ref, w_ref, wsem):
        copy.wait()
    for b in range(place.batches):
        arrived(alllen_ref.at[b], lrecv.at[b])
    length = alllen_ref[place.base + lax.div(place.q, 2), lax.rem(place.q, 2), 0:1, :]
    lane = lane_of((TILE, LANES))
    row = lax.broadcasted_iota(jnp.int32, (TILE, LANES), 0)

    def project(x, start):
        rows = pl.ds(start, TILE)
        unit, _ = center_of(x.astype(F32))
        normed = (unit * gain).astype(B16)
        normed_ref[rows, :] = normed
        proj = dot(normed, w_ref[...])
        cosine, sine = cos_ref[rows, :], sin_ref[rows, :]
        real = row + start < length
        q_rest = jnp.where(lane == HD, 1.0, 0.0)
        k_rest = jnp.where(lane == HD, jnp.where(real, 0.0, NEGATIVE), jnp.where(lane < HD + 4, 1.0, 0.0))
        v_rest = jnp.where(real, 1.0, 0.0)
        for p in range(pairs):
            for part, (to_ref, rest) in enumerate(((qp_ref, q_rest), (kp_ref, k_rest), (vp_ref, v_rest))):
                at = (part * pairs + p) * LANES
                values = proj[:, at : at + LANES]
                if part < 2:
                    values = values * cosine + partner_of(values, lane) * sine
                if part == 0:
                    values = values * (1.0 / math.sqrt(HD))
                to_ref[2 * p, rows, :] = jnp.where(lane < HD, values, rest).astype(B16)
                to_ref[2 * p + 1, rows, :] = jnp.where(lane < HD, pltpu.roll(values, HD, 1), rest).astype(B16)

    @pl.loop(0, n)
    def _(step):
        j = order(step)

        @pl.when(jnp.logical_and(step == 1, far_corner))
        def _():
            tokens_left(0)
            post_tokens(1)

        arrived(seq_ref.at[j, place.u], trecv.at[j])
        for other in range(1, share):
            forward(j, other).start()
        arrived(allpos_ref.at[j], precv.at[j])
        start = pl.multiple_of(j * block, block)
        for i in range(block // LANES):
            cosine, sine = turn_tables(allpos_ref[j, i : i + 1, :], freq_ref)
            rows = pl.ds(pl.multiple_of(start + i * LANES, LANES), LANES)
            cos_ref[rows, :] = cosine
            sin_ref[rows, :] = sine
        if block // share == TILE:
            for other in range(share):
                u = lax.rem(place.u + share - other, share)
                if other:
                    arrived(seq_ref.at[j, u], frecv.at[j, other - 1])
                project(seq_ref[j, u], pl.multiple_of(start + u * TILE, TILE))
        else:
            for other in range(1, share):
                u = lax.rem(place.u + share - other, share)
                arrived(seq_ref.at[j, u], frecv.at[j, other - 1])
            for i in range(block // TILE):
                whole = seq_ref[j].reshape(block, seq_ref.shape[3])
                project(whole[i * TILE : (i + 1) * TILE], pl.multiple_of(start + i * TILE, TILE))

    ready = [(normed_ref, normed_out), (kp_ref, kp_out), (vp_ref, vp_out), (cos_ref, cos_out), (sin_ref, sin_out)]

    def whole_copies():
        for number, (src, dst) in enumerate(ready):
            yield pltpu.make_async_copy(src, dst, osem.at[number])

    def pair_copies(p):
        yield pltpu.make_async_copy(att_ref.at[p], att_out.at[p], psem.at[p, 0])
        yield pltpu.make_async_copy(qp_ref.at[pl.ds(2 * p, 2)], qp_out.at[pl.ds(2 * p, 2)], psem.at[p, 1])

    for copy in whole_copies():
        copy.start()
    later = jnp.where(lane_of((QUERIES, QUERIES)) <= lax.broadcasted_iota(jnp.int32, (QUERIES, QUERIES), 0), 0.0, NEGATIVE)

    lane = lane_of((QUERIES, LANES))

    @pl.loop(0, pairs)
    def _(p):
        for i in range(total // QUERIES):
            start = i * QUERIES
            found = []
            for e in (0, 1):
                h = 2 * p + e
                q = qp_ref[h, start : start + QUERIES, :]
                near = dot_nt(q, kp_ref[h, start : start + QUERIES, :]) + later
                top = jnp.max(near, -1, keepdims=True)
                if i:
                    far = dot_nt(q, kp_ref[h, :start, :])
                    top = jnp.maximum(top, jnp.max(far, -1, keepdims=True))
                out = dot(jnp.exp(near - top).astype(B16), vp_ref[h, start : start + QUERIES, :])
                if i:
                    out = out + dot(jnp.exp(far - top).astype(B16), vp_ref[h, :start, :])
                found.append(out)
                high, mid, low = three(-(top + jnp.log(out)))
                q_new = jnp.where(lane == HD + 1, high, jnp.where(lane == HD + 2, mid, jnp.where(lane == HD + 3, low, q.astype(F32))))
                qp_ref[h, start : start + QUERIES, :] = q_new.astype(B16)
            even, odd = found
            low_half = lane < HD
            att = jnp.where(low_half, even, pltpu.roll(odd, HD, 1)) / jnp.where(low_half, pltpu.roll(even, HD, 1), odd)
            att_ref[p, start : start + QUERIES, :] = att
            j, within = start // block, start % block
            out_ref[j, p, within : within + QUERIES, :] = att.astype(B16)
            if within + QUERIES == block:
                mine, far_copy, near_copy = leave(p, j)

                @pl.when(jnp.logical_not(mine))
                def _():
                    far_copy.start()

                @pl.when(mine)
                def _():
                    near_copy.start()
        for copy in pair_copies(p):
            copy.start()

    for copy in whole_copies():
        copy.wait()
    copies.drain()

    @pl.when(jnp.logical_not(far_corner))
    def _():
        tokens_left(0)

    tokens_left(1)
    for j in range(n):
        for other in range(1, share):
            forward(j, other).wait_send()
    for p in range(pairs):
        for copy in pair_copies(p):
            copy.wait()
        for s in (0, 1):
            for u in range(place.share):
                arrived(o_ref.at[s, u, p], recv.at[s, u, p])
        for j in range(blocks):
            mine, far_copy, _ = leave(p, j)

            @pl.when(jnp.logical_not(mine))
            def _():
                far_copy.wait_send()


def attend(tokens, positions, lengths, w_all, gain):
    n = lax.axis_size("seq")
    batches = lax.axis_size("batch")
    share = n // 2
    _, block, width = tokens.shape
    total = n * block
    pairs = w_all.shape[1] // (3 * share * LANES)
    dma = pltpu.SemaphoreType.DMA

    def shape(dims, kind=B16):
        return jax.ShapeDtypeStruct(dims, kind)

    heads = (2 * pairs, total, LANES)
    table = (total, LANES)
    frequency = (1.0 / 10000.0 ** (np.arange(HD // 2) * 2.0 / HD)).astype(np.float32)
    return pl.pallas_call(
        functools.partial(attend_kernel, pairs),
        out_shape=(
            shape((2, share, pairs, block, LANES)), shape((pairs, total, LANES), F32), shape((total, width)),
            shape(heads), shape(heads), shape(heads), shape(table, F32), shape(table, F32),
            shape((batches, 2, 8, LANES), jnp.int32),
        ),
        in_specs=[SMEM] + [ANY] * 2 + [VMEM] * 3,
        out_specs=(ANY,) * 8 + (VMEM,),
        scratch_shapes=[
            pltpu.VMEM((n, share, block // share, width), B16),
            pltpu.VMEM((n, block // LANES, LANES), jnp.int32),
            pltpu.VMEM((width, 3 * pairs * LANES), B16),
            pltpu.VMEM((pairs, total, LANES), F32),
            pltpu.VMEM((total, width), B16),
            pltpu.VMEM(heads, B16),
            pltpu.VMEM(heads, B16),
            pltpu.VMEM(heads, B16),
            pltpu.VMEM(table, F32),
            pltpu.VMEM(table, F32),
            pltpu.VMEM((n, pairs, block, LANES), B16),
            pltpu.VMEM((2, block // LANES, LANES), jnp.int32),
            pltpu.VMEM((2, 8, LANES), jnp.int32),
            dma((3,)), dma((pairs, n)), dma((2, share, pairs)), dma((2, share)), dma((n,)), dma((n, share - 1)),
            dma((n, share - 1)), dma((2, share)), dma((n,)), dma((batches,)), dma((batches,)), dma((5,)), dma((pairs, 2)),
        ],
        compiler_params=pltpu.CompilerParams(
            vmem_limit_bytes=56 * 2**20, collective_id=1, has_side_effects=True
        ),
        cost_estimate=pl.CostEstimate(flops=30 * 10**9, bytes_accessed=30 * 2**20, transcendentals=13 * 10**6),
        name="attention_forward",
    )(
        lengths, tokens.reshape(2, share, block // share, width), w_all, positions, gain,
        np.broadcast_to(frequency[:, None], (HD // 2, LANES)).copy(),
    )


def lay_gradient(do_ref, att_ref, dop_ref, p):
    block = do_ref.shape[2]
    lane = lane_of((TILE, LANES))
    low_half = lane < HD
    for i in range(dop_ref.shape[1] // TILE):
        start = i * TILE
        grad = do_ref[start // block, p, start % block : start % block + TILE, :].astype(F32)
        product = grad * att_ref[p, start : start + TILE, :]
        for e in (0, 1):
            side = low_half if e == 0 else jnp.logical_not(low_half)
            high, mid, low = three(-jnp.sum(jnp.where(side, product, 0.0), -1, keepdims=True))
            head = grad if e == 0 else pltpu.roll(grad, HD, 1)
            rest = jnp.where(lane == HD, high, jnp.where(lane == HD + 1, mid, jnp.where(lane == HD + 2, low, 0.0)))
            dop_ref[e, start : start + TILE, :] = jnp.where(low_half, head, rest).astype(B16)


def pair_back(pairs, p, qp_ref, kp_ref, vp_ref, cos_ref, sin_ref, dop_ref, kt_ref, dq_ref, pg_ref, point):
    total = dop_ref.shape[1]
    tiles = total // TILE
    lane = lane_of((TILE, LANES))
    low_half = lane < HD
    earlier = jnp.where(lane_of((TILE, TILE)) >= lax.broadcasted_iota(jnp.int32, (TILE, TILE), 0), 0.0, NEGATIVE)

    def packed(even, odd):
        return jnp.where(low_half, even, pltpu.roll(odd, HD, 1))

    def unrotated(values, rows):
        return values * cos_ref[rows, :] - partner_of(values, lane) * sin_ref[rows, :]

    for i in range(tiles):
        rows = slice(i * TILE, (i + 1) * TILE)
        for e in (0, 1):
            kt_ref[e, :, rows] = jnp.transpose(kp_ref[2 * p + e, rows, :].astype(F32))[:HD].astype(B16)
    for j in range(tiles):
        start = j * TILE
        near_rows = slice(start, start + TILE)
        dks, dvs = [], []
        for e in (0, 1):
            h = 2 * p + e
            kj, vj = kp_ref[h, near_rows, :], vp_ref[h, near_rows, :]
            dk = dv = None
            for part in (0, 1):
                rows = near_rows if part == 0 else slice(start + TILE, total)
                if rows.start == total:
                    continue
                qs, dos = qp_ref[h, rows, :], dop_ref[e, rows, :]
                scores = dot_nt(kj, qs)
                if part == 0:
                    scores = scores + earlier
                probs = jnp.exp(scores)
                dv_part = dot(probs.astype(B16), dos)
                grads = (probs * dot_nt(vj, dos)).astype(B16)
                dk_part = dot(grads, qs)
                dq_part = dot(kt_ref[e, :, near_rows], grads)
                if j == 0:
                    dq_ref[e, :, rows] = dq_part
                else:
                    dq_ref[e, :, rows] += dq_part
                dk = dk_part if dk is None else dk + dk_part
                dv = dv_part if dv is None else dv + dv_part
            dks.append(dk)
            dvs.append(dv)
        pg_ref[pairs + p, near_rows, :] = unrotated(packed(*dks), near_rows).astype(B16)
        pg_ref[2 * pairs + p, near_rows, :] = packed(*dvs).astype(B16)
        point(j)
    for i in range(tiles):
        rows = slice(i * TILE, (i + 1) * TILE)
        both = jnp.concatenate([dq_ref[0, :, rows], dq_ref[1, :, rows]], axis=0)
        dq = jnp.transpose(both) * (1.0 / math.sqrt(HD))
        pg_ref[p, rows, :] = unrotated(dq, rows).astype(B16)


def plain_back_kernel(
    pairs, qp_ref, kp_ref, vp_ref, do_ref, att_ref, cos_ref, sin_ref, normed_ref, wall_ref, wgrad_ref, gn_ref, gaing_ref,
    dop_ref, kt_ref, dq_ref, pg_ref, w_ref, wsem,
):
    place = Place()
    for copy in own_columns(place, wall_ref, w_ref, wsem):
        copy.start()

    @pl.loop(0, pairs)
    def _(p):
        lay_gradient(do_ref, att_ref, dop_ref, p)
        pair_back(pairs, p, qp_ref, kp_ref, vp_ref, cos_ref, sin_ref, dop_ref, kt_ref, dq_ref, pg_ref, lambda j: None)

    for copy in own_columns(place, wall_ref, w_ref, wsem):
        copy.wait()
    gaing_ref[...] = jnp.zeros_like(gaing_ref)

    @pl.loop(0, normed_ref.shape[0] // TILE)
    def _(t):
        rows = pl.ds(pl.multiple_of(t * TILE, TILE), TILE)
        grads = jnp.concatenate([pg_ref[g, rows, :] for g in range(3 * pairs)], axis=1)
        grad = dot_nt(grads, w_ref[...])
        gaing_ref[...] += folded(grad * normed_ref[rows, :].astype(F32))
        gn_ref[rows, :] = grad.astype(B16)

    for part in range(3):
        grads = jnp.concatenate([pg_ref[part * pairs + p] for p in range(pairs)], axis=1)
        wgrad_ref[:, part * pairs * LANES : (part + 1) * pairs * LANES] = dot_tn(normed_ref[...], grads).astype(B16)


def plain_back(qp, kp, vp, grad, att, cosine, sine, normed, w_all):
    total, width = normed.shape
    pairs = att.shape[0]
    w = jax.ShapeDtypeStruct((width, 3 * pairs * LANES), B16)
    return pl.pallas_call(
        functools.partial(plain_back_kernel, pairs),
        out_shape=(w, jax.ShapeDtypeStruct((total, width), B16), jax.ShapeDtypeStruct((8, width), F32)),
        in_specs=[VMEM] * 8 + [ANY],
        out_specs=(VMEM,) * 3,
        scratch_shapes=[
            pltpu.VMEM((2, total, LANES), B16),
            pltpu.VMEM((2, HD, total), B16),
            pltpu.VMEM((2, HD, total), F32),
            pltpu.VMEM((3 * pairs, total, LANES), B16),
            pltpu.VMEM(w.shape, B16),
            pltpu.SemaphoreType.DMA((3,)),
        ],
        compiler_params=pltpu.CompilerParams(vmem_limit_bytes=56 * 2**20),
        cost_estimate=pl.CostEstimate(flops=60 * 10**9, bytes_accessed=30 * 2**20, transcendentals=13 * 10**6),
        name="attention_backward",
    )(qp, kp, vp, grad, att, cosine, sine, normed, w_all)


UNITS = 3
FAMILIES = {"e": ("seq", "z"), "o": ("seq", "z"), "q0": ("z", "seq"), "q1": ("all",), "q2": ("all",)}
EARLY = {
    (0, -1): [("send1", "e1"), ("scatter", "e2")],
    (0, 2): [("sum1", "e1"), ("scatter", "o0"), ("share", "e1")],
    (0, 4): [("sum0", "e2"), ("gather0", "e0")],
    (0, 6): [("sum0", "o0")],
    (1, 1): [("gather0", "e1"), ("sum1", "e2"), ("sum1", "o0"), ("share", "e2"), ("share", "o0"), ("swap", "e0")],
    (1, 4): [("sum0", "q0")],
    (2, 0): [("swap", "e1"), ("gather0", "e2"), ("sum1", "q0"), ("share", "q0")],
    (2, 2): [("sum0", "q1"), ("share", "q1")],
}
LATE = (
    ("gather0", "o0"),
    ("gather0", "q0"),
    ("sum0", "q2"),
    ("share", "q2"),
    ("swap", "q1"),
    ("swap", "e2"),
    ("swap", "q0"),
    ("swap", "o0"),
    ("swap", "q2"),
)
SMALL = (0, 3, 6)
FINISH = 5


def summing_back_kernel(
    pairs, qp_in, kp_in, vp_in, do_in, att_in, cos_in, sin_in, normed_in, small_ref, half_sum_ref, mine_ref,
    outmine_ref, gain_ref, wall_ref, x_ref, gmid_ref, _, sums_ref, osums_ref, qsums_ref, total_ref, input_ref,
    dop_ref, kt_ref, dq_ref, pg_ref, w_ref, wg_ref, gn_ref, gnrecv_ref, sbuf_ref, srecv0_ref, srecv1_ref, srecv2_ref,
    slots_ref, xin_ref, gmidin_ref, qp_ref, kp_ref, vp_ref, do_ref, att_ref, cos_ref, sin_ref, normed_ref,
    pairsem, wholesem, wsem, insem, gsend, grecv, osend, orecv, ssend, srecv, *rest,
):
    def take(count):
        nonlocal rest
        taken, rest = rest[:count], rest[count:]
        return taken

    e_bufs, o_bufs = take(2 * len(FAMILIES["e"])), take(2 * len(FAMILIES["o"]))
    q_bufs = [take(2 * len(FAMILIES["q%d" % p])) for p in range(pairs)]
    sems = {}
    for name in ("e0", "e1", "e2", "o") + tuple("q%d" % p for p in range(pairs)):
        sems[name] = take(4 * len(FAMILIES["e" if name[0] == "e" else name]) + 3)
    e1_bufs = take(2)
    place = Place()
    core = place.core
    width = normed_ref.shape[1]
    slabs = width // LANES
    rows_q = wg_ref.shape[0] // pairs

    def pair_loads(p):
        both = pl.ds(2 * p, 2)
        moved = [(src.at[both], dst.at[both]) for src, dst in ((qp_in, qp_ref), (kp_in, kp_ref), (vp_in, vp_ref))]
        moved += [(do_in.at[:, p], do_ref.at[:, p]), (att_in.at[p], att_ref.at[p])]
        return [pltpu.make_async_copy(src, dst, pairsem.at[p, i]) for i, (src, dst) in enumerate(moved)]

    def whole_loads():
        moved = ((cos_in, cos_ref), (sin_in, sin_ref), (normed_in, normed_ref))
        return [pltpu.make_async_copy(src, dst, wholesem.at[i]) for i, (src, dst) in enumerate(moved)]

    for copy in pair_loads(0) + whole_loads() + [copy for p in range(1, pairs) for copy in pair_loads(p)]:
        copy.start()
    for copy in own_columns(place, wall_ref, w_ref, wsem):
        copy.start()
    greet(place, (core,))
    inputs = [
        pltpu.make_async_copy(x_ref, xin_ref, insem.at[0]), pltpu.make_async_copy(gmid_ref, gmidin_ref, insem.at[1])
    ]
    for copy in inputs:
        copy.start()
    units = {}
    for number, held in ((0, None), (1, half_sum_ref)):
        bufs = (None, held, *e1_bufs)
        units["e%d" % number] = (
            Sum(place, FAMILIES["e"], mine_ref.shape[0], None, bufs, sums_ref, number, sems["e%d" % number]), 0
        )
    last = Sum(place, FAMILIES["e"], mine_ref.shape[0], lambda unit: mine_ref, e_bufs, sums_ref, UNITS - 1, sems["e2"])
    units["e2"] = (last, 0)
    units["o0"] = (
        Sum(place, FAMILIES["o"], outmine_ref.shape[0], lambda unit: outmine_ref, o_bufs, osums_ref, 0, sems["o"]), 0
    )
    for p in range(pairs):
        name = "q%d" % p
        own = wg_ref.at[pl.ds(p * rows_q, rows_q)]
        units[name] = (
            Sum(place, FAMILIES[name], rows_q, lambda unit, own=own: own, q_bufs[p], qsums_ref, p, sems[name]), 0
        )
    partner = last.partner

    def stage(name, key):
        family, unit = units[key]
        if name[:3] == "sum":
            family.sum(unit, int(name[3:]))
        elif name[:4] == "send":
            family.send(unit, int(name[4:]))
        elif name[:6] == "gather":
            family.gather(unit, int(name[6:]), collected=key == "e0")
        else:
            getattr(family, name)(unit)

    def point(p, j):
        for (at_p, at_j), todo in EARLY.items():
            if at_j == j:

                @pl.when(p == at_p)
                def _(todo=todo):
                    for name, key in todo:
                        stage(name, key)

    @pl.loop(0, pairs)
    def _(p):
        point(p, -1)
        for copy in pair_loads(p):
            copy.wait()
        lay_gradient(do_ref, att_ref, dop_ref, p)

        @pl.when(p == 0)
        def _():
            for copy in whole_loads():
                copy.wait()

        pair_back(
            pairs, p, qp_ref, kp_ref, vp_ref, cos_ref, sin_ref, dop_ref, kt_ref, dq_ref, pg_ref, functools.partial(point, p)
        )
        grads = jnp.concatenate([pg_ref[part * pairs + p] for part in range(3)], axis=1)
        found = dot_tn(normed_ref[...], grads).astype(B16)
        for part in range(3):
            rows = pl.ds(pl.multiple_of(p * rows_q + part * width, 16), width)
            wg_ref[rows, :] = found[:, part * LANES : (part + 1) * LANES]
        for at_p in range(pairs):

            @pl.when(p == at_p)
            def _(at_p=at_p):
                stage("scatter", "q%d" % at_p)

    for copy in own_columns(place, wall_ref, w_ref, wsem):
        copy.wait()

    def aside(j):
        return remote(gn_ref.at[j], gnrecv_ref.at[j], gsend.at[j], grecv.at[j], partner)

    def leave(j):
        src, dst, arrival = gn_ref.at[4 + j], slots_ref.at[lax.rem(place.q, 2), core], orecv.at[lax.rem(place.q, 2), core]
        device = place.owner(place.q, j)
        return place.is_me(device), remote(src, dst, osend.at[j], arrival, device), pltpu.make_async_copy(src, dst, arrival)

    def normed_grad(i):
        rows = pl.ds(pl.multiple_of(i * TILE, TILE), TILE)
        grads = jnp.concatenate([pg_ref[g, rows, :] for g in range(3 * pairs)], axis=1)
        grad = dot_nt(grads, w_ref[...])
        return grad, folded(grad * normed_ref[rows, :].astype(F32))

    gain_grad = jnp.zeros((8, width), F32)
    for j in range(4):
        grad, part = normed_grad(2 * j + 1 - core)
        gain_grad = gain_grad + part
        for i in range(slabs):
            gn_ref[j, i * TILE : (i + 1) * TILE, :] = grad[:, i * LANES : (i + 1) * LANES].astype(B16)
        aside(j).start()
    for j in range(4):
        grad, part = normed_grad(2 * j + core)
        gain_grad = gain_grad + part
        arrived(gnrecv_ref.at[j], grecv.at[j])
        for i in range(slabs):
            rows = slice(i * TILE, (i + 1) * TILE)
            gn_ref[4 + j, rows, :] = (
                grad[:, i * LANES : (i + 1) * LANES] + gnrecv_ref[j, rows, :].astype(F32)
            ).astype(B16)
        mine, far, near = leave(j)

        @pl.when(jnp.logical_not(mine))
        def _():
            far.start()

        @pl.when(mine)
        def _():
            near.start()

    bottom = lax.broadcasted_iota(jnp.int32, sbuf_ref.shape[1:], 0) == sbuf_ref.shape[1] - 1
    sbuf_ref[0] = jnp.where(bottom, jnp.sum(gain_grad, axis=0, keepdims=True), small_ref[...])
    (seq_me, _, seq_device), (z_me, _, z_device) = last.levels
    levels = [(seq_me, seq_device, srecv1_ref, 1), (z_me, z_device, srecv2_ref, 4)]

    def swap():
        return remote(sbuf_ref.at[0], srecv0_ref, ssend.at[0], srecv.at[0, 0], partner)

    def spread(level):
        me, device, into, at = levels[level]
        for d in (1, 2, 3):
            yield remote(
                sbuf_ref.at[level + 1], into.at[me], ssend.at[at + d - 1], srecv.at[level + 1, me],
                device(lax.rem(me + d, 4)),
            )

    def small_stage(level):
        if level == 0:
            arrived(srecv0_ref, srecv.at[0, 0])
            value = sbuf_ref[0] + srecv0_ref[...]
        else:
            me, device, into, at = levels[level - 1]
            into[me] = sbuf_ref[level]
            for d in (1, 2, 3):
                i = lax.rem(me + d, 4)
                arrived(into.at[i], srecv.at[level, i])
            value = into[0] + into[1] + into[2] + into[3]
        if level == 2:
            total_ref[...] = value
        else:
            sbuf_ref[level + 1] = value
            for copy in spread(level):
                copy.start()

    def finish_inputs():
        for copy in inputs:
            copy.wait()
        for s in range(2):
            for h in range(2):
                arrived(slots_ref.at[s, h], orecv.at[s, h])
                rows = slice(h * TILE, (h + 1) * TILE)
                unit, spread = center_of(xin_ref[s, rows, :].astype(F32))
                grad = [slots_ref[s, h, i * TILE : (i + 1) * TILE, :] for i in range(slabs)]
                unit_grad = jnp.concatenate(grad, axis=1).astype(F32) * gain_ref[...].reshape(1, width)
                back = spread * (
                    unit_grad
                    - jnp.mean(unit_grad, -1, keepdims=True)
                    - unit * jnp.mean(unit_grad * unit, -1, keepdims=True)
                )
                input_ref[s, rows, :] = (gmidin_ref[s, rows, :] + back).astype(B16)

    swap().start()
    for number, (name, key) in enumerate(LATE):
        stage(name, key)
        if number in SMALL:
            small_stage(SMALL.index(number))
        if number == FINISH:
            finish_inputs()
    for j in range(4):
        mine, far, _ = leave(j)

        @pl.when(jnp.logical_not(mine))
        def _():
            far.wait_send()

        aside(j).wait_send()
    swap().wait_send()
    for level in (0, 1):
        for copy in spread(level):
            copy.wait_send()
    for key, (family, unit) in units.items():
        levels = range(len(family.levels))
        family.close(unit, out={"e0": (), "e1": (1,)}.get(key, levels), back=(0,) if key == "e0" else levels)
        family.end(unit)


def summing_back(qp, kp, vp, grad, att, cosine, sine, normed, small, half_sum, mine, outmine, gain, w_all, x, gmid, sums):
    total, width = normed.shape
    pairs = att.shape[0]
    slabs = width // LANES
    rows_e, rows_o, rows_q = mine.shape[0], outmine.shape[0], 3 * width
    dma = pltpu.SemaphoreType.DMA

    def shape(dims, kind=B16):
        return jax.ShapeDtypeStruct(dims, kind)

    return pl.pallas_call(
        functools.partial(summing_back_kernel, pairs),
        out_shape=(
            shape((UNITS, 2, rows_e, LANES)), shape((1, 2, rows_o, LANES)), shape((pairs, 2, rows_q, LANES)),
            shape(small.shape, F32), shape(x.shape),
        ),
        in_specs=[ANY] * 8 + [VMEM] * 5 + [ANY] * 4,
        out_specs=(ANY,) * 3 + (VMEM,) * 2,
        input_output_aliases={16: 0},
        scratch_shapes=[
            pltpu.VMEM((2, total, LANES), B16),
            pltpu.VMEM((2, HD, total), B16),
            pltpu.VMEM((2, HD, total), F32),
            pltpu.VMEM((3 * pairs, total, LANES), B16),
            pltpu.VMEM((width, 3 * pairs * LANES), B16),
            pltpu.VMEM((pairs * rows_q, LANES), B16),
            pltpu.VMEM((8, slabs * TILE, LANES), B16),
            pltpu.VMEM((4, slabs * TILE, LANES), B16),
            pltpu.VMEM((3,) + small.shape, F32),
            pltpu.VMEM(small.shape, F32),
            pltpu.VMEM((4,) + small.shape, F32),
            pltpu.VMEM((4,) + small.shape, F32),
            pltpu.VMEM((2, 2, slabs * TILE, LANES), B16),
            pltpu.VMEM(x.shape, B16),
            pltpu.VMEM(gmid.shape, F32),
            *(pltpu.VMEM(value.shape, value.dtype) for value in (qp, kp, vp, grad, att, cosine, sine, normed)),
            dma((pairs, 5)), dma((3,)), dma((3,)), dma((2,)), dma((4,)), dma((4,)), dma((4,)), dma((2, 2)), dma((7,)), dma((3, 4)),
            *sum_buffers(FAMILIES["e"], 1, rows_e), *sum_buffers(FAMILIES["o"], 1, rows_o),
            *(buf for p in range(pairs) for buf in sum_buffers(FAMILIES["q%d" % p], 1, rows_q)),
            *(sem for _ in range(UNITS) for sem in sum_sems(FAMILIES["e"], 1)), *sum_sems(FAMILIES["o"], 1),
            *(sem for p in range(pairs) for sem in sum_sems(FAMILIES["q%d" % p], 1)),
            *sum_buffers(FAMILIES["e"][1:], 1, rows_e // 4),
        ],
        compiler_params=pltpu.CompilerParams(
            vmem_limit_bytes=62 * 2**20, collective_id=3, has_side_effects=True
        ),
        cost_estimate=pl.CostEstimate(flops=60 * 10**9, bytes_accessed=60 * 2**20, transcendentals=13 * 10**6),
        name="attention_backward_and_sums",
    )(qp, kp, vp, grad, att, cosine, sine, normed, small, half_sum, mine, outmine, gain, w_all, x, gmid, sums)


def widen_kernel(downt_ref, upt_ref, outs_ref, q_ref, down_ref, up_ref, out_ref, qkv_ref):
    width = out_ref.shape[1]
    for i in range(2):
        down_ref[i * LANES : (i + 1) * LANES, :] = jnp.transpose(downt_ref[i * width : (i + 1) * width, :].astype(F32))
    at = 0
    for unit in range(upt_ref.shape[0]):
        for i in range(upt_ref.shape[2]):
            up_ref[:, at : at + LANES] = upt_ref[unit, 0, i].astype(F32)
            at += LANES
    for i in range(outs_ref.shape[0]):
        out_ref[:, i * LANES : (i + 1) * LANES] = outs_ref[i].astype(F32)
    at = 0
    for part in range(3):
        for u in range(q_ref.shape[1]):
            for p in range(q_ref.shape[0]):
                qkv_ref[:, at : at + LANES] = q_ref[p, u, part].astype(F32)
                at += LANES


def widen(sums, osums, qsums, width, inner):
    steps = inner // (2 * LANES)
    pairs, share = qsums.shape[:2]
    slabs = width // LANES
    some = width // steps
    turn = steps // UNITS

    def shape(dims):
        return jax.ShapeDtypeStruct(dims, F32)

    def by_row(columns):
        return pl.BlockSpec((some, columns), lambda c: (c, 0))

    return pl.pallas_call(
        widen_kernel,
        grid=(steps,),
        out_shape=(shape((inner, width)), shape((width, inner)), shape((width, width)), shape((width, 3 * width))),
        in_specs=[
            pl.BlockSpec((2 * width, LANES), lambda c: (lax.div(c, turn) * 2 * turn + lax.rem(c, turn), 0)),
            pl.BlockSpec((UNITS, 1, 2 * turn, some, LANES), lambda c: (0, 1, 0, c, 0)),
            pl.BlockSpec((slabs, some, LANES), lambda c: (0, c, 0)),
            pl.BlockSpec((pairs, share, 3, some, LANES), lambda c: (0, 0, 0, c, 0)),
        ],
        out_specs=(
            pl.BlockSpec((2 * LANES, width), lambda c: (c, 0)), by_row(inner), by_row(width), by_row(3 * width)
        ),
        compiler_params=pltpu.CompilerParams(vmem_limit_bytes=62 * 2**20),
        name="widen_sums",
    )(
        sums.reshape(-1, LANES), sums.reshape(UNITS, 2, 2 * turn, width, LANES), osums.reshape(slabs, width, LANES),
        qsums.reshape(pairs, share, 3, width, LANES),
    )


def slabs_of(ref, s, rows):
    return jnp.concatenate([ref[s, u, p, rows, :] for u in range(ref.shape[1]) for p in range(ref.shape[2])], axis=1)


def folded(values):
    return jnp.sum(values.reshape(values.shape[0] // 8, 8, values.shape[1]), axis=0)


LAST = 2
ORDER = ("seq", "z")


def swap_half(width):
    return PIECE * width // LANES


def loss_factor(alllen_ref, slots):
    count = None
    for b in range(alllen_ref.shape[0]):
        for s in (0, 1):
            part = alllen_ref[b, s, 0:1, :]
            count = part if count is None else count + part
    return slots / count.astype(F32)


def middle_kernel(
    kept, steps, hist_steps, summing, scale_ref, len_ref, alllen_ref, o_ref, x_ref, cot_ref, wout_ref, gain_ref, up_ref,
    down_ref, hist_ref, mixed_ref, gmid_ref, do_ref, small_ref, *rest,
):
    if summing:
        sums_ref, half_sum_ref, mine_ref, outmine_ref = rest[:4]
        rest = rest[4:]
    else:
        grads_ref, outg_ref = rest[:2]
        rest = rest[2:]
    (
        middle_ref, ntwo_ref, gmlp_ref, ntwot_ref, gmlpt_ref, blk_ref, gntwo_ref, og_ref, act_ref, pre_ref, gaing_ref,
        mixg_ref, gatt_ref, send, recv,
    ) = rest[:15]
    place = Place()
    core = place.core
    step = pl.program_id(0)
    rows_all, width = x_ref.shape
    block = o_ref.shape[3]
    slab = hist_ref.shape[1]
    slabs = width // LANES
    own = scale_ref[kept]
    factor = loss_factor(alllen_ref, place.batches * 2 * place.count * block)
    gain = gain_ref[...].reshape(1, width)

    def grad_top(start, count):
        s = lax.div(start, block)
        index = lax.broadcasted_iota(jnp.int32, (count, LANES), 0) + lax.rem(start, block) + place.k * block
        scale = jnp.where(index < len_ref[s], factor, 0.0)[:, :1]
        return cot_ref[pl.ds(pl.multiple_of(start, count), count), :].astype(F32) * scale

    def leave(t, u):
        s, part = t * TILE // block, t * TILE % block // TILE
        within = pl.ds(part * TILE, TILE)
        src, dst, arrival = gatt_ref.at[s, u, :, within, :], do_ref.at[place.k, :, within, :], recv.at[place.k, part]
        device = place.worker(2 * place.core + s, u)
        return place.is_me(device), remote(src, dst, send.at[t, u], arrival, device), pltpu.make_async_copy(src, dst, arrival)

    @pl.when(step == 0)
    def _():
        greet(place, (core,) if summing else ())

    if summing:
        early_ref, landing_ref, lout_ref, aside_ref, aout_ref = rest[15:20]
        xsend, xrecv = rest[20:22]
        half = swap_half(width)
        partner = (place.base + 1 - core, place.k)

        def chunk_of(unit):
            return early_ref.at[pl.ds(unit * 2 * half, 2 * half)]

        sums = Sum(place, ORDER, 2 * half, chunk_of, rest[22:26], sums_ref, 0, rest[26:])

        def cross(c):
            return remote(aside_ref.at[c % 2], landing_ref.at[c % 4], xsend.at[c], xrecv.at[c], partner)

        def cross_out():
            return remote(aout_ref, lout_ref, xsend.at[steps], xrecv.at[steps], partner)

        def hold(c, down, up):
            if c >= 2:
                cross(c - 2).wait_send()
            into = early_ref.at[pl.ds(c * half, half)] if c < 2 * LAST else mine_ref.at[pl.ds((c - 2 * LAST) * half, half)]
            for i in range(PIECE // LANES):
                rows, lanes = slice(i * width, (i + 1) * width), slice(i * LANES, (i + 1) * LANES)
                first = jnp.where(core == 0, down[:, lanes], up[:, lanes])
                other = jnp.where(core == 0, up[:, lanes], down[:, lanes])
                into[rows, :] = first.astype(B16)
                aside_ref[c % 2, rows, :] = other.astype(B16)
            cross(c).start()

        def add(c):
            arrived(landing_ref.at[c % 4], xrecv.at[c])
            into = early_ref.at[pl.ds(c * half, half)] if c < 2 * LAST else mine_ref.at[pl.ds((c - 2 * LAST) * half, half)]
            for i in range(PIECE // LANES):
                rows = slice(i * width, (i + 1) * width)
                into[rows, :] = (into[rows, :].astype(F32) + landing_ref[c % 4, rows, :].astype(F32)).astype(B16)

        def between(c):
            if c >= 1:
                add(c - 1)
            if c == 2:
                sums.scatter(0)
            if c == 4:
                sums.scatter(1)
            if c == 5:
                sums.sum(0, 0)

    @pl.when(step == 0)
    def _():
        for t in range(rows_all // TILE):
            rows = slice(t * TILE, (t + 1) * TILE)
            within = t * TILE % block
            att = slabs_of(o_ref, t * TILE // block, slice(within, within + TILE))
            middle = x_ref[rows, :].astype(F32) + dot(att, wout_ref[...])
            middle_ref[rows, :] = middle
            unit, _ = center_of(middle)
            ntwo = unit * gain
            gmlp = own * grad_top(t * TILE, TILE)
            ntwo_ref[rows, :] = ntwo.astype(B16)
            gmlp_ref[rows, :] = gmlp.astype(B16)
            ntwot_ref[:, rows] = jnp.transpose(ntwo).astype(B16)
            gmlpt_ref[:, rows] = jnp.transpose(gmlp).astype(B16)
            blk_ref[rows, :] = middle
            gntwo_ref[rows, :] = jnp.zeros((TILE, width), F32)
        mixg_ref[...] = jnp.zeros_like(mixg_ref)
        gaing_ref[...] = jnp.zeros_like(gaing_ref)
        og_ref[...] = jnp.zeros_like(og_ref)

    @pl.when(step < steps)
    def _():
        up, down = up_ref[...], down_ref[...]
        slope = math.sqrt(2.0 / math.pi)
        for t in range(rows_all // ROWS):
            rows = slice(t * ROWS, (t + 1) * ROWS)
            pre = dot(ntwo_ref[rows, :], up)
            square = pre * pre
            bent = jnp.tanh(slope * pre * (1.0 + 0.044715 * square))
            half_ = 0.5 + 0.5 * bent
            act = (pre * half_).astype(B16)
            slopes = half_ + 0.5 * slope * pre * (1.0 - bent * bent) * (1.0 + 3 * 0.044715 * square)
            pre_grad = (dot_nt(gmlp_ref[rows, :], down) * slopes).astype(B16)
            act_ref[rows, :] = act
            pre_ref[rows, :] = pre_grad
            blk_ref[rows, :] += dot(act, down)
            gntwo_ref[rows, :] += dot_nt(pre_grad, up)
        if summing:
            for c in range(steps):

                @pl.when(step == c)
                def _(c=c):
                    between(c)

    @pl.when(step == steps - 1)
    def _():
        for t in range(rows_all // TILE):
            rows = slice(t * TILE, (t + 1) * TILE)
            s, within = t * TILE // block, t * TILE % block
            top = grad_top(t * TILE, TILE)
            unit, spread = center_of(middle_ref[rows, :])
            gain_grad = gntwo_ref[rows, :]
            gaing_ref[...] += folded(gain_grad * unit)
            unit_grad = gain_grad * gain
            back = spread * (
                unit_grad
                - jnp.mean(unit_grad, -1, keepdims=True)
                - unit * jnp.mean(unit_grad * unit, -1, keepdims=True)
            )
            total = own * top + back
            gmid_ref[rows, :] = total
            att_grad = dot_nt(total.astype(B16), wout_ref[...]).astype(B16)
            at = 0
            for u in range(o_ref.shape[1]):
                for p in range(o_ref.shape[2]):
                    gatt_ref[s, u, p, within : within + TILE, :] = att_grad[:, at : at + LANES]
                    at += LANES
                mine, far, near = leave(t, u)

                @pl.when(jnp.logical_not(mine))
                def _():
                    far.start()

                @pl.when(mine)
                def _():
                    near.start()
    @pl.when(step < steps)
    def _():
        downg = dot(gmlpt_ref[...], act_ref[...])
        upg = dot(ntwot_ref[...], pre_ref[...])
        if summing:
            for c in range(steps):

                @pl.when(step == c)
                def _(c=c):
                    hold(c, downg, upg)
        else:
            for i in range(PIECE // LANES):
                lanes = slice(i * LANES, (i + 1) * LANES)
                grads_ref[0, i * width : (i + 1) * width, :] = downg[:, lanes].astype(B16)
                at = PIECE * slabs + i * width
                grads_ref[0, at : at + width, :] = upg[:, lanes].astype(B16)

    @pl.when(step == steps - 1)
    def _():
        for t in range(rows_all // TILE):
            rows = slice(t * TILE, (t + 1) * TILE)
            s, within = t * TILE // block, t * TILE % block
            og_ref[...] += dot_tn(slabs_of(o_ref, s, slice(within, within + TILE)), gmid_ref[rows, :].astype(B16))
        if summing:
            for i in range(slabs // 2):
                rows = slice(i * width, (i + 1) * width)
                left, right = og_ref[:, i * LANES : (i + 1) * LANES], og_ref[:, (i + slabs // 2) * LANES : (i + slabs // 2 + 1) * LANES]
                outmine_ref[rows, :] = jnp.where(core == 0, left, right).astype(B16)
                aout_ref[rows, :] = jnp.where(core == 0, right, left).astype(B16)
            cross_out().start()
        else:
            outg_ref[...] = og_ref[...].astype(B16)

    @pl.when(step >= steps)
    def _():
        start = pl.multiple_of((step - steps) * slab, slab)
        top = grad_top(start, slab)
        out = blk_ref[pl.ds(start, slab), :]
        mixed = own * out
        mixg_ref[kept] += folded(out * top)
        for j in range(kept):
            stored = hist_ref[j].astype(F32)
            mixed = mixed + scale_ref[j] * stored
            mixg_ref[j] += folded(stored * top)
        mixed_ref[...] = mixed.astype(B16)

    if summing:

        @pl.when(step == steps)
        def _():
            sums.sum(0, 1)
            sums.share(0)

        @pl.when(step == steps + 2)
        def _():
            add(5)

        @pl.when(step == steps + 4)
        def _():
            sums.sum(1, 0, onward=False)
            half_sum_ref[...] = rest[23][1]

        @pl.when(step == steps + hist_steps - 1)
        def _():
            arrived(lout_ref, xrecv.at[steps])
            for i in range(slabs // 2):
                rows = slice(i * width, (i + 1) * width)
                outmine_ref[rows, :] = (outmine_ref[rows, :].astype(F32) + lout_ref[rows, :].astype(F32)).astype(B16)
            sums.collect(0, 1)
            sums.close(0, out=(0, 1), back=(1,))
            sums.close(1, out=(0,))
            for c in (steps - 2, steps - 1):
                cross(c).wait_send()
            cross_out().wait_send()

    @pl.when(step == steps + hist_steps - 1)
    def _():
        small_ref[0:1, :] = jnp.sum(gaing_ref[...], axis=0, keepdims=True)
        for j in range(kept + 1):
            small_ref[j + 1 : j + 2, :] = jnp.sum(mixg_ref[j], axis=0, keepdims=True)
        small_ref[kept + 2 :, :] = jnp.zeros((small_ref.shape[0] - kept - 2, width), F32)
        for part in range(block // TILE):
            for j in range(place.count):
                arrived(do_ref.at[j, :, pl.ds(part * TILE, TILE), :], recv.at[j, part])
        for t in range(rows_all // TILE):
            for u in range(place.share):
                mine, far, _ = leave(t, u)

                @pl.when(jnp.logical_not(mine))
                def _():
                    far.wait_send()


def middle_part(scale, lengths, all_lengths, o, x, cot, wout, gain, up, down, hist, summing):
    rows, width = x.shape
    kept = hist.shape[0]
    inner = up.shape[1]
    steps = inner // PIECE
    hist_steps = 8
    slab = rows // hist_steps
    _, share, pairs, block, _ = o.shape
    blocks = 2 * share
    dma = pltpu.SemaphoreType.DMA
    slabs = width // LANES
    half = swap_half(width)

    def fixed(values):
        zeros = (0,) * len(values.shape)
        return pl.BlockSpec(values.shape, lambda c: zeros, pipeline_mode=pl.Buffered(1))

    def shape(dims, kind):
        return jax.ShapeDtypeStruct(dims, kind)

    hist_spec = pl.BlockSpec((kept, slab, width), lambda c: (0, jnp.maximum(c - steps, 0), 0))
    mixed_spec = pl.BlockSpec((slab, width), lambda c: (jnp.maximum(c - steps, 0), 0))
    up_spec = pl.BlockSpec((width, PIECE), lambda c: (0, jnp.minimum(c, steps - 1)))
    down_spec = pl.BlockSpec((PIECE, width), lambda c: (jnp.minimum(c, steps - 1), 0))
    gmid = shape((rows, width), F32)
    small = shape((16, width), F32)
    outs = [shape((rows, width), B16), gmid, shape((blocks, pairs, block, LANES), B16), small]
    out_specs = [mixed_spec, fixed(gmid), ANY, fixed(small)]
    scratch = [
        pltpu.VMEM((rows, width), F32),
        pltpu.VMEM((rows, width), B16),
        pltpu.VMEM((rows, width), B16),
        pltpu.VMEM((width, rows), B16),
        pltpu.VMEM((width, rows), B16),
        pltpu.VMEM((rows, width), F32),
        pltpu.VMEM((rows, width), F32),
        pltpu.VMEM(wout.shape, F32),
        pltpu.VMEM((rows, PIECE), B16),
        pltpu.VMEM((rows, PIECE), B16),
        pltpu.VMEM((8, width), F32),
        pltpu.VMEM((kept + 1, 8, width), F32),
        pltpu.VMEM(o.shape, B16),
        dma((rows // TILE, share)), dma((blocks, block // TILE)),
    ]
    if summing:
        out_rows = slabs // 2 * width
        more = [
            shape((LAST + 1, 2, 2 * half, LANES), B16), shape((half // 2, LANES), B16), shape((2 * half, LANES), B16),
            shape((out_rows, LANES), B16),
        ]
        scratch += [
            pltpu.VMEM((LAST * 2 * half, LANES), B16),
            pltpu.VMEM((4, half, LANES), B16),
            pltpu.VMEM((out_rows, LANES), B16),
            pltpu.VMEM((2, half, LANES), B16),
            pltpu.VMEM((out_rows, LANES), B16),
            dma((steps + 1,)), dma((steps + 1,)),
            *sum_buffers(ORDER, LAST, 2 * half), *sum_sems(ORDER, LAST),
        ]
        outs += more
        out_specs += [ANY] + [fixed(value) for value in more[1:]]
    else:
        outs += [shape((steps, 2 * half, LANES), B16), shape(wout.shape, B16)]
        out_specs += [pl.BlockSpec((1, 2 * half, LANES), lambda c: (jnp.minimum(c, steps - 1), 0, 0)), fixed(outs[-1])]
    return pl.pallas_call(
        functools.partial(middle_kernel, kept, steps, hist_steps, summing),
        grid=(steps + hist_steps,),
        out_shape=tuple(outs),
        in_specs=[SMEM, SMEM, fixed(all_lengths), fixed(o), fixed(x), fixed(cot), fixed(wout), fixed(gain), up_spec, down_spec, hist_spec],
        out_specs=tuple(out_specs),
        scratch_shapes=scratch,
        compiler_params=pltpu.CompilerParams(
            vmem_limit_bytes=62 * 2**20, collective_id=2, has_side_effects=True
        ),
        cost_estimate=pl.CostEstimate(flops=33 * 10**9, bytes_accessed=60 * 2**20, transcendentals=3 * 10**6),
        name="mlp_both_ways",
    )(scale, lengths, all_lengths, o, x, cot, wout, gain, up, down, hist)


def history_kernel(block, scale_ref, len_ref, alllen_ref, cot_ref, hgrad_ref):
    place = Place()
    factor = loss_factor(alllen_ref, place.batches * 2 * place.count * block)
    kept, count, _ = hgrad_ref.shape
    start = pl.program_id(1) * count + place.k * block
    index = lax.broadcasted_iota(jnp.int32, (count, LANES), 0) + start
    scale = jnp.where(index < len_ref[pl.program_id(0)], factor, 0.0)[:, :1]
    top = cot_ref[...].astype(F32) * scale
    for j in range(kept):
        hgrad_ref[j] = (scale_ref[j] * top).astype(B16)


def history_part(scale, lengths, all_lengths, cot, kept, block):
    rows, width = cot.shape
    tiles = block // TILE
    return pl.pallas_call(
        functools.partial(history_kernel, block),
        grid=(rows // block, tiles),
        out_shape=jax.ShapeDtypeStruct((kept, rows, width), B16),
        in_specs=[
            SMEM, SMEM, pl.BlockSpec(all_lengths.shape, lambda s, t: (0, 0, 0, 0)),
            pl.BlockSpec((TILE, width), lambda s, t: (s * tiles + t, 0)),
        ],
        out_specs=pl.BlockSpec((kept, TILE, width), lambda s, t: (0, s * tiles + t, 0)),
        compiler_params=pltpu.CompilerParams(vmem_limit_bytes=62 * 2**20),
        cost_estimate=pl.CostEstimate(flops=10**7, bytes_accessed=14 * 2**20, transcendentals=0),
        name="history_gradient",
    )(scale, lengths, all_lengths, cot)


def finish_kernel(x_ref, gain_ref, gmid_ref, gn_ref, out_ref):
    unit, spread = center_of(x_ref[0].astype(F32))
    unit_grad = jnp.concatenate([gn_ref[0, 0, i] for i in range(gn_ref.shape[2])], axis=1).astype(F32) * gain_ref[...]
    back = spread * (
        unit_grad - jnp.mean(unit_grad, -1, keepdims=True) - unit * jnp.mean(unit_grad * unit, -1, keepdims=True)
    )
    out_ref[0] = (gmid_ref[0] + back).astype(B16)


def finish(x, gain, gmid, gn):
    seqs, block, width = x.shape
    by_row = pl.BlockSpec((1, TILE, width), lambda s, t: (s, t, 0))
    return pl.pallas_call(
        finish_kernel,
        grid=(seqs, block // TILE),
        out_shape=jax.ShapeDtypeStruct(x.shape, B16),
        in_specs=[
            by_row,
            pl.BlockSpec(gain.shape, lambda s, t: (0, 0)),
            by_row,
            pl.BlockSpec((1, 1, width // LANES, TILE, LANES), lambda s, t: (s, t, 0, 0, 0)),
        ],
        out_specs=by_row,
        compiler_params=pltpu.CompilerParams(vmem_limit_bytes=62 * 2**20),
        name="norm_backward",
    )(x, gain, gmid, gn)


def whole_pairs(weight, heads):
    if heads % 2 == 0:
        return weight
    parted = weight.reshape(weight.shape[0], -1, heads * HD)
    return jnp.pad(parted, ((0, 0), (0, 0), (0, HD))).reshape(weight.shape[0], -1)


def body(
    tokens, history, cotangent, qkv_weight, out_weight, up_weight, down_weight, attn_gain, mlp_gain, depth_mix, lengths,
    positions,
):
    seqs, block, width = tokens.shape
    kept = history.shape[0]
    n = lax.axis_size("seq")
    batches = lax.axis_size("batch")
    place = Place()
    share = n // 2
    heads = H // share
    pairs = (heads + 1) // 2
    rows = seqs * block
    total = n * block

    wide_qkv = whole_pairs(qkv_weight, heads)
    o, att, normed, qp, kp, vp, cosine, sine, all_lengths = attend(tokens, positions, lengths, wide_qkv, attn_gain)

    wide_out = jnp.pad(
        out_weight.reshape(share, heads * HD, width), ((0, 0), (0, (2 * pairs - heads) * HD), (0, 0))
    ).reshape(-1, width)
    summing = n == 4 and batches == 8
    hgrad = history_part(depth_mix, lengths, all_lengths, cotangent.reshape(rows, width), kept, block)
    mixed, gmid, grad, small, *parts = middle_part(
        depth_mix, lengths, all_lengths, o, tokens.reshape(rows, width), cotangent.reshape(rows, width), wide_out, mlp_gain, up_weight,
        down_weight, history.reshape(kept, rows, width), summing,
    )
    inner = up_weight.shape[1]
    slabs = width // LANES
    if summing:
        early_sums, half_sum, own_grads, own_out = parts
        sums, osums, qsums, small, input_grad = summing_back(
            qp, kp, vp, grad, att, cosine, sine, normed, small, half_sum[None], own_grads, own_out, attn_gain, wide_qkv,
            tokens, gmid.reshape(tokens.shape), early_sums,
        )
        down_grad, up_grad, out_grad, qkv_grad = widen(sums, osums, qsums, width, inner)
    else:
        qkvg, gn, gain_part = plain_back(qp, kp, vp, grad, att, cosine, sine, normed, wide_qkv)
        slots = to_owners(gn.reshape(n, block, width), "exchange_normed_grad", 3)
        normed_grad = slots.astype(F32).sum(1).reshape(seqs, block // TILE, TILE, slabs, LANES).swapaxes(2, 3)
        small = lax.psum(small.at[-1].set(gain_part.sum(0)), ("batch", "seq"))
        mine = qkvg.reshape(width, 3, 1, 2 * pairs * HD)[..., : heads * HD]
        spread = jnp.zeros((width, 3, share, heads * HD), B16)
        spread = lax.dynamic_update_slice(spread, mine, (0, 0, place.u, 0)).reshape(width, -1)
        both, out_grad, qkv_grad = (v.astype(F32) for v in lax.psum((*parts, spread), ("batch", "seq")))
        chunks = jnp.moveaxis(both.reshape(inner // PIECE, 2, PIECE // LANES, width, LANES), 3, 1)
        down_grad = chunks[:, :, 0].swapaxes(0, 1).reshape(width, inner).T
        up_grad = chunks[:, :, 1].swapaxes(0, 1).reshape(width, inner)
        out_grad = out_grad.reshape(share, 2 * pairs * HD, width)[:, : heads * HD].reshape(H * HD, width)
        input_grad = finish(tokens, attn_gain[None, :], gmid.reshape(tokens.shape), normed_grad)
    return (
        mixed.reshape(tokens.shape),
        input_grad,
        hgrad.reshape(history.shape),
        qkv_grad,
        out_grad,
        up_grad,
        down_grad,
        small[-1] / attn_gain,
        small[0],
        small[1 : kept + 2].sum(1),
    )


def solution(mesh):
    placed = (
        P("batch", "seq", None),
        P(None, "batch", "seq", None),
        P("batch", "seq", None),
        P(),
        P(),
        P(),
        P(),
        P(),
        P(),
        P(),
        P("batch"),
        P("batch", "seq"),
    )
    return jax.shard_map(
        body,
        mesh=mesh,
        in_specs=placed,
        out_specs=(
            P("batch", "seq", None),
            P("batch", "seq", None),
            P(None, "batch", "seq", None),
            P(),
            P(),
            P(),
            P(),
            P(),
            P(),
            P(),
        ),
        check_vma=False,
    )
```

```python
import functools
import math

import jax
import jax.numpy as jnp
import numpy as np
from jax import lax
from jax.experimental import pallas as pl
from jax.experimental.pallas import tpu as pltpu
from jax.sharding import PartitionSpec as P

H = 12
HD = 64
LANES = 128
TILE = 256
PIECE = 512
QUERIES = 256
ROWS = 512
NEGATIVE = -1e30
epsilon = 1e-05
MESH = pl.DeviceIdType.MESH
F32 = jnp.float32
B16 = jnp.bfloat16
VMEM = pl.BlockSpec(memory_space=pltpu.VMEM)
SMEM = pl.BlockSpec(memory_space=pltpu.SMEM)
ANY = pl.BlockSpec(memory_space=pl.ANY)


def dot(a, b):
    return jnp.dot(a, b, preferred_element_type=F32)


def dot_nt(a, b):
    return lax.dot_general(a, b, (((1,), (1,)), ((), ())), preferred_element_type=F32)


def dot_tn(a, b):
    return lax.dot_general(a, b, (((0,), (0,)), ((), ())), preferred_element_type=F32)


def turned(values):
    return jnp.transpose(values)


def lane_of(shape):
    return lax.broadcasted_iota(jnp.int32, shape, 1)


def three(values):
    high = values.astype(B16).astype(F32)
    rest = values - high
    middle = rest.astype(B16).astype(F32)
    return high, middle, rest - middle


class Place:
    def __init__(self):
        self.count = lax.axis_size("seq")
        self.each = self.count // 4
        self.share = 2 * self.each
        self.batches = lax.axis_size("batch")
        self.b = lax.axis_index("batch")
        self.k = lax.axis_index("seq")
        self.core = lax.rem(self.b, 2)
        self.base = self.b - self.core
        self.q = lax.div(self.k, self.each)
        self.u = lax.rem(self.k, self.each) * 2 + self.core

    def worker(self, q, u):
        return (self.base + u % 2, q * self.each + u // 2)

    def owner(self, q, j):
        return (self.base + lax.div(q, 2), j)

    def is_me(self, device):
        return jnp.logical_and(device[0] == self.b, device[1] == self.k)


def greet(place, other_planes=()):
    barrier = pltpu.get_barrier_semaphore()
    met = 0
    for other in (0, 1):
        for step in range(place.count):
            if other == 0 and step == 0:
                continue
            core = lax.rem(place.core + other, 2)
            k = lax.rem(place.k + step, place.count)
            pl.semaphore_signal(barrier, inc=1, device_id=(place.base + core, k), device_id_type=MESH)
            met += 1
    for step in range(place.batches // 2 - 1):
        base = lax.rem(place.base + 2 * (step + 1), place.batches)
        for core in other_planes:
            pl.semaphore_signal(barrier, inc=1, device_id=(base + core, place.k), device_id_type=MESH)
            met += 1
    pl.semaphore_wait(barrier, met)


class Copies:
    def __init__(self, place):
        self.place = place
        self.sent = []

    def post(self, src, dst, send_sem, recv_sem, device):
        mine = self.place.is_me(device)
        far = pltpu.make_async_remote_copy(
            src_ref=src, dst_ref=dst, send_sem=send_sem, recv_sem=recv_sem,
            device_id=device, device_id_type=MESH,
        )

        @pl.when(jnp.logical_not(mine))
        def _():
            far.start()

        @pl.when(mine)
        def _():
            pltpu.make_async_copy(src, dst, recv_sem).start()

        self.sent.append((mine, far))

    def drain(self):
        for mine, far in self.sent:
            @pl.when(jnp.logical_not(mine))
            def _():
                far.wait_send()


def remote(src, dst, send_sem, recv_sem, device):
    return pltpu.make_async_remote_copy(
        src_ref=src, dst_ref=dst, send_sem=send_sem, recv_sem=recv_sem, device_id=device, device_id_type=MESH
    )


def arrived(slot, sem):
    pltpu.make_async_copy(slot, slot, sem).wait()


def to_owners_kernel(src_ref, dst_ref, send, recv):
    place = Place()
    greet(place)
    copies = Copies(place)
    for step in range(place.count):
        j = lax.rem(place.k + step, place.count)
        s = lax.rem(place.q, 2)
        copies.post(src_ref.at[j], dst_ref.at[s, place.u], send.at[step], recv.at[s, place.u], place.owner(place.q, j))
    for s in (0, 1):
        for u in range(place.share):
            arrived(dst_ref.at[s, u], recv.at[s, u])
    copies.drain()


def to_owners(values, name, number):
    n = lax.axis_size("seq")
    dma = pltpu.SemaphoreType.DMA
    return pl.pallas_call(
        to_owners_kernel,
        out_shape=jax.ShapeDtypeStruct((2, n // 2) + values.shape[1:], values.dtype),
        in_specs=[ANY],
        out_specs=ANY,
        scratch_shapes=[dma((n,)), dma((2, n // 2))],
        compiler_params=pltpu.CompilerParams(collective_id=number, has_side_effects=True),
        name=name,
    )(values)


class Sum:
    def __init__(self, place, order, rows, source, bufs, result, first, sems):
        groups = {
            "z": (lax.div(place.base, 2), 4, lambda i: (2 * i + place.core, place.k)),
            "seq": (place.k, 4, lambda i: (place.b, i)),
            "all": (2 * place.base + place.k, 16, lambda i: (2 * lax.div(i, 4) + place.core, lax.rem(i, 4))),
        }
        self.levels = [groups[name] for name in order]
        self.rows = []
        for _, size, _ in self.levels:
            rows = rows // size
            self.rows.append(rows)
        count = len(order)
        self.core = place.core
        self.partner = (place.base + 1 - place.core, place.k)
        self.source, self.result, self.first = source, result, first
        self.recvs, self.helds = bufs[0::2], bufs[1::2]
        self.out_sems = [sems[2 * i : 2 * i + 2] for i in range(count)]
        self.back_sems = [sems[2 * count + 2 * i : 2 * count + 2 * i + 2] for i in range(count)]
        self.here, self.swap_send, self.swap_recv = sems[4 * count :]

    def others(self, level):
        me, size, _ = self.levels[level]
        return [lax.rem(me + d, size) for d in range(1, size)]

    def shard(self, unit, level, i):
        held = self.source(unit) if level == 0 else self.helds[level - 1].at[unit]
        return held.at[pl.ds(pl.multiple_of(i * self.rows[level], 16), self.rows[level])]

    def region(self, unit, level, i):
        start = i * self.rows[level]
        for before in range(level):
            start = start + self.levels[before][0] * self.rows[before]
        return self.result.at[self.first + unit, self.core, pl.ds(pl.multiple_of(start, 16), self.rows[level])]

    def outward(self, unit, level):
        me, _, device = self.levels[level]
        send, recv = self.out_sems[level]
        for d, i in enumerate(self.others(level)):
            yield remote(
                self.shard(unit, level, i), self.recvs[level].at[unit, me], send.at[unit, d], recv.at[unit, me], device(i)
            )

    def back(self, unit, level):
        me, _, device = self.levels[level]
        send, recv = self.back_sems[level]
        last = level == len(self.levels) - 1
        region = self.region(unit, level, me)
        for d, i in enumerate(self.others(level)):
            src = self.helds[level].at[unit] if last else region
            yield remote(src, region, send.at[unit, d], recv.at[unit, me], device(i))

    def keep(self, unit):
        last = len(self.levels) - 1
        return pltpu.make_async_copy(
            self.helds[last].at[unit], self.region(unit, last, self.levels[last][0]), self.here.at[unit]
        )

    def cross(self, unit):
        region = self.result.at[self.first + unit, self.core]
        return remote(region, region, self.swap_send.at[unit], self.swap_recv.at[unit], self.partner)

    def scatter(self, unit):
        self.send(unit, 0)

    def sum(self, unit, level, onward=True):
        others = self.others(level)
        recv = self.recvs[level]
        for i in others:
            arrived(recv.at[unit, i], self.out_sems[level][1].at[unit, i])
        own = self.shard(unit, level, self.levels[level][0])
        pieces = 4 if self.rows[level] % 64 == 0 else 1
        size = self.rows[level] // pieces
        for piece in range(pieces):
            rows = slice(piece * size, (piece + 1) * size)
            total = own[rows, :].astype(F32)
            for i in others:
                total = total + recv[unit, i, rows, :].astype(F32)
            self.helds[level][unit, rows, :] = total.astype(B16)
        if onward and level + 1 < len(self.levels):
            self.send(unit, level + 1)

    def send(self, unit, level):
        for copy in self.outward(unit, level):
            copy.start()

    def share(self, unit):
        self.keep(unit).start()
        for copy in self.back(unit, len(self.levels) - 1):
            copy.start()

    def collect(self, unit, level):
        if level == len(self.levels) - 1:
            self.keep(unit).wait()
        for i in self.others(level):
            arrived(self.region(unit, level, i), self.back_sems[level][1].at[unit, i])

    def gather(self, unit, level, collected=False):
        if not collected:
            self.collect(unit, level + 1)
        for copy in self.back(unit, level):
            copy.start()

    def swap(self, unit):
        self.collect(unit, 0)
        self.cross(unit).start()

    def close(self, unit, out=(), back=()):
        for level in range(len(self.levels)):
            for copy in self.outward(unit, level) if level in out else ():
                copy.wait_send()
            for copy in self.back(unit, level) if level in back else ():
                copy.wait_send()

    def end(self, unit):
        self.cross(unit).wait_send()
        arrived(self.result.at[self.first + unit, 1 - self.core], self.swap_recv.at[unit])


SIZES = {"z": 4, "seq": 4, "all": 16}


def sum_buffers(order, units, rows):
    bufs = []
    for name in order:
        rows //= SIZES[name]
        bufs += [pltpu.VMEM((units, SIZES[name], rows, LANES), B16), pltpu.VMEM((units, rows, LANES), B16)]
    return bufs


def sum_sems(order, units):
    dma = pltpu.SemaphoreType.DMA
    each = [dma((units, count)) for name in order for count in (SIZES[name] - 1, SIZES[name])]
    return each + each + [dma((units,))] * 3


def center_of(values):
    center = values - jnp.mean(values, -1, keepdims=True)
    spread = lax.rsqrt(jnp.mean(center * center, -1, keepdims=True) + epsilon)
    return center * spread, spread


def partner_of(values, lane):
    return jnp.where(lax.rem(lane, HD) < HD // 2, pltpu.roll(values, LANES - HD // 2, 1), pltpu.roll(values, HD // 2, 1))


def own_columns(place, all_ref, w_ref, sems):
    wide = w_ref.shape[1] // 3
    return [
        pltpu.make_async_copy(
            all_ref.at[:, pl.ds(pl.multiple_of((part * place.share + place.u) * wide, LANES), wide)],
            w_ref.at[:, pl.ds(part * wide, wide)],
            sems.at[part],
        )
        for part in range(3)
    ]


def turn_tables(position_row, freq_ref):
    turned = freq_ref[...] * position_row.astype(F32)
    cosine, sine = jnp.cos(turned), jnp.sin(turned)
    return (
        jnp.transpose(jnp.concatenate([cosine] * 4, axis=0)),
        jnp.transpose(jnp.concatenate([-sine, sine, -sine, sine], axis=0)),
    )


def attend_kernel(
    pairs, len_in, tok_ref, wall_ref, pos_in, gain_in, freq_ref,
    o_ref, att_out, normed_out, qp_out, kp_out, vp_out, cos_out, sin_out, nt_out, alllen_ref,
    seq_ref, allpos_ref, w_ref, att_ref, normed_ref, qp_ref, kp_ref, vp_ref, cos_ref, sin_ref, out_ref, pos_ref, len_ref,
    kt_ref, nt_ref, wsem, send, recv, tsend, trecv, fsend, frecv, psend, precv, lsend, lrecv, osem, psem,
):
    place = Place()
    n, share = place.count, place.share
    for copy in own_columns(place, wall_ref, w_ref, wsem):
        copy.start()
    blocks, _, block, _ = out_ref.shape
    for s in (0, 1):
        len_ref[s] = jnp.full(len_ref.shape[1:], len_in[s], jnp.int32)
        for i in range(block // LANES):
            pos_ref[s, i : i + 1, :] = pos_in[s : s + 1, i * LANES : (i + 1) * LANES]
    gain = gain_in[...].reshape(1, gain_in.shape[0])
    greet(place, (0, 1))
    total = blocks * block
    tiles = total // TILE
    copies = Copies(place)
    for s in (0, 1):
        q = 2 * place.core + s
        for u in range(share):
            device = place.worker(q, u)
            copies.post(pos_ref.at[s], allpos_ref.at[place.k], psend.at[s, u], precv.at[place.k], device)
    for step in range(place.batches):
        b = lax.rem(place.b + step, place.batches)
        copies.post(len_ref, alllen_ref.at[place.b], lsend.at[step], lrecv.at[place.b], (b, place.k))
    first = lax.rem(place.k, 2)
    if n == 4:
        far_corner = lax.div(place.k, 2) != place.core
        order = lambda step: (
            place.k
            + jnp.where(step == 1, 1 - 2 * lax.rem(place.k, 2), 0)
            + jnp.where(step == 2, 2 - 4 * lax.div(place.k, 2), 0)
            + jnp.where(step == 3, 3 - 2 * place.k, 0)
        )
    else:
        far_corner = place.k < 0
        order = lambda step: lax.rem(place.k + step, n)

    def token_copies(turn):
        s = first if turn == 0 else 1 - first
        for u in range(share):
            device = place.worker(2 * place.core + s, u)
            src, dst, arrival = tok_ref.at[s, u], seq_ref.at[place.k, u], trecv.at[place.k]
            yield place.is_me(device), remote(src, dst, tsend.at[turn, u], arrival, device), pltpu.make_async_copy(
                src, dst, arrival
            )

    def post_tokens(turn):
        for mine, far_copy, near_copy in token_copies(turn):

            @pl.when(jnp.logical_not(mine))
            def _():
                far_copy.start()

            @pl.when(mine)
            def _():
                near_copy.start()

    def tokens_left(turn):
        for mine, far_copy, _ in token_copies(turn):

            @pl.when(jnp.logical_not(mine))
            def _():
                far_copy.wait_send()

    post_tokens(0)

    @pl.when(jnp.logical_not(far_corner))
    def _():
        post_tokens(1)

    def forward(j, other):
        u = lax.rem(place.u + other, share)
        device = (place.base + lax.rem(u, 2), place.q * place.each + lax.div(u, 2))
        piece = seq_ref.at[j, place.u]
        return remote(piece, piece, fsend.at[j, other - 1], frecv.at[j, other - 1], device)

    def leave(p, j):
        src, dst = out_ref.at[j, p], o_ref.at[lax.rem(place.q, 2), place.u, p]
        arrival = recv.at[lax.rem(place.q, 2), place.u, p]
        device = place.owner(place.q, j)
        return place.is_me(device), remote(src, dst, send.at[p, j], arrival, device), pltpu.make_async_copy(src, dst, arrival)

    for copy in own_columns(place, wall_ref, w_ref, wsem):
        copy.wait()
    for b in range(place.batches):
        arrived(alllen_ref.at[b], lrecv.at[b])
    length = alllen_ref[place.base + lax.div(place.q, 2), lax.rem(place.q, 2), 0:1, :]
    lane = lane_of((TILE, LANES))
    row = lax.broadcasted_iota(jnp.int32, (TILE, LANES), 0)

    def project(x, start):
        rows = pl.ds(start, TILE)
        unit, _ = center_of(x.astype(F32))
        normed = (unit * gain).astype(B16)
        normed_ref[rows, :] = normed
        nt_ref[:, rows] = turned(normed)
        proj = dot(normed, w_ref[...])
        cosine, sine = cos_ref[rows, :], sin_ref[rows, :]
        real = row + start < length
        q_rest = jnp.where(lane == HD, 1.0, 0.0)
        k_rest = jnp.where(lane == HD, jnp.where(real, 0.0, NEGATIVE), jnp.where(lane < HD + 4, 1.0, 0.0))
        v_rest = jnp.where(real, 1.0, 0.0)
        for p in range(pairs):
            for part, (to_ref, rest) in enumerate(((qp_ref, q_rest), (kp_ref, k_rest), (vp_ref, v_rest))):
                at = (part * pairs + p) * LANES
                values = proj[:, at : at + LANES]
                if part < 2:
                    values = values * cosine + partner_of(values, lane) * sine
                if part == 0:
                    values = values * (1.0 / math.sqrt(HD))
                to_ref[2 * p, rows, :] = jnp.where(lane < HD, values, rest).astype(B16)
                to_ref[2 * p + 1, rows, :] = jnp.where(lane < HD, pltpu.roll(values, HD, 1), rest).astype(B16)

    @pl.loop(0, n)
    def _(step):
        j = order(step)

        @pl.when(jnp.logical_and(step == 1, far_corner))
        def _():
            tokens_left(0)
            post_tokens(1)

        arrived(seq_ref.at[j, place.u], trecv.at[j])
        for other in range(1, share):
            forward(j, other).start()
        arrived(allpos_ref.at[j], precv.at[j])
        start = pl.multiple_of(j * block, block)
        for i in range(block // LANES):
            cosine, sine = turn_tables(allpos_ref[j, i : i + 1, :], freq_ref)
            rows = pl.ds(pl.multiple_of(start + i * LANES, LANES), LANES)
            cos_ref[rows, :] = cosine
            sin_ref[rows, :] = sine
        if block // share == TILE:
            for other in range(share):
                u = lax.rem(place.u + share - other, share)
                if other:
                    arrived(seq_ref.at[j, u], frecv.at[j, other - 1])
                project(seq_ref[j, u], pl.multiple_of(start + u * TILE, TILE))
        else:
            for other in range(1, share):
                u = lax.rem(place.u + share - other, share)
                arrived(seq_ref.at[j, u], frecv.at[j, other - 1])
            for i in range(block // TILE):
                whole = seq_ref[j].reshape(block, seq_ref.shape[3])
                project(whole[i * TILE : (i + 1) * TILE], pl.multiple_of(start + i * TILE, TILE))

    ready = [(normed_ref, normed_out), (kp_ref, kp_out), (vp_ref, vp_out), (cos_ref, cos_out), (sin_ref, sin_out), (nt_ref, nt_out)]

    def whole_copies():
        for number, (src, dst) in enumerate(ready):
            yield pltpu.make_async_copy(src, dst, osem.at[number])

    def pair_copies(p):
        yield pltpu.make_async_copy(att_ref.at[p], att_out.at[p], psem.at[p, 0])
        yield pltpu.make_async_copy(qp_ref.at[pl.ds(2 * p, 2)], qp_out.at[pl.ds(2 * p, 2)], psem.at[p, 1])

    for copy in whole_copies():
        copy.start()
    later = jnp.where(lane_of((QUERIES, QUERIES)) <= lax.broadcasted_iota(jnp.int32, (QUERIES, QUERIES), 0), 0.0, NEGATIVE)

    lane = lane_of((QUERIES, LANES))

    @pl.loop(0, pairs)
    def _(p):
        for e in (0, 1):
            for i in range(tiles):
                rows = slice(i * TILE, (i + 1) * TILE)
                kt_ref[e, :, rows] = turned(kp_ref[2 * p + e, rows, :])
        for i in range(total // QUERIES):
            start = i * QUERIES
            found = []
            for e in (0, 1):
                h = 2 * p + e
                q = qp_ref[h, start : start + QUERIES, :]
                near = dot(q, kt_ref[e, :, start : start + QUERIES]) + later
                top = jnp.max(near, -1, keepdims=True)
                if i:
                    far = dot(q, kt_ref[e, :, :start])
                    top = jnp.maximum(top, jnp.max(far, -1, keepdims=True))
                out = dot(jnp.exp(near - top).astype(B16), vp_ref[h, start : start + QUERIES, :])
                if i:
                    out = out + dot(jnp.exp(far - top).astype(B16), vp_ref[h, :start, :])
                found.append(out)
                high, mid, low = three(-(top + jnp.log(out)))
                q_new = jnp.where(lane == HD + 1, high, jnp.where(lane == HD + 2, mid, jnp.where(lane == HD + 3, low, q.astype(F32))))
                qp_ref[h, start : start + QUERIES, :] = q_new.astype(B16)
            even, odd = found
            low_half = lane < HD
            att = jnp.where(low_half, even, pltpu.roll(odd, HD, 1)) / jnp.where(low_half, pltpu.roll(even, HD, 1), odd)
            att_ref[p, start : start + QUERIES, :] = att
            j, within = start // block, start % block
            out_ref[j, p, within : within + QUERIES, :] = att.astype(B16)
            if within + QUERIES == block:
                mine, far_copy, near_copy = leave(p, j)

                @pl.when(jnp.logical_not(mine))
                def _():
                    far_copy.start()

                @pl.when(mine)
                def _():
                    near_copy.start()
        for copy in pair_copies(p):
            copy.start()

    for copy in whole_copies():
        copy.wait()
    copies.drain()

    @pl.when(jnp.logical_not(far_corner))
    def _():
        tokens_left(0)

    tokens_left(1)
    for j in range(n):
        for other in range(1, share):
            forward(j, other).wait_send()
    for p in range(pairs):
        for copy in pair_copies(p):
            copy.wait()
        for s in (0, 1):
            for u in range(place.share):
                arrived(o_ref.at[s, u, p], recv.at[s, u, p])
        for j in range(blocks):
            mine, far_copy, _ = leave(p, j)

            @pl.when(jnp.logical_not(mine))
            def _():
                far_copy.wait_send()


def attend(tokens, positions, lengths, w_all, gain):
    n = lax.axis_size("seq")
    batches = lax.axis_size("batch")
    share = n // 2
    _, block, width = tokens.shape
    total = n * block
    pairs = w_all.shape[1] // (3 * share * LANES)
    dma = pltpu.SemaphoreType.DMA

    def shape(dims, kind=B16):
        return jax.ShapeDtypeStruct(dims, kind)

    heads = (2 * pairs, total, LANES)
    table = (total, LANES)
    frequency = (1.0 / 10000.0 ** (np.arange(HD // 2) * 2.0 / HD)).astype(np.float32)
    return pl.pallas_call(
        functools.partial(attend_kernel, pairs),
        out_shape=(
            shape((2, share, pairs, block, LANES)), shape((pairs, total, LANES), F32), shape((total, width)),
            shape(heads), shape(heads), shape(heads), shape(table, F32), shape(table, F32),
            shape((width, total)), shape((batches, 2, 8, LANES), jnp.int32),
        ),
        in_specs=[SMEM] + [ANY] * 2 + [VMEM] * 3,
        out_specs=(ANY,) * 9 + (VMEM,),
        scratch_shapes=[
            pltpu.VMEM((n, share, block // share, width), B16),
            pltpu.VMEM((n, block // LANES, LANES), jnp.int32),
            pltpu.VMEM((width, 3 * pairs * LANES), B16),
            pltpu.VMEM((pairs, total, LANES), F32),
            pltpu.VMEM((total, width), B16),
            pltpu.VMEM(heads, B16),
            pltpu.VMEM(heads, B16),
            pltpu.VMEM(heads, B16),
            pltpu.VMEM(table, F32),
            pltpu.VMEM(table, F32),
            pltpu.VMEM((n, pairs, block, LANES), B16),
            pltpu.VMEM((2, block // LANES, LANES), jnp.int32),
            pltpu.VMEM((2, 8, LANES), jnp.int32),
            pltpu.VMEM((2, LANES, total), B16),
            pltpu.VMEM((width, total), B16),
            dma((3,)), dma((pairs, n)), dma((2, share, pairs)), dma((2, share)), dma((n,)), dma((n, share - 1)),
            dma((n, share - 1)), dma((2, share)), dma((n,)), dma((batches,)), dma((batches,)), dma((6,)), dma((pairs, 2)),
        ],
        compiler_params=pltpu.CompilerParams(
            vmem_limit_bytes=56 * 2**20, collective_id=1, has_side_effects=True
        ),
        cost_estimate=pl.CostEstimate(flops=30 * 10**9, bytes_accessed=30 * 2**20, transcendentals=13 * 10**6),
        name="attention_forward",
    )(
        lengths, tokens.reshape(2, share, block // share, width), w_all, positions, gain,
        np.broadcast_to(frequency[:, None], (HD // 2, LANES)).copy(),
    )


def lay_gradient(do_ref, att_ref, dop_ref, dot_ref, p):
    block = do_ref.shape[2]
    lane = lane_of((TILE, LANES))
    low_half = lane < HD
    for i in range(dop_ref.shape[1] // TILE):
        start = i * TILE
        grad = do_ref[start // block, p, start % block : start % block + TILE, :].astype(F32)
        product = grad * att_ref[p, start : start + TILE, :]
        for e in (0, 1):
            side = low_half if e == 0 else jnp.logical_not(low_half)
            high, mid, low = three(-jnp.sum(jnp.where(side, product, 0.0), -1, keepdims=True))
            head = grad if e == 0 else pltpu.roll(grad, HD, 1)
            rest = jnp.where(lane == HD, high, jnp.where(lane == HD + 1, mid, jnp.where(lane == HD + 2, low, 0.0)))
            both = jnp.where(low_half, head, rest).astype(B16)
            dop_ref[e, start : start + TILE, :] = both
            dot_ref[e, :, start : start + TILE] = turned(both)


def pair_back(pairs, p, qp_ref, kp_ref, vp_ref, cos_ref, sin_ref, dop_ref, dot_ref, kt_ref, qt_ref, dq_ref, pg_ref, point):
    total = dop_ref.shape[1]
    tiles = total // TILE
    lane = lane_of((TILE, LANES))
    low_half = lane < HD
    earlier = jnp.where(lane_of((TILE, TILE)) >= lax.broadcasted_iota(jnp.int32, (TILE, TILE), 0), 0.0, NEGATIVE)

    def packed(even, odd):
        return jnp.where(low_half, even, pltpu.roll(odd, HD, 1))

    def unrotated(values, rows):
        return values * cos_ref[rows, :] - partner_of(values, lane) * sin_ref[rows, :]

    for i in range(tiles):
        rows = slice(i * TILE, (i + 1) * TILE)
        for e in (0, 1):
            kt_ref[e, :, rows] = turned(kp_ref[2 * p + e, rows, :])[:HD]
            qt_ref[e, :, rows] = turned(qp_ref[2 * p + e, rows, :])
    for j in range(tiles):
        start = j * TILE
        near_rows = slice(start, start + TILE)
        dks, dvs = [], []
        for e in (0, 1):
            h = 2 * p + e
            kj, vj = kp_ref[h, near_rows, :], vp_ref[h, near_rows, :]
            dk = dv = None
            for part in (0, 1):
                rows = near_rows if part == 0 else slice(start + TILE, total)
                if rows.start == total:
                    continue
                qs, dos = qp_ref[h, rows, :], dop_ref[e, rows, :]
                scores = dot(kj, qt_ref[e, :, rows])
                if part == 0:
                    scores = scores + earlier
                probs = jnp.exp(scores)
                dv_part = dot(probs.astype(B16), dos)
                grads = (probs * dot(vj, dot_ref[e, :, rows])).astype(B16)
                dk_part = dot(grads, qs)
                dq_part = dot(kt_ref[e, :, near_rows], grads)
                if j == 0:
                    dq_ref[e, :, rows] = dq_part
                else:
                    dq_ref[e, :, rows] += dq_part
                dk = dk_part if dk is None else dk + dk_part
                dv = dv_part if dv is None else dv + dv_part
            dks.append(dk)
            dvs.append(dv)
        pg_ref[pairs + p, near_rows, :] = unrotated(packed(*dks), near_rows).astype(B16)
        pg_ref[2 * pairs + p, near_rows, :] = packed(*dvs).astype(B16)
        point(j)
    for i in range(tiles):
        rows = slice(i * TILE, (i + 1) * TILE)
        both = jnp.concatenate([dq_ref[0, :, rows], dq_ref[1, :, rows]], axis=0)
        dq = jnp.transpose(both) * (1.0 / math.sqrt(HD))
        pg_ref[p, rows, :] = unrotated(dq, rows).astype(B16)


def plain_back_kernel(
    pairs, qp_ref, kp_ref, vp_ref, do_ref, att_ref, cos_ref, sin_ref, normed_ref, wall_ref, wgrad_ref, gn_ref, gaing_ref,
    dop_ref, dot_ref, kt_ref, qt_ref, dq_ref, pg_ref, w_ref, wsem,
):
    place = Place()
    for copy in own_columns(place, wall_ref, w_ref, wsem):
        copy.start()

    @pl.loop(0, pairs)
    def _(p):
        lay_gradient(do_ref, att_ref, dop_ref, dot_ref, p)
        pair_back(pairs, p, qp_ref, kp_ref, vp_ref, cos_ref, sin_ref, dop_ref, dot_ref, kt_ref, qt_ref, dq_ref, pg_ref, lambda j: None)

    for copy in own_columns(place, wall_ref, w_ref, wsem):
        copy.wait()
    gaing_ref[...] = jnp.zeros_like(gaing_ref)

    @pl.loop(0, normed_ref.shape[0] // TILE)
    def _(t):
        rows = pl.ds(pl.multiple_of(t * TILE, TILE), TILE)
        grads = jnp.concatenate([pg_ref[g, rows, :] for g in range(3 * pairs)], axis=1)
        grad = dot_nt(grads, w_ref[...])
        gaing_ref[...] += folded(grad * normed_ref[rows, :].astype(F32))
        gn_ref[rows, :] = grad.astype(B16)

    for part in range(3):
        grads = jnp.concatenate([pg_ref[part * pairs + p] for p in range(pairs)], axis=1)
        wgrad_ref[:, part * pairs * LANES : (part + 1) * pairs * LANES] = dot_tn(normed_ref[...], grads).astype(B16)


def plain_back(qp, kp, vp, grad, att, cosine, sine, normed, w_all):
    total, width = normed.shape
    pairs = att.shape[0]
    w = jax.ShapeDtypeStruct((width, 3 * pairs * LANES), B16)
    return pl.pallas_call(
        functools.partial(plain_back_kernel, pairs),
        out_shape=(w, jax.ShapeDtypeStruct((total, width), B16), jax.ShapeDtypeStruct((8, width), F32)),
        in_specs=[VMEM] * 8 + [ANY],
        out_specs=(VMEM,) * 3,
        scratch_shapes=[
            pltpu.VMEM((2, total, LANES), B16),
            pltpu.VMEM((2, LANES, total), B16),
            pltpu.VMEM((2, HD, total), B16),
            pltpu.VMEM((2, LANES, total), B16),
            pltpu.VMEM((2, HD, total), F32),
            pltpu.VMEM((3 * pairs, total, LANES), B16),
            pltpu.VMEM(w.shape, B16),
            pltpu.SemaphoreType.DMA((3,)),
        ],
        compiler_params=pltpu.CompilerParams(vmem_limit_bytes=56 * 2**20),
        cost_estimate=pl.CostEstimate(flops=60 * 10**9, bytes_accessed=30 * 2**20, transcendentals=13 * 10**6),
        name="attention_backward",
    )(qp, kp, vp, grad, att, cosine, sine, normed, w_all)


UNITS = 3
FAMILIES = {"e": ("seq", "z"), "o": ("seq", "z"), "q0": ("z", "seq"), "q1": ("all",), "q2": ("all",)}
EARLY = {
    (0, -1): [("send1", "e1"), ("scatter", "e2")],
    (0, 2): [("sum1", "e1"), ("scatter", "o0"), ("share", "e1")],
    (0, 4): [("sum0", "e2"), ("gather0", "e0")],
    (0, 6): [("sum0", "o0")],
    (1, 1): [("gather0", "e1"), ("sum1", "e2"), ("sum1", "o0"), ("share", "e2"), ("share", "o0"), ("swap", "e0")],
    (1, 4): [("sum0", "q0")],
    (2, 0): [("swap", "e1"), ("gather0", "e2"), ("sum1", "q0"), ("share", "q0")],
    (2, 2): [("sum0", "q1"), ("share", "q1")],
}
LATE = (
    ("gather0", "o0"),
    ("gather0", "q0"),
    ("sum0", "q2"),
    ("share", "q2"),
    ("swap", "q1"),
    ("swap", "e2"),
    ("swap", "q0"),
    ("swap", "o0"),
    ("swap", "q2"),
)
SMALL = (0, 3, 6)
FINISH = 5


def summing_back_kernel(
    pairs, qp_in, kp_in, vp_in, do_in, att_in, cos_in, sin_in, normed_in, nt_in, small_ref, half_sum_ref, mine_ref,
    outmine_ref, gain_ref, wall_ref, x_ref, gmid_ref, _, sums_ref, osums_ref, qsums_ref, total_ref, input_ref,
    dop_ref, dot_ref, kt_ref, qt_ref, dq_ref, pg_ref, w_ref, wg_ref, gn_ref, gnrecv_ref, sbuf_ref, srecv0_ref, srecv1_ref, srecv2_ref,
    slots_ref, xin_ref, gmidin_ref, qp_ref, kp_ref, vp_ref, do_ref, att_ref, cos_ref, sin_ref, normed_ref, nt_ref,
    pairsem, wholesem, wsem, insem, gsend, grecv, osend, orecv, ssend, srecv, *rest,
):
    def take(count):
        nonlocal rest
        taken, rest = rest[:count], rest[count:]
        return taken

    e_bufs, o_bufs = take(2 * len(FAMILIES["e"])), take(2 * len(FAMILIES["o"]))
    q_bufs = [take(2 * len(FAMILIES["q%d" % p])) for p in range(pairs)]
    sems = {}
    for name in ("e0", "e1", "e2", "o") + tuple("q%d" % p for p in range(pairs)):
        sems[name] = take(4 * len(FAMILIES["e" if name[0] == "e" else name]) + 3)
    e1_bufs = take(2)
    place = Place()
    core = place.core
    width = normed_ref.shape[1]
    slabs = width // LANES
    rows_q = wg_ref.shape[0] // pairs

    def pair_loads(p):
        both = pl.ds(2 * p, 2)
        moved = [(src.at[both], dst.at[both]) for src, dst in ((qp_in, qp_ref), (kp_in, kp_ref), (vp_in, vp_ref))]
        moved += [(do_in.at[:, p], do_ref.at[:, p]), (att_in.at[p], att_ref.at[p])]
        return [pltpu.make_async_copy(src, dst, pairsem.at[p, i]) for i, (src, dst) in enumerate(moved)]

    def whole_loads():
        moved = ((cos_in, cos_ref), (sin_in, sin_ref), (nt_in, nt_ref), (normed_in, normed_ref))
        return [pltpu.make_async_copy(src, dst, wholesem.at[i]) for i, (src, dst) in enumerate(moved)]

    for copy in pair_loads(0) + whole_loads() + [copy for p in range(1, pairs) for copy in pair_loads(p)]:
        copy.start()
    for copy in own_columns(place, wall_ref, w_ref, wsem):
        copy.start()
    greet(place, (core,))
    inputs = [
        pltpu.make_async_copy(x_ref, xin_ref, insem.at[0]), pltpu.make_async_copy(gmid_ref, gmidin_ref, insem.at[1])
    ]
    for copy in inputs:
        copy.start()
    units = {}
    for number, held in ((0, None), (1, half_sum_ref)):
        bufs = (None, held, *e1_bufs)
        units["e%d" % number] = (
            Sum(place, FAMILIES["e"], mine_ref.shape[0], None, bufs, sums_ref, number, sems["e%d" % number]), 0
        )
    last = Sum(place, FAMILIES["e"], mine_ref.shape[0], lambda unit: mine_ref, e_bufs, sums_ref, UNITS - 1, sems["e2"])
    units["e2"] = (last, 0)
    units["o0"] = (
        Sum(place, FAMILIES["o"], outmine_ref.shape[0], lambda unit: outmine_ref, o_bufs, osums_ref, 0, sems["o"]), 0
    )
    for p in range(pairs):
        name = "q%d" % p
        own = wg_ref.at[pl.ds(p * rows_q, rows_q)]
        units[name] = (
            Sum(place, FAMILIES[name], rows_q, lambda unit, own=own: own, q_bufs[p], qsums_ref, p, sems[name]), 0
        )
    partner = last.partner

    def stage(name, key):
        family, unit = units[key]
        if name[:3] == "sum":
            family.sum(unit, int(name[3:]))
        elif name[:4] == "send":
            family.send(unit, int(name[4:]))
        elif name[:6] == "gather":
            family.gather(unit, int(name[6:]), collected=key == "e0")
        else:
            getattr(family, name)(unit)

    def point(p, j):
        for (at_p, at_j), todo in EARLY.items():
            if at_j == j:

                @pl.when(p == at_p)
                def _(todo=todo):
                    for name, key in todo:
                        stage(name, key)

    @pl.loop(0, pairs)
    def _(p):
        point(p, -1)
        for copy in pair_loads(p):
            copy.wait()
        lay_gradient(do_ref, att_ref, dop_ref, dot_ref, p)

        @pl.when(p == 0)
        def _():
            for copy in whole_loads():
                copy.wait()

        pair_back(
            pairs, p, qp_ref, kp_ref, vp_ref, cos_ref, sin_ref, dop_ref, dot_ref, kt_ref, qt_ref, dq_ref, pg_ref, functools.partial(point, p)
        )
        grads = jnp.concatenate([pg_ref[part * pairs + p] for part in range(3)], axis=1)
        found = dot(nt_ref[...], grads).astype(B16)
        for part in range(3):
            rows = pl.ds(pl.multiple_of(p * rows_q + part * width, 16), width)
            wg_ref[rows, :] = found[:, part * LANES : (part + 1) * LANES]
        for at_p in range(pairs):

            @pl.when(p == at_p)
            def _(at_p=at_p):
                stage("scatter", "q%d" % at_p)

    for copy in own_columns(place, wall_ref, w_ref, wsem):
        copy.wait()

    def aside(j):
        return remote(gn_ref.at[j], gnrecv_ref.at[j], gsend.at[j], grecv.at[j], partner)

    def leave(j):
        src, dst, arrival = gn_ref.at[4 + j], slots_ref.at[lax.rem(place.q, 2), core], orecv.at[lax.rem(place.q, 2), core]
        device = place.owner(place.q, j)
        return place.is_me(device), remote(src, dst, osend.at[j], arrival, device), pltpu.make_async_copy(src, dst, arrival)

    def normed_grad(i):
        rows = pl.ds(pl.multiple_of(i * TILE, TILE), TILE)
        grads = jnp.concatenate([pg_ref[g, rows, :] for g in range(3 * pairs)], axis=1)
        grad = dot_nt(grads, w_ref[...])
        return grad, folded(grad * normed_ref[rows, :].astype(F32))

    gain_grad = jnp.zeros((8, width), F32)
    for j in range(4):
        grad, part = normed_grad(2 * j + 1 - core)
        gain_grad = gain_grad + part
        for i in range(slabs):
            gn_ref[j, i * TILE : (i + 1) * TILE, :] = grad[:, i * LANES : (i + 1) * LANES].astype(B16)
        aside(j).start()
    for j in range(4):
        grad, part = normed_grad(2 * j + core)
        gain_grad = gain_grad + part
        arrived(gnrecv_ref.at[j], grecv.at[j])
        for i in range(slabs):
            rows = slice(i * TILE, (i + 1) * TILE)
            gn_ref[4 + j, rows, :] = (
                grad[:, i * LANES : (i + 1) * LANES] + gnrecv_ref[j, rows, :].astype(F32)
            ).astype(B16)
        mine, far, near = leave(j)

        @pl.when(jnp.logical_not(mine))
        def _():
            far.start()

        @pl.when(mine)
        def _():
            near.start()

    bottom = lax.broadcasted_iota(jnp.int32, sbuf_ref.shape[1:], 0) == sbuf_ref.shape[1] - 1
    sbuf_ref[0] = jnp.where(bottom, jnp.sum(gain_grad, axis=0, keepdims=True), small_ref[...])
    (seq_me, _, seq_device), (z_me, _, z_device) = last.levels
    levels = [(seq_me, seq_device, srecv1_ref, 1), (z_me, z_device, srecv2_ref, 4)]

    def swap():
        return remote(sbuf_ref.at[0], srecv0_ref, ssend.at[0], srecv.at[0, 0], partner)

    def spread(level):
        me, device, into, at = levels[level]
        for d in (1, 2, 3):
            yield remote(
                sbuf_ref.at[level + 1], into.at[me], ssend.at[at + d - 1], srecv.at[level + 1, me],
                device(lax.rem(me + d, 4)),
            )

    def small_stage(level):
        if level == 0:
            arrived(srecv0_ref, srecv.at[0, 0])
            value = sbuf_ref[0] + srecv0_ref[...]
        else:
            me, device, into, at = levels[level - 1]
            into[me] = sbuf_ref[level]
            for d in (1, 2, 3):
                i = lax.rem(me + d, 4)
                arrived(into.at[i], srecv.at[level, i])
            value = into[0] + into[1] + into[2] + into[3]
        if level == 2:
            total_ref[...] = value
        else:
            sbuf_ref[level + 1] = value
            for copy in spread(level):
                copy.start()

    def finish_inputs():
        for copy in inputs:
            copy.wait()
        for s in range(2):
            for h in range(2):
                arrived(slots_ref.at[s, h], orecv.at[s, h])
                rows = slice(h * TILE, (h + 1) * TILE)
                unit, spread = center_of(xin_ref[s, rows, :].astype(F32))
                grad = [slots_ref[s, h, i * TILE : (i + 1) * TILE, :] for i in range(slabs)]
                unit_grad = jnp.concatenate(grad, axis=1).astype(F32) * gain_ref[...].reshape(1, width)
                back = spread * (
                    unit_grad
                    - jnp.mean(unit_grad, -1, keepdims=True)
                    - unit * jnp.mean(unit_grad * unit, -1, keepdims=True)
                )
                input_ref[s, rows, :] = (gmidin_ref[s, rows, :] + back).astype(B16)

    swap().start()
    for number, (name, key) in enumerate(LATE):
        stage(name, key)
        if number in SMALL:
            small_stage(SMALL.index(number))
        if number == FINISH:
            finish_inputs()
    for j in range(4):
        mine, far, _ = leave(j)

        @pl.when(jnp.logical_not(mine))
        def _():
            far.wait_send()

        aside(j).wait_send()
    swap().wait_send()
    for level in (0, 1):
        for copy in spread(level):
            copy.wait_send()
    for key, (family, unit) in units.items():
        levels = range(len(family.levels))
        family.close(unit, out={"e0": (), "e1": (1,)}.get(key, levels), back=(0,) if key == "e0" else levels)
        family.end(unit)


def summing_back(qp, kp, vp, grad, att, cosine, sine, normed, normed_t, small, half_sum, mine, outmine, gain, w_all, x, gmid, sums):
    total, width = normed.shape
    pairs = att.shape[0]
    slabs = width // LANES
    rows_e, rows_o, rows_q = mine.shape[0], outmine.shape[0], 3 * width
    dma = pltpu.SemaphoreType.DMA

    def shape(dims, kind=B16):
        return jax.ShapeDtypeStruct(dims, kind)

    return pl.pallas_call(
        functools.partial(summing_back_kernel, pairs),
        out_shape=(
            shape((UNITS, 2, rows_e, LANES)), shape((1, 2, rows_o, LANES)), shape((pairs, 2, rows_q, LANES)),
            shape(small.shape, F32), shape(x.shape),
        ),
        in_specs=[ANY] * 9 + [VMEM] * 5 + [ANY] * 4,
        out_specs=(ANY,) * 3 + (VMEM,) * 2,
        input_output_aliases={17: 0},
        scratch_shapes=[
            pltpu.VMEM((2, total, LANES), B16),
            pltpu.VMEM((2, LANES, total), B16),
            pltpu.VMEM((2, HD, total), B16),
            pltpu.VMEM((2, LANES, total), B16),
            pltpu.VMEM((2, HD, total), F32),
            pltpu.VMEM((3 * pairs, total, LANES), B16),
            pltpu.VMEM((width, 3 * pairs * LANES), B16),
            pltpu.VMEM((pairs * rows_q, LANES), B16),
            pltpu.VMEM((8, slabs * TILE, LANES), B16),
            pltpu.VMEM((4, slabs * TILE, LANES), B16),
            pltpu.VMEM((3,) + small.shape, F32),
            pltpu.VMEM(small.shape, F32),
            pltpu.VMEM((4,) + small.shape, F32),
            pltpu.VMEM((4,) + small.shape, F32),
            pltpu.VMEM((2, 2, slabs * TILE, LANES), B16),
            pltpu.VMEM(x.shape, B16),
            pltpu.VMEM(gmid.shape, F32),
            *(pltpu.VMEM(value.shape, value.dtype) for value in (qp, kp, vp, grad, att, cosine, sine, normed, normed_t)),
            dma((pairs, 5)), dma((4,)), dma((3,)), dma((2,)), dma((4,)), dma((4,)), dma((4,)), dma((2, 2)), dma((7,)), dma((3, 4)),
            *sum_buffers(FAMILIES["e"], 1, rows_e), *sum_buffers(FAMILIES["o"], 1, rows_o),
            *(buf for p in range(pairs) for buf in sum_buffers(FAMILIES["q%d" % p], 1, rows_q)),
            *(sem for _ in range(UNITS) for sem in sum_sems(FAMILIES["e"], 1)), *sum_sems(FAMILIES["o"], 1),
            *(sem for p in range(pairs) for sem in sum_sems(FAMILIES["q%d" % p], 1)),
            *sum_buffers(FAMILIES["e"][1:], 1, rows_e // 4),
        ],
        compiler_params=pltpu.CompilerParams(
            vmem_limit_bytes=62 * 2**20, collective_id=3, has_side_effects=True
        ),
        cost_estimate=pl.CostEstimate(flops=60 * 10**9, bytes_accessed=60 * 2**20, transcendentals=13 * 10**6),
        name="attention_backward_and_sums",
    )(qp, kp, vp, grad, att, cosine, sine, normed, normed_t, small, half_sum, mine, outmine, gain, w_all, x, gmid, sums)


def widen_kernel(downt_ref, upt_ref, outs_ref, q_ref, down_ref, up_ref, out_ref, qkv_ref):
    width = out_ref.shape[1]
    for i in range(2):
        down_ref[i * LANES : (i + 1) * LANES, :] = jnp.transpose(downt_ref[i * width : (i + 1) * width, :].astype(F32))
    at = 0
    for unit in range(upt_ref.shape[0]):
        for i in range(upt_ref.shape[2]):
            up_ref[:, at : at + LANES] = upt_ref[unit, 0, i].astype(F32)
            at += LANES
    for i in range(outs_ref.shape[0]):
        out_ref[:, i * LANES : (i + 1) * LANES] = outs_ref[i].astype(F32)
    at = 0
    for part in range(3):
        for u in range(q_ref.shape[1]):
            for p in range(q_ref.shape[0]):
                qkv_ref[:, at : at + LANES] = q_ref[p, u, part].astype(F32)
                at += LANES


def widen(sums, osums, qsums, width, inner):
    steps = inner // (2 * LANES)
    pairs, share = qsums.shape[:2]
    slabs = width // LANES
    some = width // steps
    turn = steps // UNITS

    def shape(dims):
        return jax.ShapeDtypeStruct(dims, F32)

    def by_row(columns):
        return pl.BlockSpec((some, columns), lambda c: (c, 0))

    return pl.pallas_call(
        widen_kernel,
        grid=(steps,),
        out_shape=(shape((inner, width)), shape((width, inner)), shape((width, width)), shape((width, 3 * width))),
        in_specs=[
            pl.BlockSpec((2 * width, LANES), lambda c: (lax.div(c, turn) * 2 * turn + lax.rem(c, turn), 0)),
            pl.BlockSpec((UNITS, 1, 2 * turn, some, LANES), lambda c: (0, 1, 0, c, 0)),
            pl.BlockSpec((slabs, some, LANES), lambda c: (0, c, 0)),
            pl.BlockSpec((pairs, share, 3, some, LANES), lambda c: (0, 0, 0, c, 0)),
        ],
        out_specs=(
            pl.BlockSpec((2 * LANES, width), lambda c: (c, 0)), by_row(inner), by_row(width), by_row(3 * width)
        ),
        compiler_params=pltpu.CompilerParams(vmem_limit_bytes=62 * 2**20),
        name="widen_sums",
    )(
        sums.reshape(-1, LANES), sums.reshape(UNITS, 2, 2 * turn, width, LANES), osums.reshape(slabs, width, LANES),
        qsums.reshape(pairs, share, 3, width, LANES),
    )


def slabs_of(ref, s, rows):
    return jnp.concatenate([ref[s, u, p, rows, :] for u in range(ref.shape[1]) for p in range(ref.shape[2])], axis=1)


def folded(values):
    return jnp.sum(values.reshape(values.shape[0] // 8, 8, values.shape[1]), axis=0)


LAST = 2
ORDER = ("seq", "z")


def swap_half(width):
    return PIECE * width // LANES


def loss_factor(alllen_ref, slots):
    count = None
    for b in range(alllen_ref.shape[0]):
        for s in (0, 1):
            part = alllen_ref[b, s, 0:1, :]
            count = part if count is None else count + part
    return slots / count.astype(F32)


def middle_kernel(
    kept, steps, hist_steps, summing, scale_ref, len_ref, alllen_ref, o_ref, x_ref, cot_ref, wout_ref, gain_ref, up_ref,
    down_ref, hist_ref, mixed_ref, gmid_ref, do_ref, small_ref, *rest,
):
    if summing:
        sums_ref, half_sum_ref, mine_ref, outmine_ref = rest[:4]
        rest = rest[4:]
    else:
        grads_ref, outg_ref = rest[:2]
        rest = rest[2:]
    (
        middle_ref, ntwo_ref, gmlp_ref, ntwot_ref, gmlpt_ref, blk_ref, gntwo_ref, og_ref, act_ref, pre_ref, gaing_ref,
        mixg_ref, gatt_ref, send, recv,
    ) = rest[:15]
    place = Place()
    core = place.core
    step = pl.program_id(0)
    rows_all, width = x_ref.shape
    block = o_ref.shape[3]
    slab = hist_ref.shape[1]
    slabs = width // LANES
    own = scale_ref[kept]
    factor = loss_factor(alllen_ref, place.batches * 2 * place.count * block)
    gain = gain_ref[...].reshape(1, width)

    def grad_top(start, count):
        s = lax.div(start, block)
        index = lax.broadcasted_iota(jnp.int32, (count, LANES), 0) + lax.rem(start, block) + place.k * block
        scale = jnp.where(index < len_ref[s], factor, 0.0)[:, :1]
        return cot_ref[pl.ds(pl.multiple_of(start, count), count), :].astype(F32) * scale

    def leave(t, u):
        s, part = t * TILE // block, t * TILE % block // TILE
        within = pl.ds(part * TILE, TILE)
        src, dst, arrival = gatt_ref.at[s, u, :, within, :], do_ref.at[place.k, :, within, :], recv.at[place.k, part]
        device = place.worker(2 * place.core + s, u)
        return place.is_me(device), remote(src, dst, send.at[t, u], arrival, device), pltpu.make_async_copy(src, dst, arrival)

    @pl.when(step == 0)
    def _():
        greet(place, (core,) if summing else ())

    if summing:
        early_ref, landing_ref, lout_ref, aside_ref, aout_ref = rest[15:20]
        xsend, xrecv = rest[20:22]
        half = swap_half(width)
        partner = (place.base + 1 - core, place.k)

        def chunk_of(unit):
            return early_ref.at[pl.ds(unit * 2 * half, 2 * half)]

        sums = Sum(place, ORDER, 2 * half, chunk_of, rest[22:26], sums_ref, 0, rest[26:])

        def cross(c):
            return remote(aside_ref.at[c % 2], landing_ref.at[c % 4], xsend.at[c], xrecv.at[c], partner)

        def cross_out():
            return remote(aout_ref, lout_ref, xsend.at[steps], xrecv.at[steps], partner)

        def hold(c, down, up):
            if c >= 2:
                cross(c - 2).wait_send()
            into = early_ref.at[pl.ds(c * half, half)] if c < 2 * LAST else mine_ref.at[pl.ds((c - 2 * LAST) * half, half)]
            for i in range(PIECE // LANES):
                rows, lanes = slice(i * width, (i + 1) * width), slice(i * LANES, (i + 1) * LANES)
                first = jnp.where(core == 0, down[:, lanes], up[:, lanes])
                other = jnp.where(core == 0, up[:, lanes], down[:, lanes])
                into[rows, :] = first.astype(B16)
                aside_ref[c % 2, rows, :] = other.astype(B16)
            cross(c).start()

        def add(c):
            arrived(landing_ref.at[c % 4], xrecv.at[c])
            into = early_ref.at[pl.ds(c * half, half)] if c < 2 * LAST else mine_ref.at[pl.ds((c - 2 * LAST) * half, half)]
            for i in range(PIECE // LANES):
                rows = slice(i * width, (i + 1) * width)
                into[rows, :] = (into[rows, :].astype(F32) + landing_ref[c % 4, rows, :].astype(F32)).astype(B16)

        def between(c):
            if c >= 1:
                add(c - 1)
            if c == 2:
                sums.scatter(0)
            if c == 4:
                sums.scatter(1)
            if c == 5:
                sums.sum(0, 0)

    @pl.when(step == 0)
    def _():
        for t in range(rows_all // TILE):
            rows = slice(t * TILE, (t + 1) * TILE)
            within = t * TILE % block
            att = slabs_of(o_ref, t * TILE // block, slice(within, within + TILE))
            middle = x_ref[rows, :].astype(F32) + dot(att, wout_ref[...])
            middle_ref[rows, :] = middle
            unit, _ = center_of(middle)
            ntwo = unit * gain
            gmlp = own * grad_top(t * TILE, TILE)
            ntwo_ref[rows, :] = ntwo.astype(B16)
            gmlp_ref[rows, :] = gmlp.astype(B16)
            ntwot_ref[:, rows] = jnp.transpose(ntwo).astype(B16)
            gmlpt_ref[:, rows] = jnp.transpose(gmlp).astype(B16)
            blk_ref[rows, :] = middle
            gntwo_ref[rows, :] = jnp.zeros((TILE, width), F32)
        mixg_ref[...] = jnp.zeros_like(mixg_ref)
        gaing_ref[...] = jnp.zeros_like(gaing_ref)
        og_ref[...] = jnp.zeros_like(og_ref)

    @pl.when(step < steps)
    def _():
        up, down = up_ref[...], down_ref[...]
        up_t, down_t = turned(up), turned(down)
        slope = math.sqrt(2.0 / math.pi)
        for t in range(rows_all // ROWS):
            rows = slice(t * ROWS, (t + 1) * ROWS)
            pre = dot(ntwo_ref[rows, :], up)
            square = pre * pre
            bent = jnp.tanh(slope * pre * (1.0 + 0.044715 * square))
            half_ = 0.5 + 0.5 * bent
            act = (pre * half_).astype(B16)
            slopes = half_ + 0.5 * slope * pre * (1.0 - bent * bent) * (1.0 + 3 * 0.044715 * square)
            pre_grad = (dot(gmlp_ref[rows, :], down_t) * slopes).astype(B16)
            act_ref[rows, :] = act
            pre_ref[rows, :] = pre_grad
            blk_ref[rows, :] += dot(act, down)
            gntwo_ref[rows, :] += dot(pre_grad, up_t)
        if summing:
            for c in range(steps):

                @pl.when(step == c)
                def _(c=c):
                    between(c)

    @pl.when(step == steps - 1)
    def _():
        for t in range(rows_all // TILE):
            rows = slice(t * TILE, (t + 1) * TILE)
            s, within = t * TILE // block, t * TILE % block
            top = grad_top(t * TILE, TILE)
            unit, spread = center_of(middle_ref[rows, :])
            gain_grad = gntwo_ref[rows, :]
            gaing_ref[...] += folded(gain_grad * unit)
            unit_grad = gain_grad * gain
            back = spread * (
                unit_grad
                - jnp.mean(unit_grad, -1, keepdims=True)
                - unit * jnp.mean(unit_grad * unit, -1, keepdims=True)
            )
            total = own * top + back
            gmid_ref[rows, :] = total
            att_grad = dot_nt(total.astype(B16), wout_ref[...]).astype(B16)
            at = 0
            for u in range(o_ref.shape[1]):
                for p in range(o_ref.shape[2]):
                    gatt_ref[s, u, p, within : within + TILE, :] = att_grad[:, at : at + LANES]
                    at += LANES
                mine, far, near = leave(t, u)

                @pl.when(jnp.logical_not(mine))
                def _():
                    far.start()

                @pl.when(mine)
                def _():
                    near.start()
    @pl.when(step < steps)
    def _():
        downg = dot(gmlpt_ref[...], act_ref[...])
        upg = dot(ntwot_ref[...], pre_ref[...])
        if summing:
            for c in range(steps):

                @pl.when(step == c)
                def _(c=c):
                    hold(c, downg, upg)
        else:
            for i in range(PIECE // LANES):
                lanes = slice(i * LANES, (i + 1) * LANES)
                grads_ref[0, i * width : (i + 1) * width, :] = downg[:, lanes].astype(B16)
                at = PIECE * slabs + i * width
                grads_ref[0, at : at + width, :] = upg[:, lanes].astype(B16)

    @pl.when(step == steps - 1)
    def _():
        for t in range(rows_all // TILE):
            rows = slice(t * TILE, (t + 1) * TILE)
            s, within = t * TILE // block, t * TILE % block
            og_ref[...] += dot_tn(slabs_of(o_ref, s, slice(within, within + TILE)), gmid_ref[rows, :].astype(B16))
        if summing:
            for i in range(slabs // 2):
                rows = slice(i * width, (i + 1) * width)
                left, right = og_ref[:, i * LANES : (i + 1) * LANES], og_ref[:, (i + slabs // 2) * LANES : (i + slabs // 2 + 1) * LANES]
                outmine_ref[rows, :] = jnp.where(core == 0, left, right).astype(B16)
                aout_ref[rows, :] = jnp.where(core == 0, right, left).astype(B16)
            cross_out().start()
        else:
            outg_ref[...] = og_ref[...].astype(B16)

    @pl.when(step >= steps)
    def _():
        start = pl.multiple_of((step - steps) * slab, slab)
        top = grad_top(start, slab)
        out = blk_ref[pl.ds(start, slab), :]
        mixed = own * out
        mixg_ref[kept] += folded(out * top)
        for j in range(kept):
            stored = hist_ref[j].astype(F32)
            mixed = mixed + scale_ref[j] * stored
            mixg_ref[j] += folded(stored * top)
        mixed_ref[...] = mixed.astype(B16)

    if summing:

        @pl.when(step == steps)
        def _():
            sums.sum(0, 1)
            sums.share(0)

        @pl.when(step == steps + 2)
        def _():
            add(5)

        @pl.when(step == steps + 4)
        def _():
            sums.sum(1, 0, onward=False)
            half_sum_ref[...] = rest[23][1]

        @pl.when(step == steps + hist_steps - 1)
        def _():
            arrived(lout_ref, xrecv.at[steps])
            for i in range(slabs // 2):
                rows = slice(i * width, (i + 1) * width)
                outmine_ref[rows, :] = (outmine_ref[rows, :].astype(F32) + lout_ref[rows, :].astype(F32)).astype(B16)
            sums.collect(0, 1)
            sums.close(0, out=(0, 1), back=(1,))
            sums.close(1, out=(0,))
            for c in (steps - 2, steps - 1):
                cross(c).wait_send()
            cross_out().wait_send()

    @pl.when(step == steps + hist_steps - 1)
    def _():
        small_ref[0:1, :] = jnp.sum(gaing_ref[...], axis=0, keepdims=True)
        for j in range(kept + 1):
            small_ref[j + 1 : j + 2, :] = jnp.sum(mixg_ref[j], axis=0, keepdims=True)
        small_ref[kept + 2 :, :] = jnp.zeros((small_ref.shape[0] - kept - 2, width), F32)
        for part in range(block // TILE):
            for j in range(place.count):
                arrived(do_ref.at[j, :, pl.ds(part * TILE, TILE), :], recv.at[j, part])
        for t in range(rows_all // TILE):
            for u in range(place.share):
                mine, far, _ = leave(t, u)

                @pl.when(jnp.logical_not(mine))
                def _():
                    far.wait_send()


def middle_part(scale, lengths, all_lengths, o, x, cot, wout, gain, up, down, hist, summing):
    rows, width = x.shape
    kept = hist.shape[0]
    inner = up.shape[1]
    steps = inner // PIECE
    hist_steps = 8
    slab = rows // hist_steps
    _, share, pairs, block, _ = o.shape
    blocks = 2 * share
    dma = pltpu.SemaphoreType.DMA
    slabs = width // LANES
    half = swap_half(width)

    def fixed(values):
        zeros = (0,) * len(values.shape)
        return pl.BlockSpec(values.shape, lambda c: zeros, pipeline_mode=pl.Buffered(1))

    def shape(dims, kind):
        return jax.ShapeDtypeStruct(dims, kind)

    hist_spec = pl.BlockSpec((kept, slab, width), lambda c: (0, jnp.maximum(c - steps, 0), 0))
    mixed_spec = pl.BlockSpec((slab, width), lambda c: (jnp.maximum(c - steps, 0), 0))
    up_spec = pl.BlockSpec((width, PIECE), lambda c: (0, jnp.minimum(c, steps - 1)))
    down_spec = pl.BlockSpec((PIECE, width), lambda c: (jnp.minimum(c, steps - 1), 0))
    gmid = shape((rows, width), F32)
    small = shape((16, width), F32)
    outs = [shape((rows, width), B16), gmid, shape((blocks, pairs, block, LANES), B16), small]
    out_specs = [mixed_spec, fixed(gmid), ANY, fixed(small)]
    scratch = [
        pltpu.VMEM((rows, width), F32),
        pltpu.VMEM((rows, width), B16),
        pltpu.VMEM((rows, width), B16),
        pltpu.VMEM((width, rows), B16),
        pltpu.VMEM((width, rows), B16),
        pltpu.VMEM((rows, width), F32),
        pltpu.VMEM((rows, width), F32),
        pltpu.VMEM(wout.shape, F32),
        pltpu.VMEM((rows, PIECE), B16),
        pltpu.VMEM((rows, PIECE), B16),
        pltpu.VMEM((8, width), F32),
        pltpu.VMEM((kept + 1, 8, width), F32),
        pltpu.VMEM(o.shape, B16),
        dma((rows // TILE, share)), dma((blocks, block // TILE)),
    ]
    if summing:
        out_rows = slabs // 2 * width
        more = [
            shape((LAST + 1, 2, 2 * half, LANES), B16), shape((half // 2, LANES), B16), shape((2 * half, LANES), B16),
            shape((out_rows, LANES), B16),
        ]
        scratch += [
            pltpu.VMEM((LAST * 2 * half, LANES), B16),
            pltpu.VMEM((4, half, LANES), B16),
            pltpu.VMEM((out_rows, LANES), B16),
            pltpu.VMEM((2, half, LANES), B16),
            pltpu.VMEM((out_rows, LANES), B16),
            dma((steps + 1,)), dma((steps + 1,)),
            *sum_buffers(ORDER, LAST, 2 * half), *sum_sems(ORDER, LAST),
        ]
        outs += more
        out_specs += [ANY] + [fixed(value) for value in more[1:]]
    else:
        outs += [shape((steps, 2 * half, LANES), B16), shape(wout.shape, B16)]
        out_specs += [pl.BlockSpec((1, 2 * half, LANES), lambda c: (jnp.minimum(c, steps - 1), 0, 0)), fixed(outs[-1])]
    return pl.pallas_call(
        functools.partial(middle_kernel, kept, steps, hist_steps, summing),
        grid=(steps + hist_steps,),
        out_shape=tuple(outs),
        in_specs=[SMEM, SMEM, fixed(all_lengths), fixed(o), fixed(x), fixed(cot), fixed(wout), fixed(gain), up_spec, down_spec, hist_spec],
        out_specs=tuple(out_specs),
        scratch_shapes=scratch,
        compiler_params=pltpu.CompilerParams(
            vmem_limit_bytes=62 * 2**20, collective_id=2, has_side_effects=True
        ),
        cost_estimate=pl.CostEstimate(flops=33 * 10**9, bytes_accessed=60 * 2**20, transcendentals=3 * 10**6),
        name="mlp_both_ways",
    )(scale, lengths, all_lengths, o, x, cot, wout, gain, up, down, hist)


def history_kernel(block, scale_ref, len_ref, alllen_ref, cot_ref, hgrad_ref):
    place = Place()
    factor = loss_factor(alllen_ref, place.batches * 2 * place.count * block)
    kept, count, _ = hgrad_ref.shape
    start = pl.program_id(1) * count + place.k * block
    index = lax.broadcasted_iota(jnp.int32, (count, LANES), 0) + start
    scale = jnp.where(index < len_ref[pl.program_id(0)], factor, 0.0)[:, :1]
    top = cot_ref[...].astype(F32) * scale
    for j in range(kept):
        hgrad_ref[j] = (scale_ref[j] * top).astype(B16)


def history_part(scale, lengths, all_lengths, cot, kept, block):
    rows, width = cot.shape
    tiles = block // TILE
    return pl.pallas_call(
        functools.partial(history_kernel, block),
        grid=(rows // block, tiles),
        out_shape=jax.ShapeDtypeStruct((kept, rows, width), B16),
        in_specs=[
            SMEM, SMEM, pl.BlockSpec(all_lengths.shape, lambda s, t: (0, 0, 0, 0)),
            pl.BlockSpec((TILE, width), lambda s, t: (s * tiles + t, 0)),
        ],
        out_specs=pl.BlockSpec((kept, TILE, width), lambda s, t: (0, s * tiles + t, 0)),
        compiler_params=pltpu.CompilerParams(vmem_limit_bytes=62 * 2**20),
        cost_estimate=pl.CostEstimate(flops=10**7, bytes_accessed=14 * 2**20, transcendentals=0),
        name="history_gradient",
    )(scale, lengths, all_lengths, cot)


def finish_kernel(x_ref, gain_ref, gmid_ref, gn_ref, out_ref):
    unit, spread = center_of(x_ref[0].astype(F32))
    unit_grad = jnp.concatenate([gn_ref[0, 0, i] for i in range(gn_ref.shape[2])], axis=1).astype(F32) * gain_ref[...]
    back = spread * (
        unit_grad - jnp.mean(unit_grad, -1, keepdims=True) - unit * jnp.mean(unit_grad * unit, -1, keepdims=True)
    )
    out_ref[0] = (gmid_ref[0] + back).astype(B16)


def finish(x, gain, gmid, gn):
    seqs, block, width = x.shape
    by_row = pl.BlockSpec((1, TILE, width), lambda s, t: (s, t, 0))
    return pl.pallas_call(
        finish_kernel,
        grid=(seqs, block // TILE),
        out_shape=jax.ShapeDtypeStruct(x.shape, B16),
        in_specs=[
            by_row,
            pl.BlockSpec(gain.shape, lambda s, t: (0, 0)),
            by_row,
            pl.BlockSpec((1, 1, width // LANES, TILE, LANES), lambda s, t: (s, t, 0, 0, 0)),
        ],
        out_specs=by_row,
        compiler_params=pltpu.CompilerParams(vmem_limit_bytes=62 * 2**20),
        name="norm_backward",
    )(x, gain, gmid, gn)


def whole_pairs(weight, heads):
    if heads % 2 == 0:
        return weight
    parted = weight.reshape(weight.shape[0], -1, heads * HD)
    return jnp.pad(parted, ((0, 0), (0, 0), (0, HD))).reshape(weight.shape[0], -1)


def body(
    tokens, history, cotangent, qkv_weight, out_weight, up_weight, down_weight, attn_gain, mlp_gain, depth_mix, lengths,
    positions,
):
    seqs, block, width = tokens.shape
    kept = history.shape[0]
    n = lax.axis_size("seq")
    batches = lax.axis_size("batch")
    place = Place()
    share = n // 2
    heads = H // share
    pairs = (heads + 1) // 2
    rows = seqs * block
    total = n * block

    wide_qkv = whole_pairs(qkv_weight, heads)
    o, att, normed, qp, kp, vp, cosine, sine, normed_t, all_lengths = attend(tokens, positions, lengths, wide_qkv, attn_gain)

    wide_out = jnp.pad(
        out_weight.reshape(share, heads * HD, width), ((0, 0), (0, (2 * pairs - heads) * HD), (0, 0))
    ).reshape(-1, width)
    summing = n == 4 and batches == 8
    hgrad = history_part(depth_mix, lengths, all_lengths, cotangent.reshape(rows, width), kept, block)
    mixed, gmid, grad, small, *parts = middle_part(
        depth_mix, lengths, all_lengths, o, tokens.reshape(rows, width), cotangent.reshape(rows, width), wide_out, mlp_gain, up_weight,
        down_weight, history.reshape(kept, rows, width), summing,
    )
    inner = up_weight.shape[1]
    slabs = width // LANES
    if summing:
        early_sums, half_sum, own_grads, own_out = parts
        sums, osums, qsums, small, input_grad = summing_back(
            qp, kp, vp, grad, att, cosine, sine, normed, normed_t, small, half_sum[None], own_grads, own_out, attn_gain, wide_qkv,
            tokens, gmid.reshape(tokens.shape), early_sums,
        )
        down_grad, up_grad, out_grad, qkv_grad = widen(sums, osums, qsums, width, inner)
    else:
        qkvg, gn, gain_part = plain_back(qp, kp, vp, grad, att, cosine, sine, normed, wide_qkv)
        slots = to_owners(gn.reshape(n, block, width), "exchange_normed_grad", 3)
        normed_grad = slots.astype(F32).sum(1).reshape(seqs, block // TILE, TILE, slabs, LANES).swapaxes(2, 3)
        small = lax.psum(small.at[-1].set(gain_part.sum(0)), ("batch", "seq"))
        mine = qkvg.reshape(width, 3, 1, 2 * pairs * HD)[..., : heads * HD]
        spread = jnp.zeros((width, 3, share, heads * HD), B16)
        spread = lax.dynamic_update_slice(spread, mine, (0, 0, place.u, 0)).reshape(width, -1)
        both, out_grad, qkv_grad = (v.astype(F32) for v in lax.psum((*parts, spread), ("batch", "seq")))
        chunks = jnp.moveaxis(both.reshape(inner // PIECE, 2, PIECE // LANES, width, LANES), 3, 1)
        down_grad = chunks[:, :, 0].swapaxes(0, 1).reshape(width, inner).T
        up_grad = chunks[:, :, 1].swapaxes(0, 1).reshape(width, inner)
        out_grad = out_grad.reshape(share, 2 * pairs * HD, width)[:, : heads * HD].reshape(H * HD, width)
        input_grad = finish(tokens, attn_gain[None, :], gmid.reshape(tokens.shape), normed_grad)
    return (
        mixed.reshape(tokens.shape),
        input_grad,
        hgrad.reshape(history.shape),
        qkv_grad,
        out_grad,
        up_grad,
        down_grad,
        small[-1] / attn_gain,
        small[0],
        small[1 : kept + 2].sum(1),
    )


def solution(mesh):
    placed = (
        P("batch", "seq", None),
        P(None, "batch", "seq", None),
        P("batch", "seq", None),
        P(),
        P(),
        P(),
        P(),
        P(),
        P(),
        P(),
        P("batch"),
        P("batch", "seq"),
    )
    return jax.shard_map(
        body,
        mesh=mesh,
        in_specs=placed,
        out_specs=(
            P("batch", "seq", None),
            P("batch", "seq", None),
            P(None, "batch", "seq", None),
            P(),
            P(),
            P(),
            P(),
            P(),
            P(),
            P(),
        ),
        check_vma=False,
    )
```

```python
import functools
import math

import jax
import jax.numpy as jnp
import numpy as np
from jax import lax
from jax.experimental import pallas as pl
from jax.experimental.pallas import tpu as pltpu
from jax.sharding import PartitionSpec as P

H = 12
HD = 64
LANES = 128
TILE = 256
PIECE = 512
QUERIES = 256
ROWS = 512
NEGATIVE = -1e30
epsilon = 1e-05
MESH = pl.DeviceIdType.MESH
F32 = jnp.float32
B16 = jnp.bfloat16
VMEM = pl.BlockSpec(memory_space=pltpu.VMEM)
SMEM = pl.BlockSpec(memory_space=pltpu.SMEM)
ANY = pl.BlockSpec(memory_space=pl.ANY)


def dot(a, b):
    return jnp.dot(a, b, preferred_element_type=F32)


def dot_nt(a, b):
    return lax.dot_general(a, b, (((1,), (1,)), ((), ())), preferred_element_type=F32)


def dot_tn(a, b):
    return lax.dot_general(a, b, (((0,), (0,)), ((), ())), preferred_element_type=F32)


def turned(values):
    return jnp.transpose(values)


def lane_of(shape):
    return lax.broadcasted_iota(jnp.int32, shape, 1)


def three(values):
    high = values.astype(B16).astype(F32)
    rest = values - high
    middle = rest.astype(B16).astype(F32)
    return high, middle, rest - middle


class Place:
    def __init__(self):
        self.count = lax.axis_size("seq")
        self.each = self.count // 4
        self.share = 2 * self.each
        self.batches = lax.axis_size("batch")
        self.b = lax.axis_index("batch")
        self.k = lax.axis_index("seq")
        self.core = lax.rem(self.b, 2)
        self.base = self.b - self.core
        self.q = lax.div(self.k, self.each)
        self.u = lax.rem(self.k, self.each) * 2 + self.core

    def worker(self, q, u):
        return (self.base + u % 2, q * self.each + u // 2)

    def owner(self, q, j):
        return (self.base + lax.div(q, 2), j)

    def is_me(self, device):
        return jnp.logical_and(device[0] == self.b, device[1] == self.k)


def greet(place, other_planes=()):
    barrier = pltpu.get_barrier_semaphore()
    met = 0
    for other in (0, 1):
        for step in range(place.count):
            if other == 0 and step == 0:
                continue
            core = lax.rem(place.core + other, 2)
            k = lax.rem(place.k + step, place.count)
            pl.semaphore_signal(barrier, inc=1, device_id=(place.base + core, k), device_id_type=MESH)
            met += 1
    for step in range(place.batches // 2 - 1):
        base = lax.rem(place.base + 2 * (step + 1), place.batches)
        for core in other_planes:
            pl.semaphore_signal(barrier, inc=1, device_id=(base + core, place.k), device_id_type=MESH)
            met += 1
    pl.semaphore_wait(barrier, met)


class Copies:
    def __init__(self, place):
        self.place = place
        self.sent = []

    def post(self, src, dst, send_sem, recv_sem, device):
        mine = self.place.is_me(device)
        far = pltpu.make_async_remote_copy(
            src_ref=src, dst_ref=dst, send_sem=send_sem, recv_sem=recv_sem,
            device_id=device, device_id_type=MESH,
        )

        @pl.when(jnp.logical_not(mine))
        def _():
            far.start()

        @pl.when(mine)
        def _():
            pltpu.make_async_copy(src, dst, recv_sem).start()

        self.sent.append((mine, far))

    def drain(self):
        for mine, far in self.sent:
            @pl.when(jnp.logical_not(mine))
            def _():
                far.wait_send()


def remote(src, dst, send_sem, recv_sem, device):
    return pltpu.make_async_remote_copy(
        src_ref=src, dst_ref=dst, send_sem=send_sem, recv_sem=recv_sem, device_id=device, device_id_type=MESH
    )


def arrived(slot, sem):
    pltpu.make_async_copy(slot, slot, sem).wait()


def to_owners_kernel(src_ref, dst_ref, send, recv):
    place = Place()
    greet(place)
    copies = Copies(place)
    for step in range(place.count):
        j = lax.rem(place.k + step, place.count)
        s = lax.rem(place.q, 2)
        copies.post(src_ref.at[j], dst_ref.at[s, place.u], send.at[step], recv.at[s, place.u], place.owner(place.q, j))
    for s in (0, 1):
        for u in range(place.share):
            arrived(dst_ref.at[s, u], recv.at[s, u])
    copies.drain()


def to_owners(values, name, number):
    n = lax.axis_size("seq")
    dma = pltpu.SemaphoreType.DMA
    return pl.pallas_call(
        to_owners_kernel,
        out_shape=jax.ShapeDtypeStruct((2, n // 2) + values.shape[1:], values.dtype),
        in_specs=[ANY],
        out_specs=ANY,
        scratch_shapes=[dma((n,)), dma((2, n // 2))],
        compiler_params=pltpu.CompilerParams(collective_id=number, has_side_effects=True),
        name=name,
    )(values)


class Sum:
    def __init__(self, place, order, rows, source, bufs, result, first, sems):
        groups = {
            "z": (lax.div(place.base, 2), 4, lambda i: (2 * i + place.core, place.k)),
            "seq": (place.k, 4, lambda i: (place.b, i)),
            "all": (2 * place.base + place.k, 16, lambda i: (2 * lax.div(i, 4) + place.core, lax.rem(i, 4))),
        }
        self.levels = [groups[name] for name in order]
        self.rows = []
        for _, size, _ in self.levels:
            rows = rows // size
            self.rows.append(rows)
        count = len(order)
        self.core = place.core
        self.partner = (place.base + 1 - place.core, place.k)
        self.source, self.result, self.first = source, result, first
        self.recvs, self.helds = bufs[0::2], bufs[1::2]
        self.out_sems = [sems[2 * i : 2 * i + 2] for i in range(count)]
        self.back_sems = [sems[2 * count + 2 * i : 2 * count + 2 * i + 2] for i in range(count)]
        self.here, self.swap_send, self.swap_recv = sems[4 * count :]

    def others(self, level):
        me, size, _ = self.levels[level]
        return [lax.rem(me + d, size) for d in range(1, size)]

    def shard(self, unit, level, i):
        held = self.source(unit) if level == 0 else self.helds[level - 1].at[unit]
        return held.at[pl.ds(pl.multiple_of(i * self.rows[level], 16), self.rows[level])]

    def region(self, unit, level, i):
        start = i * self.rows[level]
        for before in range(level):
            start = start + self.levels[before][0] * self.rows[before]
        return self.result.at[self.first + unit, self.core, pl.ds(pl.multiple_of(start, 16), self.rows[level])]

    def outward(self, unit, level):
        me, _, device = self.levels[level]
        send, recv = self.out_sems[level]
        for d, i in enumerate(self.others(level)):
            yield remote(
                self.shard(unit, level, i), self.recvs[level].at[unit, me], send.at[unit, d], recv.at[unit, me], device(i)
            )

    def back(self, unit, level):
        me, _, device = self.levels[level]
        send, recv = self.back_sems[level]
        last = level == len(self.levels) - 1
        region = self.region(unit, level, me)
        for d, i in enumerate(self.others(level)):
            src = self.helds[level].at[unit] if last else region
            yield remote(src, region, send.at[unit, d], recv.at[unit, me], device(i))

    def keep(self, unit):
        last = len(self.levels) - 1
        return pltpu.make_async_copy(
            self.helds[last].at[unit], self.region(unit, last, self.levels[last][0]), self.here.at[unit]
        )

    def cross(self, unit):
        region = self.result.at[self.first + unit, self.core]
        return remote(region, region, self.swap_send.at[unit], self.swap_recv.at[unit], self.partner)

    def scatter(self, unit):
        self.send(unit, 0)

    def sum(self, unit, level, onward=True):
        others = self.others(level)
        recv = self.recvs[level]
        for i in others:
            arrived(recv.at[unit, i], self.out_sems[level][1].at[unit, i])
        own = self.shard(unit, level, self.levels[level][0])
        pieces = 4 if self.rows[level] % 64 == 0 else 1
        size = self.rows[level] // pieces
        for piece in range(pieces):
            rows = slice(piece * size, (piece + 1) * size)
            total = own[rows, :].astype(F32)
            for i in others:
                total = total + recv[unit, i, rows, :].astype(F32)
            self.helds[level][unit, rows, :] = total.astype(B16)
        if onward and level + 1 < len(self.levels):
            self.send(unit, level + 1)

    def send(self, unit, level):
        for copy in self.outward(unit, level):
            copy.start()

    def share(self, unit):
        self.keep(unit).start()
        for copy in self.back(unit, len(self.levels) - 1):
            copy.start()

    def collect(self, unit, level):
        if level == len(self.levels) - 1:
            self.keep(unit).wait()
        for i in self.others(level):
            arrived(self.region(unit, level, i), self.back_sems[level][1].at[unit, i])

    def gather(self, unit, level, collected=False):
        if not collected:
            self.collect(unit, level + 1)
        for copy in self.back(unit, level):
            copy.start()

    def swap(self, unit):
        self.collect(unit, 0)
        self.cross(unit).start()

    def close(self, unit, out=(), back=()):
        for level in range(len(self.levels)):
            for copy in self.outward(unit, level) if level in out else ():
                copy.wait_send()
            for copy in self.back(unit, level) if level in back else ():
                copy.wait_send()

    def end(self, unit):
        self.cross(unit).wait_send()
        arrived(self.result.at[self.first + unit, 1 - self.core], self.swap_recv.at[unit])


SIZES = {"z": 4, "seq": 4, "all": 16}


def sum_buffers(order, units, rows):
    bufs = []
    for name in order:
        rows //= SIZES[name]
        bufs += [pltpu.VMEM((units, SIZES[name], rows, LANES), B16), pltpu.VMEM((units, rows, LANES), B16)]
    return bufs


def sum_sems(order, units):
    dma = pltpu.SemaphoreType.DMA
    each = [dma((units, count)) for name in order for count in (SIZES[name] - 1, SIZES[name])]
    return each + each + [dma((units,))] * 3


def center_of(values):
    center = values - jnp.mean(values, -1, keepdims=True)
    spread = lax.rsqrt(jnp.mean(center * center, -1, keepdims=True) + epsilon)
    return center * spread, spread


def partner_of(values, lane):
    return jnp.where(lax.rem(lane, HD) < HD // 2, pltpu.roll(values, LANES - HD // 2, 1), pltpu.roll(values, HD // 2, 1))


def own_columns(place, all_ref, w_ref, sems):
    wide = w_ref.shape[1] // 3
    return [
        pltpu.make_async_copy(
            all_ref.at[:, pl.ds(pl.multiple_of((part * place.share + place.u) * wide, LANES), wide)],
            w_ref.at[:, pl.ds(part * wide, wide)],
            sems.at[part],
        )
        for part in range(3)
    ]


def turn_tables(position_row, freq_ref):
    turned = freq_ref[...] * position_row.astype(F32)
    cosine, sine = jnp.cos(turned), jnp.sin(turned)
    return (
        jnp.transpose(jnp.concatenate([cosine] * 4, axis=0)),
        jnp.transpose(jnp.concatenate([-sine, sine, -sine, sine], axis=0)),
    )


def attend_kernel(
    pairs, len_in, tok_ref, wall_ref, pos_in, gain_in, freq_ref,
    o_ref, att_out, normed_out, qp_out, kp_out, vp_out, cos_out, sin_out, nt_out, alllen_ref,
    seq_ref, allpos_ref, w_ref, att_ref, normed_ref, qp_ref, kp_ref, vp_ref, cos_ref, sin_ref, out_ref, pos_ref, len_ref,
    kt_ref, nt_ref, wsem, send, recv, tsend, trecv, fsend, frecv, psend, precv, lsend, lrecv, osem, psem,
):
    place = Place()
    n, share = place.count, place.share
    for copy in own_columns(place, wall_ref, w_ref, wsem):
        copy.start()
    blocks, _, block, _ = out_ref.shape
    for s in (0, 1):
        len_ref[s] = jnp.full(len_ref.shape[1:], len_in[s], jnp.int32)
        for i in range(block // LANES):
            pos_ref[s, i : i + 1, :] = pos_in[s : s + 1, i * LANES : (i + 1) * LANES]
    gain = gain_in[...].reshape(1, gain_in.shape[0])
    greet(place, (0, 1))
    total = blocks * block
    tiles = total // TILE
    copies = Copies(place)
    for s in (0, 1):
        q = 2 * place.core + s
        for u in range(share):
            device = place.worker(q, u)
            copies.post(pos_ref.at[s], allpos_ref.at[place.k], psend.at[s, u], precv.at[place.k], device)
    for step in range(place.batches):
        b = lax.rem(place.b + step, place.batches)
        copies.post(len_ref, alllen_ref.at[place.b], lsend.at[step], lrecv.at[place.b], (b, place.k))
    first = lax.rem(place.k, 2)
    if n == 4:
        far_corner = lax.div(place.k, 2) != place.core
        order = lambda step: (
            place.k
            + jnp.where(step == 1, 1 - 2 * lax.rem(place.k, 2), 0)
            + jnp.where(step == 2, 2 - 4 * lax.div(place.k, 2), 0)
            + jnp.where(step == 3, 3 - 2 * place.k, 0)
        )
    else:
        far_corner = place.k < 0
        order = lambda step: lax.rem(place.k + step, n)

    def token_copies(turn):
        s = first if turn == 0 else 1 - first
        for u in range(share):
            device = place.worker(2 * place.core + s, u)
            src, dst, arrival = tok_ref.at[s, u], seq_ref.at[place.k, u], trecv.at[place.k]
            yield place.is_me(device), remote(src, dst, tsend.at[turn, u], arrival, device), pltpu.make_async_copy(
                src, dst, arrival
            )

    def post_tokens(turn):
        for mine, far_copy, near_copy in token_copies(turn):

            @pl.when(jnp.logical_not(mine))
            def _():
                far_copy.start()

            @pl.when(mine)
            def _():
                near_copy.start()

    def tokens_left(turn):
        for mine, far_copy, _ in token_copies(turn):

            @pl.when(jnp.logical_not(mine))
            def _():
                far_copy.wait_send()

    post_tokens(0)

    @pl.when(jnp.logical_not(far_corner))
    def _():
        post_tokens(1)

    def forward(j, other):
        u = lax.rem(place.u + other, share)
        device = (place.base + lax.rem(u, 2), place.q * place.each + lax.div(u, 2))
        piece = seq_ref.at[j, place.u]
        return remote(piece, piece, fsend.at[j, other - 1], frecv.at[j, other - 1], device)

    def leave(p, j):
        src, dst = out_ref.at[j, p], o_ref.at[lax.rem(place.q, 2), place.u, p]
        arrival = recv.at[lax.rem(place.q, 2), place.u, p]
        device = place.owner(place.q, j)
        return place.is_me(device), remote(src, dst, send.at[p, j], arrival, device), pltpu.make_async_copy(src, dst, arrival)

    for copy in own_columns(place, wall_ref, w_ref, wsem):
        copy.wait()
    for b in range(place.batches):
        arrived(alllen_ref.at[b], lrecv.at[b])
    length = alllen_ref[place.base + lax.div(place.q, 2), lax.rem(place.q, 2), 0:1, :]
    lane = lane_of((TILE, LANES))
    row = lax.broadcasted_iota(jnp.int32, (TILE, LANES), 0)

    def project(x, start):
        rows = pl.ds(start, TILE)
        unit, _ = center_of(x.astype(F32))
        normed = (unit * gain).astype(B16)
        normed_ref[rows, :] = normed
        nt_ref[:, rows] = turned(normed)
        proj = dot(normed, w_ref[...])
        cosine, sine = cos_ref[rows, :], sin_ref[rows, :]
        real = row + start < length
        q_rest = jnp.where(lane == HD, 1.0, 0.0)
        k_rest = jnp.where(lane == HD, jnp.where(real, 0.0, NEGATIVE), jnp.where(lane < HD + 4, 1.0, 0.0))
        v_rest = jnp.where(real, 1.0, 0.0)
        for p in range(pairs):
            for part, (to_ref, rest) in enumerate(((qp_ref, q_rest), (kp_ref, k_rest), (vp_ref, v_rest))):
                at = (part * pairs + p) * LANES
                values = proj[:, at : at + LANES]
                if part < 2:
                    values = values * cosine + partner_of(values, lane) * sine
                if part == 0:
                    values = values * (1.0 / math.sqrt(HD))
                to_ref[2 * p, rows, :] = jnp.where(lane < HD, values, rest).astype(B16)
                to_ref[2 * p + 1, rows, :] = jnp.where(lane < HD, pltpu.roll(values, HD, 1), rest).astype(B16)

    @pl.loop(0, n)
    def _(step):
        j = order(step)

        @pl.when(jnp.logical_and(step == 1, far_corner))
        def _():
            tokens_left(0)
            post_tokens(1)

        arrived(seq_ref.at[j, place.u], trecv.at[j])
        for other in range(1, share):
            forward(j, other).start()
        arrived(allpos_ref.at[j], precv.at[j])
        start = pl.multiple_of(j * block, block)
        for i in range(block // LANES):
            cosine, sine = turn_tables(allpos_ref[j, i : i + 1, :], freq_ref)
            rows = pl.ds(pl.multiple_of(start + i * LANES, LANES), LANES)
            cos_ref[rows, :] = cosine
            sin_ref[rows, :] = sine
        if block // share == TILE:
            for other in range(share):
                u = lax.rem(place.u + share - other, share)
                if other:
                    arrived(seq_ref.at[j, u], frecv.at[j, other - 1])
                project(seq_ref[j, u], pl.multiple_of(start + u * TILE, TILE))
        else:
            for other in range(1, share):
                u = lax.rem(place.u + share - other, share)
                arrived(seq_ref.at[j, u], frecv.at[j, other - 1])
            for i in range(block // TILE):
                whole = seq_ref[j].reshape(block, seq_ref.shape[3])
                project(whole[i * TILE : (i + 1) * TILE], pl.multiple_of(start + i * TILE, TILE))

    ready = [(normed_ref, normed_out), (kp_ref, kp_out), (vp_ref, vp_out), (cos_ref, cos_out), (sin_ref, sin_out), (nt_ref, nt_out)]

    def whole_copies():
        for number, (src, dst) in enumerate(ready):
            yield pltpu.make_async_copy(src, dst, osem.at[number])

    def pair_copies(p):
        yield pltpu.make_async_copy(att_ref.at[p], att_out.at[p], psem.at[p, 0])
        yield pltpu.make_async_copy(qp_ref.at[pl.ds(2 * p, 2)], qp_out.at[pl.ds(2 * p, 2)], psem.at[p, 1])

    for copy in whole_copies():
        copy.start()
    later = jnp.where(lane_of((QUERIES, QUERIES)) <= lax.broadcasted_iota(jnp.int32, (QUERIES, QUERIES), 0), 0.0, NEGATIVE)

    lane = lane_of((QUERIES, LANES))

    @pl.loop(0, pairs)
    def _(p):
        for e in (0, 1):
            for i in range(tiles):
                rows = slice(i * TILE, (i + 1) * TILE)
                kt_ref[e, :, rows] = turned(kp_ref[2 * p + e, rows, :])
        for i in range(total // QUERIES):
            start = i * QUERIES
            found = []
            for e in (0, 1):
                h = 2 * p + e
                q = qp_ref[h, start : start + QUERIES, :]
                near = dot(q, kt_ref[e, :, start : start + QUERIES]) + later
                top = jnp.max(near, -1, keepdims=True)
                if i:
                    far = dot(q, kt_ref[e, :, :start])
                    top = jnp.maximum(top, jnp.max(far, -1, keepdims=True))
                out = dot(jnp.exp(near - top).astype(B16), vp_ref[h, start : start + QUERIES, :])
                if i:
                    out = out + dot(jnp.exp(far - top).astype(B16), vp_ref[h, :start, :])
                found.append(out)
                high, mid, low = three(-(top + jnp.log(out)))
                q_new = jnp.where(lane == HD + 1, high, jnp.where(lane == HD + 2, mid, jnp.where(lane == HD + 3, low, q.astype(F32))))
                qp_ref[h, start : start + QUERIES, :] = q_new.astype(B16)
            even, odd = found
            low_half = lane < HD
            att = jnp.where(low_half, even, pltpu.roll(odd, HD, 1)) / jnp.where(low_half, pltpu.roll(even, HD, 1), odd)
            att_ref[p, start : start + QUERIES, :] = att
            j, within = start // block, start % block
            out_ref[j, p, within : within + QUERIES, :] = att.astype(B16)
            if within + QUERIES == block:
                mine, far_copy, near_copy = leave(p, j)

                @pl.when(jnp.logical_not(mine))
                def _():
                    far_copy.start()

                @pl.when(mine)
                def _():
                    near_copy.start()
        for copy in pair_copies(p):
            copy.start()

    for copy in whole_copies():
        copy.wait()
    copies.drain()

    @pl.when(jnp.logical_not(far_corner))
    def _():
        tokens_left(0)

    tokens_left(1)
    for j in range(n):
        for other in range(1, share):
            forward(j, other).wait_send()
    for p in range(pairs):
        for copy in pair_copies(p):
            copy.wait()
        for s in (0, 1):
            for u in range(place.share):
                arrived(o_ref.at[s, u, p], recv.at[s, u, p])
        for j in range(blocks):
            mine, far_copy, _ = leave(p, j)

            @pl.when(jnp.logical_not(mine))
            def _():
                far_copy.wait_send()


def attend(tokens, positions, lengths, w_all, gain):
    n = lax.axis_size("seq")
    batches = lax.axis_size("batch")
    share = n // 2
    _, block, width = tokens.shape
    total = n * block
    pairs = w_all.shape[1] // (3 * share * LANES)
    dma = pltpu.SemaphoreType.DMA

    def shape(dims, kind=B16):
        return jax.ShapeDtypeStruct(dims, kind)

    heads = (2 * pairs, total, LANES)
    table = (total, LANES)
    frequency = (1.0 / 10000.0 ** (np.arange(HD // 2) * 2.0 / HD)).astype(np.float32)
    return pl.pallas_call(
        functools.partial(attend_kernel, pairs),
        out_shape=(
            shape((2, share, pairs, block, LANES)), shape((pairs, total, LANES), F32), shape((total, width)),
            shape(heads), shape(heads), shape(heads), shape(table, F32), shape(table, F32),
            shape((width, total)), shape((batches, 2, 8, LANES), jnp.int32),
        ),
        in_specs=[SMEM] + [ANY] * 2 + [VMEM] * 3,
        out_specs=(ANY,) * 9 + (VMEM,),
        scratch_shapes=[
            pltpu.VMEM((n, share, block // share, width), B16),
            pltpu.VMEM((n, block // LANES, LANES), jnp.int32),
            pltpu.VMEM((width, 3 * pairs * LANES), B16),
            pltpu.VMEM((pairs, total, LANES), F32),
            pltpu.VMEM((total, width), B16),
            pltpu.VMEM(heads, B16),
            pltpu.VMEM(heads, B16),
            pltpu.VMEM(heads, B16),
            pltpu.VMEM(table, F32),
            pltpu.VMEM(table, F32),
            pltpu.VMEM((n, pairs, block, LANES), B16),
            pltpu.VMEM((2, block // LANES, LANES), jnp.int32),
            pltpu.VMEM((2, 8, LANES), jnp.int32),
            pltpu.VMEM((2, LANES, total), B16),
            pltpu.VMEM((width, total), B16),
            dma((3,)), dma((pairs, n)), dma((2, share, pairs)), dma((2, share)), dma((n,)), dma((n, share - 1)),
            dma((n, share - 1)), dma((2, share)), dma((n,)), dma((batches,)), dma((batches,)), dma((6,)), dma((pairs, 2)),
        ],
        compiler_params=pltpu.CompilerParams(
            vmem_limit_bytes=56 * 2**20, collective_id=1, has_side_effects=True
        ),
        cost_estimate=pl.CostEstimate(flops=30 * 10**9, bytes_accessed=30 * 2**20, transcendentals=13 * 10**6),
        name="attention_forward",
    )(
        lengths, tokens.reshape(2, share, block // share, width), w_all, positions, gain,
        np.broadcast_to(frequency[:, None], (HD // 2, LANES)).copy(),
    )


def lay_gradient(do_ref, att_ref, dop_ref, dot_ref, p):
    block = do_ref.shape[2]
    lane = lane_of((TILE, LANES))
    low_half = lane < HD
    for i in range(dop_ref.shape[1] // TILE):
        start = i * TILE
        grad = do_ref[start // block, p, start % block : start % block + TILE, :].astype(F32)
        product = grad * att_ref[p, start : start + TILE, :]
        for e in (0, 1):
            side = low_half if e == 0 else jnp.logical_not(low_half)
            high, mid, low = three(-jnp.sum(jnp.where(side, product, 0.0), -1, keepdims=True))
            head = grad if e == 0 else pltpu.roll(grad, HD, 1)
            rest = jnp.where(lane == HD, high, jnp.where(lane == HD + 1, mid, jnp.where(lane == HD + 2, low, 0.0)))
            both = jnp.where(low_half, head, rest).astype(B16)
            dop_ref[e, start : start + TILE, :] = both
            dot_ref[e, :, start : start + TILE] = turned(both)


def pair_back(pairs, p, qp_ref, kp_ref, vp_ref, cos_ref, sin_ref, dop_ref, dot_ref, kt_ref, qt_ref, dq_ref, pg_ref, point):
    total = dop_ref.shape[1]
    tiles = total // TILE
    lane = lane_of((TILE, LANES))
    low_half = lane < HD
    earlier = jnp.where(lane_of((TILE, TILE)) >= lax.broadcasted_iota(jnp.int32, (TILE, TILE), 0), 0.0, NEGATIVE)

    def packed(even, odd):
        return jnp.where(low_half, even, pltpu.roll(odd, HD, 1))

    def unrotated(values, rows):
        return values * cos_ref[rows, :] - partner_of(values, lane) * sin_ref[rows, :]

    for i in range(tiles):
        rows = slice(i * TILE, (i + 1) * TILE)
        for e in (0, 1):
            kt_ref[e, :, rows] = turned(kp_ref[2 * p + e, rows, :])[:HD]
            qt_ref[e, :, rows] = turned(qp_ref[2 * p + e, rows, :])
    for j in range(tiles):
        start = j * TILE
        near_rows = slice(start, start + TILE)
        dks, dvs = [], []
        for e in (0, 1):
            h = 2 * p + e
            kj, vj = kp_ref[h, near_rows, :], vp_ref[h, near_rows, :]
            dk = dv = None
            for part in (0, 1):
                rows = near_rows if part == 0 else slice(start + TILE, total)
                if rows.start == total:
                    continue
                qs, dos = qp_ref[h, rows, :], dop_ref[e, rows, :]
                scores = dot(kj, qt_ref[e, :, rows])
                if part == 0:
                    scores = scores + earlier
                probs = jnp.exp(scores)
                dv_part = dot(probs.astype(B16), dos)
                grads = (probs * dot(vj, dot_ref[e, :, rows])).astype(B16)
                dk_part = dot(grads, qs)
                dq_part = dot(kt_ref[e, :, near_rows], grads)
                if j == 0:
                    dq_ref[e, :, rows] = dq_part
                else:
                    dq_ref[e, :, rows] += dq_part
                dk = dk_part if dk is None else dk + dk_part
                dv = dv_part if dv is None else dv + dv_part
            dks.append(dk)
            dvs.append(dv)
        pg_ref[pairs + p, near_rows, :] = unrotated(packed(*dks), near_rows).astype(B16)
        pg_ref[2 * pairs + p, near_rows, :] = packed(*dvs).astype(B16)
        point(j)
    for i in range(tiles):
        rows = slice(i * TILE, (i + 1) * TILE)
        both = jnp.concatenate([dq_ref[0, :, rows], dq_ref[1, :, rows]], axis=0)
        dq = jnp.transpose(both) * (1.0 / math.sqrt(HD))
        pg_ref[p, rows, :] = unrotated(dq, rows).astype(B16)


def plain_back_kernel(
    pairs, qp_ref, kp_ref, vp_ref, do_ref, att_ref, cos_ref, sin_ref, normed_ref, wall_ref, wgrad_ref, gn_ref, gaing_ref,
    dop_ref, dot_ref, kt_ref, qt_ref, dq_ref, pg_ref, w_ref, wsem,
):
    place = Place()
    for copy in own_columns(place, wall_ref, w_ref, wsem):
        copy.start()

    @pl.loop(0, pairs)
    def _(p):
        lay_gradient(do_ref, att_ref, dop_ref, dot_ref, p)
        pair_back(pairs, p, qp_ref, kp_ref, vp_ref, cos_ref, sin_ref, dop_ref, dot_ref, kt_ref, qt_ref, dq_ref, pg_ref, lambda j: None)

    for copy in own_columns(place, wall_ref, w_ref, wsem):
        copy.wait()
    gaing_ref[...] = jnp.zeros_like(gaing_ref)

    @pl.loop(0, normed_ref.shape[0] // TILE)
    def _(t):
        rows = pl.ds(pl.multiple_of(t * TILE, TILE), TILE)
        grads = jnp.concatenate([pg_ref[g, rows, :] for g in range(3 * pairs)], axis=1)
        grad = dot_nt(grads, w_ref[...])
        gaing_ref[...] += folded(grad * normed_ref[rows, :].astype(F32))
        gn_ref[rows, :] = grad.astype(B16)

    for part in range(3):
        grads = jnp.concatenate([pg_ref[part * pairs + p] for p in range(pairs)], axis=1)
        wgrad_ref[:, part * pairs * LANES : (part + 1) * pairs * LANES] = dot_tn(normed_ref[...], grads).astype(B16)


def plain_back(qp, kp, vp, grad, att, cosine, sine, normed, w_all):
    total, width = normed.shape
    pairs = att.shape[0]
    w = jax.ShapeDtypeStruct((width, 3 * pairs * LANES), B16)
    return pl.pallas_call(
        functools.partial(plain_back_kernel, pairs),
        out_shape=(w, jax.ShapeDtypeStruct((total, width), B16), jax.ShapeDtypeStruct((8, width), F32)),
        in_specs=[VMEM] * 8 + [ANY],
        out_specs=(VMEM,) * 3,
        scratch_shapes=[
            pltpu.VMEM((2, total, LANES), B16),
            pltpu.VMEM((2, LANES, total), B16),
            pltpu.VMEM((2, HD, total), B16),
            pltpu.VMEM((2, LANES, total), B16),
            pltpu.VMEM((2, HD, total), F32),
            pltpu.VMEM((3 * pairs, total, LANES), B16),
            pltpu.VMEM(w.shape, B16),
            pltpu.SemaphoreType.DMA((3,)),
        ],
        compiler_params=pltpu.CompilerParams(vmem_limit_bytes=56 * 2**20),
        cost_estimate=pl.CostEstimate(flops=60 * 10**9, bytes_accessed=30 * 2**20, transcendentals=13 * 10**6),
        name="attention_backward",
    )(qp, kp, vp, grad, att, cosine, sine, normed, w_all)


UNITS = 3
FAMILIES = {"e": ("seq", "z"), "o": ("z", "seq"), "q0": ("z", "seq"), "q1": ("seq", "z"), "q2": ("all",)}
EARLY = {
    (0, -1): [("send1", "e1"), ("scatter", "e2")],
    (0, 0): [("scatter", "o0")],
    (0, 2): [("sum1", "e1"), ("share", "e1"), ("gather0", "e0")],
    (0, 5): [("sum0", "e2")],
    (1, -1): [("sum0", "o0")],
    (1, 1): [("gather0", "e1")],
    (1, 2): [("sum1", "o0"), ("swap", "e0"), ("share", "o0")],
    (1, 3): [("sum1", "e2"), ("share", "e2")],
    (2, 0): [("swap", "e1"), ("sum0", "q0"), ("gather0", "o0")],
    (2, 1): [("gather0", "e2")],
    (2, 2): [("sum1", "q0"), ("sum0", "q1"), ("share", "q0")],
    (2, 7): [("swap", "o0")],
}
LATE = (
    ("sum1", "q1"),
    ("share", "q1"),
    ("gather0", "q0"),
    ("sum0", "q2"),
    ("share", "q2"),
    ("gather0", "q1"),
    ("swap", "e2"),
    ("swap", "q0"),
    ("swap", "q1"),
    ("swap", "q2"),
)
SMALL = (0, 3, 6)
FINISH = 7


def summing_back_kernel(
    pairs, qp_in, kp_in, vp_in, do_in, att_in, cos_in, sin_in, normed_in, nt_in, small_ref, half_sum_ref, mine_ref,
    outmine_ref, gain_ref, wall_ref, x_ref, gmid_ref, _, sums_ref, osums_ref, qsums_ref, total_ref, input_ref,
    dop_ref, dot_ref, kt_ref, qt_ref, dq_ref, pg_ref, w_ref, wg_ref, gn_ref, gnrecv_ref, sbuf_ref, srecv0_ref, srecv1_ref, srecv2_ref,
    slots_ref, xin_ref, gmidin_ref, qp_ref, kp_ref, vp_ref, do_ref, att_ref, cos_ref, sin_ref, normed_ref, nt_ref,
    pairsem, wholesem, wsem, insem, gsend, grecv, osend, orecv, ssend, srecv, *rest,
):
    def take(count):
        nonlocal rest
        taken, rest = rest[:count], rest[count:]
        return taken

    e_bufs, o_bufs = take(2 * len(FAMILIES["e"])), take(2 * len(FAMILIES["o"]))
    q_bufs = [take(2 * len(FAMILIES["q%d" % p])) for p in range(pairs)]
    sems = {}
    for name in ("e0", "e1", "e2", "o") + tuple("q%d" % p for p in range(pairs)):
        sems[name] = take(4 * len(FAMILIES["e" if name[0] == "e" else name]) + 3)
    e1_bufs = take(2)
    place = Place()
    core = place.core
    width = normed_ref.shape[1]
    slabs = width // LANES
    rows_q = wg_ref.shape[0] // pairs

    def pair_loads(p):
        both = pl.ds(2 * p, 2)
        moved = [(src.at[both], dst.at[both]) for src, dst in ((qp_in, qp_ref), (kp_in, kp_ref), (vp_in, vp_ref))]
        moved += [(do_in.at[:, p], do_ref.at[:, p]), (att_in.at[p], att_ref.at[p])]
        return [pltpu.make_async_copy(src, dst, pairsem.at[p, i]) for i, (src, dst) in enumerate(moved)]

    def whole_loads():
        moved = ((cos_in, cos_ref), (sin_in, sin_ref), (nt_in, nt_ref), (normed_in, normed_ref))
        return [pltpu.make_async_copy(src, dst, wholesem.at[i]) for i, (src, dst) in enumerate(moved)]

    for copy in pair_loads(0) + whole_loads() + [copy for p in range(1, pairs) for copy in pair_loads(p)]:
        copy.start()
    for copy in own_columns(place, wall_ref, w_ref, wsem):
        copy.start()
    greet(place, (core,))
    inputs = [
        pltpu.make_async_copy(x_ref, xin_ref, insem.at[0]), pltpu.make_async_copy(gmid_ref, gmidin_ref, insem.at[1])
    ]
    for copy in inputs:
        copy.start()
    units = {}
    for number, held in ((0, None), (1, half_sum_ref)):
        bufs = (None, held, *e1_bufs)
        units["e%d" % number] = (
            Sum(place, FAMILIES["e"], mine_ref.shape[0], None, bufs, sums_ref, number, sems["e%d" % number]), 0
        )
    last = Sum(place, FAMILIES["e"], mine_ref.shape[0], lambda unit: mine_ref, e_bufs, sums_ref, UNITS - 1, sems["e2"])
    units["e2"] = (last, 0)
    units["o0"] = (
        Sum(place, FAMILIES["o"], outmine_ref.shape[0], lambda unit: outmine_ref, o_bufs, osums_ref, 0, sems["o"]), 0
    )
    for p in range(pairs):
        name = "q%d" % p
        own = wg_ref.at[pl.ds(p * rows_q, rows_q)]
        units[name] = (
            Sum(place, FAMILIES[name], rows_q, lambda unit, own=own: own, q_bufs[p], qsums_ref, p, sems[name]), 0
        )
    partner = last.partner

    def stage(name, key):
        family, unit = units[key]
        if name[:3] == "sum":
            family.sum(unit, int(name[3:]))
        elif name[:4] == "send":
            family.send(unit, int(name[4:]))
        elif name[:6] == "gather":
            family.gather(unit, int(name[6:]), collected=key == "e0")
        else:
            getattr(family, name)(unit)

    def point(p, j):
        for (at_p, at_j), todo in EARLY.items():
            if at_j == j:

                @pl.when(p == at_p)
                def _(todo=todo):
                    for name, key in todo:
                        stage(name, key)

    @pl.loop(0, pairs)
    def _(p):
        point(p, -1)
        for copy in pair_loads(p):
            copy.wait()
        lay_gradient(do_ref, att_ref, dop_ref, dot_ref, p)

        @pl.when(p == 0)
        def _():
            for copy in whole_loads():
                copy.wait()

        pair_back(
            pairs, p, qp_ref, kp_ref, vp_ref, cos_ref, sin_ref, dop_ref, dot_ref, kt_ref, qt_ref, dq_ref, pg_ref, functools.partial(point, p)
        )
        grads = jnp.concatenate([pg_ref[part * pairs + p] for part in range(3)], axis=1)
        found = dot(nt_ref[...], grads).astype(B16)
        for part in range(3):
            rows = pl.ds(pl.multiple_of(p * rows_q + part * width, 16), width)
            wg_ref[rows, :] = found[:, part * LANES : (part + 1) * LANES]
        for at_p in range(pairs):

            @pl.when(p == at_p)
            def _(at_p=at_p):
                stage("scatter", "q%d" % at_p)

    for copy in own_columns(place, wall_ref, w_ref, wsem):
        copy.wait()

    def aside(j):
        return remote(gn_ref.at[j], gnrecv_ref.at[j], gsend.at[j], grecv.at[j], partner)

    def leave(j):
        src, dst, arrival = gn_ref.at[4 + j], slots_ref.at[lax.rem(place.q, 2), core], orecv.at[lax.rem(place.q, 2), core]
        device = place.owner(place.q, j)
        return place.is_me(device), remote(src, dst, osend.at[j], arrival, device), pltpu.make_async_copy(src, dst, arrival)

    def normed_grad(i):
        rows = pl.ds(pl.multiple_of(i * TILE, TILE), TILE)
        grads = jnp.concatenate([pg_ref[g, rows, :] for g in range(3 * pairs)], axis=1)
        grad = dot_nt(grads, w_ref[...])
        return grad, folded(grad * normed_ref[rows, :].astype(F32))

    gain_grad = jnp.zeros((8, width), F32)
    for j in range(4):
        grad, part = normed_grad(2 * j + 1 - core)
        gain_grad = gain_grad + part
        for i in range(slabs):
            gn_ref[j, i * TILE : (i + 1) * TILE, :] = grad[:, i * LANES : (i + 1) * LANES].astype(B16)
        aside(j).start()
    for j in range(4):
        grad, part = normed_grad(2 * j + core)
        gain_grad = gain_grad + part
        arrived(gnrecv_ref.at[j], grecv.at[j])
        for i in range(slabs):
            rows = slice(i * TILE, (i + 1) * TILE)
            gn_ref[4 + j, rows, :] = (
                grad[:, i * LANES : (i + 1) * LANES] + gnrecv_ref[j, rows, :].astype(F32)
            ).astype(B16)
        mine, far, near = leave(j)

        @pl.when(jnp.logical_not(mine))
        def _():
            far.start()

        @pl.when(mine)
        def _():
            near.start()

    bottom = lax.broadcasted_iota(jnp.int32, sbuf_ref.shape[1:], 0) == sbuf_ref.shape[1] - 1
    sbuf_ref[0] = jnp.where(bottom, jnp.sum(gain_grad, axis=0, keepdims=True), small_ref[...])
    (seq_me, _, seq_device), (z_me, _, z_device) = last.levels
    levels = [(seq_me, seq_device, srecv1_ref, 1), (z_me, z_device, srecv2_ref, 4)]

    def swap():
        return remote(sbuf_ref.at[0], srecv0_ref, ssend.at[0], srecv.at[0, 0], partner)

    def spread(level):
        me, device, into, at = levels[level]
        for d in (1, 2, 3):
            yield remote(
                sbuf_ref.at[level + 1], into.at[me], ssend.at[at + d - 1], srecv.at[level + 1, me],
                device(lax.rem(me + d, 4)),
            )

    def small_stage(level):
        if level == 0:
            arrived(srecv0_ref, srecv.at[0, 0])
            value = sbuf_ref[0] + srecv0_ref[...]
        else:
            me, device, into, at = levels[level - 1]
            into[me] = sbuf_ref[level]
            for d in (1, 2, 3):
                i = lax.rem(me + d, 4)
                arrived(into.at[i], srecv.at[level, i])
            value = into[0] + into[1] + into[2] + into[3]
        if level == 2:
            total_ref[...] = value
        else:
            sbuf_ref[level + 1] = value
            for copy in spread(level):
                copy.start()

    def finish_inputs():
        for copy in inputs:
            copy.wait()
        for s in range(2):
            for h in range(2):
                arrived(slots_ref.at[s, h], orecv.at[s, h])
                rows = slice(h * TILE, (h + 1) * TILE)
                unit, spread = center_of(xin_ref[s, rows, :].astype(F32))
                grad = [slots_ref[s, h, i * TILE : (i + 1) * TILE, :] for i in range(slabs)]
                unit_grad = jnp.concatenate(grad, axis=1).astype(F32) * gain_ref[...].reshape(1, width)
                back = spread * (
                    unit_grad
                    - jnp.mean(unit_grad, -1, keepdims=True)
                    - unit * jnp.mean(unit_grad * unit, -1, keepdims=True)
                )
                input_ref[s, rows, :] = (gmidin_ref[s, rows, :] + back).astype(B16)

    swap().start()
    for number, (name, key) in enumerate(LATE):
        stage(name, key)
        if number in SMALL:
            small_stage(SMALL.index(number))
        if number == FINISH:
            finish_inputs()
    for j in range(4):
        mine, far, _ = leave(j)

        @pl.when(jnp.logical_not(mine))
        def _():
            far.wait_send()

        aside(j).wait_send()
    swap().wait_send()
    for level in (0, 1):
        for copy in spread(level):
            copy.wait_send()
    for key, (family, unit) in units.items():
        levels = range(len(family.levels))
        family.close(unit, out={"e0": (), "e1": (1,)}.get(key, levels), back=(0,) if key == "e0" else levels)
        family.end(unit)


def summing_back(qp, kp, vp, grad, att, cosine, sine, normed, normed_t, small, half_sum, mine, outmine, gain, w_all, x, gmid, sums):
    total, width = normed.shape
    pairs = att.shape[0]
    slabs = width // LANES
    rows_e, rows_o, rows_q = mine.shape[0], outmine.shape[0], 3 * width
    dma = pltpu.SemaphoreType.DMA

    def shape(dims, kind=B16):
        return jax.ShapeDtypeStruct(dims, kind)

    return pl.pallas_call(
        functools.partial(summing_back_kernel, pairs),
        out_shape=(
            shape((UNITS, 2, rows_e, LANES)), shape((1, 2, rows_o, LANES)), shape((pairs, 2, rows_q, LANES)),
            shape(small.shape, F32), shape(x.shape),
        ),
        in_specs=[ANY] * 9 + [VMEM] * 5 + [ANY] * 4,
        out_specs=(ANY,) * 3 + (VMEM,) * 2,
        input_output_aliases={17: 0},
        scratch_shapes=[
            pltpu.VMEM((2, total, LANES), B16),
            pltpu.VMEM((2, LANES, total), B16),
            pltpu.VMEM((2, HD, total), B16),
            pltpu.VMEM((2, LANES, total), B16),
            pltpu.VMEM((2, HD, total), F32),
            pltpu.VMEM((3 * pairs, total, LANES), B16),
            pltpu.VMEM((width, 3 * pairs * LANES), B16),
            pltpu.VMEM((pairs * rows_q, LANES), B16),
            pltpu.VMEM((8, slabs * TILE, LANES), B16),
            pltpu.VMEM((4, slabs * TILE, LANES), B16),
            pltpu.VMEM((3,) + small.shape, F32),
            pltpu.VMEM(small.shape, F32),
            pltpu.VMEM((4,) + small.shape, F32),
            pltpu.VMEM((4,) + small.shape, F32),
            pltpu.VMEM((2, 2, slabs * TILE, LANES), B16),
            pltpu.VMEM(x.shape, B16),
            pltpu.VMEM(gmid.shape, F32),
            *(pltpu.VMEM(value.shape, value.dtype) for value in (qp, kp, vp, grad, att, cosine, sine, normed, normed_t)),
            dma((pairs, 5)), dma((4,)), dma((3,)), dma((2,)), dma((4,)), dma((4,)), dma((4,)), dma((2, 2)), dma((7,)), dma((3, 4)),
            *sum_buffers(FAMILIES["e"], 1, rows_e), *sum_buffers(FAMILIES["o"], 1, rows_o),
            *(buf for p in range(pairs) for buf in sum_buffers(FAMILIES["q%d" % p], 1, rows_q)),
            *(sem for _ in range(UNITS) for sem in sum_sems(FAMILIES["e"], 1)), *sum_sems(FAMILIES["o"], 1),
            *(sem for p in range(pairs) for sem in sum_sems(FAMILIES["q%d" % p], 1)),
            *sum_buffers(FAMILIES["e"][1:], 1, rows_e // 4),
        ],
        compiler_params=pltpu.CompilerParams(
            vmem_limit_bytes=62 * 2**20, collective_id=3, has_side_effects=True
        ),
        cost_estimate=pl.CostEstimate(flops=60 * 10**9, bytes_accessed=60 * 2**20, transcendentals=13 * 10**6),
        name="attention_backward_and_sums",
    )(qp, kp, vp, grad, att, cosine, sine, normed, normed_t, small, half_sum, mine, outmine, gain, w_all, x, gmid, sums)


def widen_kernel(downt_ref, upt_ref, outs_ref, q_ref, down_ref, up_ref, out_ref, qkv_ref):
    width = out_ref.shape[1]
    for i in range(2):
        down_ref[i * LANES : (i + 1) * LANES, :] = jnp.transpose(downt_ref[i * width : (i + 1) * width, :].astype(F32))
    at = 0
    for unit in range(upt_ref.shape[0]):
        for i in range(upt_ref.shape[2]):
            up_ref[:, at : at + LANES] = upt_ref[unit, 0, i].astype(F32)
            at += LANES
    for i in range(outs_ref.shape[0]):
        out_ref[:, i * LANES : (i + 1) * LANES] = outs_ref[i].astype(F32)
    at = 0
    for part in range(3):
        for u in range(q_ref.shape[1]):
            for p in range(q_ref.shape[0]):
                qkv_ref[:, at : at + LANES] = q_ref[p, u, part].astype(F32)
                at += LANES


def widen(sums, osums, qsums, width, inner):
    steps = inner // (2 * LANES)
    pairs, share = qsums.shape[:2]
    slabs = width // LANES
    some = width // steps
    turn = steps // UNITS

    def shape(dims):
        return jax.ShapeDtypeStruct(dims, F32)

    def by_row(columns):
        return pl.BlockSpec((some, columns), lambda c: (c, 0))

    return pl.pallas_call(
        widen_kernel,
        grid=(steps,),
        out_shape=(shape((inner, width)), shape((width, inner)), shape((width, width)), shape((width, 3 * width))),
        in_specs=[
            pl.BlockSpec((2 * width, LANES), lambda c: (lax.div(c, turn) * 2 * turn + lax.rem(c, turn), 0)),
            pl.BlockSpec((UNITS, 1, 2 * turn, some, LANES), lambda c: (0, 1, 0, c, 0)),
            pl.BlockSpec((slabs, some, LANES), lambda c: (0, c, 0)),
            pl.BlockSpec((pairs, share, 3, some, LANES), lambda c: (0, 0, 0, c, 0)),
        ],
        out_specs=(
            pl.BlockSpec((2 * LANES, width), lambda c: (c, 0)), by_row(inner), by_row(width), by_row(3 * width)
        ),
        compiler_params=pltpu.CompilerParams(vmem_limit_bytes=62 * 2**20),
        name="widen_sums",
    )(
        sums.reshape(-1, LANES), sums.reshape(UNITS, 2, 2 * turn, width, LANES), osums.reshape(slabs, width, LANES),
        qsums.reshape(pairs, share, 3, width, LANES),
    )


def slabs_of(ref, s, rows):
    return jnp.concatenate([ref[s, u, p, rows, :] for u in range(ref.shape[1]) for p in range(ref.shape[2])], axis=1)


def folded(values):
    return jnp.sum(values.reshape(values.shape[0] // 8, 8, values.shape[1]), axis=0)


LAST = 2
ORDER = ("seq", "z")


def swap_half(width):
    return PIECE * width // LANES


def loss_factor(alllen_ref, slots):
    count = None
    for b in range(alllen_ref.shape[0]):
        for s in (0, 1):
            part = alllen_ref[b, s, 0:1, :]
            count = part if count is None else count + part
    return slots / count.astype(F32)


def middle_kernel(
    kept, steps, hist_steps, summing, scale_ref, len_ref, alllen_ref, o_ref, x_ref, cot_ref, wout_ref, gain_ref, up_ref,
    down_ref, hist_ref, mixed_ref, gmid_ref, do_ref, small_ref, *rest,
):
    if summing:
        sums_ref, half_sum_ref, mine_ref, outmine_ref = rest[:4]
        rest = rest[4:]
    else:
        grads_ref, outg_ref = rest[:2]
        rest = rest[2:]
    (
        middle_ref, ntwo_ref, gmlp_ref, ntwot_ref, gmlpt_ref, blk_ref, gntwo_ref, og_ref, act_ref, pre_ref, gaing_ref,
        mixg_ref, gatt_ref, send, recv,
    ) = rest[:15]
    place = Place()
    core = place.core
    step = pl.program_id(0)
    rows_all, width = x_ref.shape
    block = o_ref.shape[3]
    slab = hist_ref.shape[1]
    slabs = width // LANES
    own = scale_ref[kept]
    factor = loss_factor(alllen_ref, place.batches * 2 * place.count * block)
    gain = gain_ref[...].reshape(1, width)

    def grad_top(start, count):
        s = lax.div(start, block)
        index = lax.broadcasted_iota(jnp.int32, (count, LANES), 0) + lax.rem(start, block) + place.k * block
        scale = jnp.where(index < len_ref[s], factor, 0.0)[:, :1]
        return cot_ref[pl.ds(pl.multiple_of(start, count), count), :].astype(F32) * scale

    def leave(t, u):
        s, part = t * TILE // block, t * TILE % block // TILE
        within = pl.ds(part * TILE, TILE)
        src, dst, arrival = gatt_ref.at[s, u, :, within, :], do_ref.at[place.k, :, within, :], recv.at[place.k, part]
        device = place.worker(2 * place.core + s, u)
        return place.is_me(device), remote(src, dst, send.at[t, u], arrival, device), pltpu.make_async_copy(src, dst, arrival)

    @pl.when(step == 0)
    def _():
        greet(place, (core,) if summing else ())

    if summing:
        early_ref, landing_ref, lout_ref, aside_ref, aout_ref = rest[15:20]
        xsend, xrecv = rest[20:22]
        half = swap_half(width)
        partner = (place.base + 1 - core, place.k)

        def chunk_of(unit):
            return early_ref.at[pl.ds(unit * 2 * half, 2 * half)]

        sums = Sum(place, ORDER, 2 * half, chunk_of, rest[22:26], sums_ref, 0, rest[26:])

        def cross(c):
            return remote(aside_ref.at[lax.rem(c, 2)], landing_ref.at[lax.rem(c, 4)], xsend.at[c], xrecv.at[c], partner)

        def cross_out():
            return remote(aout_ref, lout_ref, xsend.at[steps], xrecv.at[steps], partner)

        def rest_copy():
            src = early_ref.at[pl.ds(2 * LAST * half, (steps - 2 * LAST) * half)]
            return pltpu.make_async_copy(src, mine_ref, xsend.at[steps + 1])

        def hold(down, up):
            start = step * half
            for i in range(PIECE // LANES):
                rows, lanes = slice(i * width, (i + 1) * width), slice(i * LANES, (i + 1) * LANES)
                first = jnp.where(core == 0, down[:, lanes], up[:, lanes])
                other = jnp.where(core == 0, up[:, lanes], down[:, lanes])
                early_ref[pl.ds(pl.multiple_of(start + i * width, 16), width), :] = first.astype(B16)
                aside_ref[lax.rem(step, 2), rows, :] = other.astype(B16)
            cross(step).start()

        def add(c):
            landed = landing_ref.at[lax.rem(c, 4)]
            arrived(landed, xrecv.at[c])
            for i in range(PIECE // LANES):
                rows = slice(i * width, (i + 1) * width)
                into = pl.ds(pl.multiple_of(c * half + i * width, 16), width)
                early_ref[into, :] = (early_ref[into, :].astype(F32) + landed[rows, :].astype(F32)).astype(B16)

        def between(c):
            if c == 2:
                sums.scatter(0)
            if c == 4:
                sums.scatter(1)
            if c == 5:
                sums.sum(0, 0)

    @pl.when(step == 0)
    def _():
        for t in range(rows_all // TILE):
            rows = slice(t * TILE, (t + 1) * TILE)
            within = t * TILE % block
            att = slabs_of(o_ref, t * TILE // block, slice(within, within + TILE))
            middle = x_ref[rows, :].astype(F32) + dot(att, wout_ref[...])
            middle_ref[rows, :] = middle
            unit, _ = center_of(middle)
            ntwo = unit * gain
            gmlp = own * grad_top(t * TILE, TILE)
            ntwo_ref[rows, :] = ntwo.astype(B16)
            gmlp_ref[rows, :] = gmlp.astype(B16)
            ntwot_ref[:, rows] = jnp.transpose(ntwo).astype(B16)
            gmlpt_ref[:, rows] = jnp.transpose(gmlp).astype(B16)
            blk_ref[rows, :] = middle
            gntwo_ref[rows, :] = jnp.zeros((TILE, width), F32)
        mixg_ref[...] = jnp.zeros_like(mixg_ref)
        gaing_ref[...] = jnp.zeros_like(gaing_ref)
        og_ref[...] = jnp.zeros_like(og_ref)

    @pl.when(step < steps)
    def _():
        up, down = up_ref[...], down_ref[...]
        up_t, down_t = turned(up), turned(down)
        slope = math.sqrt(2.0 / math.pi)
        for t in range(rows_all // ROWS):
            rows = slice(t * ROWS, (t + 1) * ROWS)
            pre = dot(ntwo_ref[rows, :], up)
            square = pre * pre
            bent = jnp.tanh(slope * pre * (1.0 + 0.044715 * square))
            half_ = 0.5 + 0.5 * bent
            act = (pre * half_).astype(B16)
            slopes = half_ + 0.5 * slope * pre * (1.0 - bent * bent) * (1.0 + 3 * 0.044715 * square)
            pre_grad = (dot(gmlp_ref[rows, :], down_t) * slopes).astype(B16)
            act_ref[rows, :] = act
            pre_ref[rows, :] = pre_grad
            blk_ref[rows, :] += dot(act, down)
            gntwo_ref[rows, :] += dot(pre_grad, up_t)
        if summing:
            @pl.when(step >= 1)
            def _():
                add(step - 1)

            @pl.when(step >= 2)
            def _():
                cross(step - 2).wait_send()

            for c in (2, 4, 5):

                @pl.when(step == c)
                def _(c=c):
                    between(c)

    @pl.when(step == steps - 1)
    def _():
        for t in range(rows_all // TILE):
            rows = slice(t * TILE, (t + 1) * TILE)
            s, within = t * TILE // block, t * TILE % block
            top = grad_top(t * TILE, TILE)
            unit, spread = center_of(middle_ref[rows, :])
            gain_grad = gntwo_ref[rows, :]
            gaing_ref[...] += folded(gain_grad * unit)
            unit_grad = gain_grad * gain
            back = spread * (
                unit_grad
                - jnp.mean(unit_grad, -1, keepdims=True)
                - unit * jnp.mean(unit_grad * unit, -1, keepdims=True)
            )
            total = own * top + back
            gmid_ref[rows, :] = total
            att_grad = dot_nt(total.astype(B16), wout_ref[...]).astype(B16)
            at = 0
            for u in range(o_ref.shape[1]):
                for p in range(o_ref.shape[2]):
                    gatt_ref[s, u, p, within : within + TILE, :] = att_grad[:, at : at + LANES]
                    at += LANES
                mine, far, near = leave(t, u)

                @pl.when(jnp.logical_not(mine))
                def _():
                    far.start()

                @pl.when(mine)
                def _():
                    near.start()
    @pl.when(step < steps)
    def _():
        downg = dot(gmlpt_ref[...], act_ref[...])
        upg = dot(ntwot_ref[...], pre_ref[...])
        if summing:
            hold(downg, upg)
        else:
            for i in range(PIECE // LANES):
                lanes = slice(i * LANES, (i + 1) * LANES)
                grads_ref[0, i * width : (i + 1) * width, :] = downg[:, lanes].astype(B16)
                at = PIECE * slabs + i * width
                grads_ref[0, at : at + width, :] = upg[:, lanes].astype(B16)

    @pl.when(step == steps - 1)
    def _():
        for t in range(rows_all // TILE):
            rows = slice(t * TILE, (t + 1) * TILE)
            s, within = t * TILE // block, t * TILE % block
            og_ref[...] += dot_tn(slabs_of(o_ref, s, slice(within, within + TILE)), gmid_ref[rows, :].astype(B16))
        if summing:
            for i in range(slabs // 2):
                rows = slice(i * width, (i + 1) * width)
                left, right = og_ref[:, i * LANES : (i + 1) * LANES], og_ref[:, (i + slabs // 2) * LANES : (i + slabs // 2 + 1) * LANES]
                outmine_ref[rows, :] = jnp.where(core == 0, left, right).astype(B16)
                aout_ref[rows, :] = jnp.where(core == 0, right, left).astype(B16)
            cross_out().start()
        else:
            outg_ref[...] = og_ref[...].astype(B16)

    @pl.when(step >= steps)
    def _():
        start = pl.multiple_of((step - steps) * slab, slab)
        top = grad_top(start, slab)
        out = blk_ref[pl.ds(start, slab), :]
        mixed = own * out
        mixg_ref[kept] += folded(out * top)
        for j in range(kept):
            stored = hist_ref[j].astype(F32)
            mixed = mixed + scale_ref[j] * stored
            mixg_ref[j] += folded(stored * top)
        mixed_ref[...] = mixed.astype(B16)

    if summing:

        @pl.when(step == steps)
        def _():
            sums.sum(0, 1)
            sums.share(0)

        @pl.when(step == steps + 2)
        def _():
            add(jnp.int32(steps - 1))
            rest_copy().start()

        @pl.when(step == steps + 4)
        def _():
            sums.sum(1, 0, onward=False)
            half_sum_ref[...] = rest[23][1]

        @pl.when(step == steps + hist_steps - 1)
        def _():
            arrived(lout_ref, xrecv.at[steps])
            for i in range(slabs // 2):
                rows = slice(i * width, (i + 1) * width)
                outmine_ref[rows, :] = (outmine_ref[rows, :].astype(F32) + lout_ref[rows, :].astype(F32)).astype(B16)
            sums.collect(0, 1)
            sums.close(0, out=(0, 1), back=(1,))
            sums.close(1, out=(0,))
            for c in (steps - 2, steps - 1):
                cross(c).wait_send()
            rest_copy().wait()
            cross_out().wait_send()

    @pl.when(step == steps + hist_steps - 1)
    def _():
        small_ref[0:1, :] = jnp.sum(gaing_ref[...], axis=0, keepdims=True)
        for j in range(kept + 1):
            small_ref[j + 1 : j + 2, :] = jnp.sum(mixg_ref[j], axis=0, keepdims=True)
        small_ref[kept + 2 :, :] = jnp.zeros((small_ref.shape[0] - kept - 2, width), F32)
        for part in range(block // TILE):
            for j in range(place.count):
                arrived(do_ref.at[j, :, pl.ds(part * TILE, TILE), :], recv.at[j, part])
        for t in range(rows_all // TILE):
            for u in range(place.share):
                mine, far, _ = leave(t, u)

                @pl.when(jnp.logical_not(mine))
                def _():
                    far.wait_send()


def middle_part(scale, lengths, all_lengths, o, x, cot, wout, gain, up, down, hist, summing):
    rows, width = x.shape
    kept = hist.shape[0]
    inner = up.shape[1]
    steps = inner // PIECE
    hist_steps = 8
    slab = rows // hist_steps
    _, share, pairs, block, _ = o.shape
    blocks = 2 * share
    dma = pltpu.SemaphoreType.DMA
    slabs = width // LANES
    half = swap_half(width)

    def fixed(values):
        zeros = (0,) * len(values.shape)
        return pl.BlockSpec(values.shape, lambda c: zeros, pipeline_mode=pl.Buffered(1))

    def shape(dims, kind):
        return jax.ShapeDtypeStruct(dims, kind)

    hist_spec = pl.BlockSpec((kept, slab, width), lambda c: (0, jnp.maximum(c - steps, 0), 0))
    mixed_spec = pl.BlockSpec((slab, width), lambda c: (jnp.maximum(c - steps, 0), 0))
    up_spec = pl.BlockSpec((width, PIECE), lambda c: (0, jnp.minimum(c, steps - 1)))
    down_spec = pl.BlockSpec((PIECE, width), lambda c: (jnp.minimum(c, steps - 1), 0))
    gmid = shape((rows, width), F32)
    small = shape((16, width), F32)
    outs = [shape((rows, width), B16), gmid, shape((blocks, pairs, block, LANES), B16), small]
    out_specs = [mixed_spec, fixed(gmid), ANY, fixed(small)]
    scratch = [
        pltpu.VMEM((rows, width), F32),
        pltpu.VMEM((rows, width), B16),
        pltpu.VMEM((rows, width), B16),
        pltpu.VMEM((width, rows), B16),
        pltpu.VMEM((width, rows), B16),
        pltpu.VMEM((rows, width), F32),
        pltpu.VMEM((rows, width), F32),
        pltpu.VMEM(wout.shape, F32),
        pltpu.VMEM((rows, PIECE), B16),
        pltpu.VMEM((rows, PIECE), B16),
        pltpu.VMEM((8, width), F32),
        pltpu.VMEM((kept + 1, 8, width), F32),
        pltpu.VMEM(o.shape, B16),
        dma((rows // TILE, share)), dma((blocks, block // TILE)),
    ]
    if summing:
        out_rows = slabs // 2 * width
        more = [
            shape((LAST + 1, 2, 2 * half, LANES), B16), shape((half // 2, LANES), B16), shape((2 * half, LANES), B16),
            shape((out_rows, LANES), B16),
        ]
        scratch += [
            pltpu.VMEM((steps * half, LANES), B16),
            pltpu.VMEM((4, half, LANES), B16),
            pltpu.VMEM((out_rows, LANES), B16),
            pltpu.VMEM((2, half, LANES), B16),
            pltpu.VMEM((out_rows, LANES), B16),
            dma((steps + 2,)), dma((steps + 1,)),
            *sum_buffers(ORDER, LAST, 2 * half), *sum_sems(ORDER, LAST),
        ]
        outs += more
        out_specs += [ANY, fixed(more[1]), ANY, fixed(more[3])]
    else:
        outs += [shape((steps, 2 * half, LANES), B16), shape(wout.shape, B16)]
        out_specs += [pl.BlockSpec((1, 2 * half, LANES), lambda c: (jnp.minimum(c, steps - 1), 0, 0)), fixed(outs[-1])]
    return pl.pallas_call(
        functools.partial(middle_kernel, kept, steps, hist_steps, summing),
        grid=(steps + hist_steps,),
        out_shape=tuple(outs),
        in_specs=[SMEM, SMEM, fixed(all_lengths), fixed(o), fixed(x), fixed(cot), fixed(wout), fixed(gain), up_spec, down_spec, hist_spec],
        out_specs=tuple(out_specs),
        scratch_shapes=scratch,
        compiler_params=pltpu.CompilerParams(
            vmem_limit_bytes=62 * 2**20, collective_id=2, has_side_effects=True
        ),
        cost_estimate=pl.CostEstimate(flops=33 * 10**9, bytes_accessed=60 * 2**20, transcendentals=3 * 10**6),
        name="mlp_both_ways",
    )(scale, lengths, all_lengths, o, x, cot, wout, gain, up, down, hist)


def history_kernel(block, scale_ref, len_ref, alllen_ref, cot_ref, hgrad_ref):
    place = Place()
    factor = loss_factor(alllen_ref, place.batches * 2 * place.count * block)
    kept, count, _ = hgrad_ref.shape
    start = pl.program_id(1) * count + place.k * block
    index = lax.broadcasted_iota(jnp.int32, (count, LANES), 0) + start
    scale = jnp.where(index < len_ref[pl.program_id(0)], factor, 0.0)[:, :1]
    top = cot_ref[...].astype(F32) * scale
    for j in range(kept):
        hgrad_ref[j] = (scale_ref[j] * top).astype(B16)


def history_part(scale, lengths, all_lengths, cot, kept, block):
    rows, width = cot.shape
    tiles = block // TILE
    return pl.pallas_call(
        functools.partial(history_kernel, block),
        grid=(rows // block, tiles),
        out_shape=jax.ShapeDtypeStruct((kept, rows, width), B16),
        in_specs=[
            SMEM, SMEM, pl.BlockSpec(all_lengths.shape, lambda s, t: (0, 0, 0, 0)),
            pl.BlockSpec((TILE, width), lambda s, t: (s * tiles + t, 0)),
        ],
        out_specs=pl.BlockSpec((kept, TILE, width), lambda s, t: (0, s * tiles + t, 0)),
        compiler_params=pltpu.CompilerParams(vmem_limit_bytes=62 * 2**20),
        cost_estimate=pl.CostEstimate(flops=10**7, bytes_accessed=14 * 2**20, transcendentals=0),
        name="history_gradient",
    )(scale, lengths, all_lengths, cot)


def finish_kernel(x_ref, gain_ref, gmid_ref, gn_ref, out_ref):
    unit, spread = center_of(x_ref[0].astype(F32))
    unit_grad = jnp.concatenate([gn_ref[0, 0, i] for i in range(gn_ref.shape[2])], axis=1).astype(F32) * gain_ref[...]
    back = spread * (
        unit_grad - jnp.mean(unit_grad, -1, keepdims=True) - unit * jnp.mean(unit_grad * unit, -1, keepdims=True)
    )
    out_ref[0] = (gmid_ref[0] + back).astype(B16)


def finish(x, gain, gmid, gn):
    seqs, block, width = x.shape
    by_row = pl.BlockSpec((1, TILE, width), lambda s, t: (s, t, 0))
    return pl.pallas_call(
        finish_kernel,
        grid=(seqs, block // TILE),
        out_shape=jax.ShapeDtypeStruct(x.shape, B16),
        in_specs=[
            by_row,
            pl.BlockSpec(gain.shape, lambda s, t: (0, 0)),
            by_row,
            pl.BlockSpec((1, 1, width // LANES, TILE, LANES), lambda s, t: (s, t, 0, 0, 0)),
        ],
        out_specs=by_row,
        compiler_params=pltpu.CompilerParams(vmem_limit_bytes=62 * 2**20),
        name="norm_backward",
    )(x, gain, gmid, gn)


def whole_pairs(weight, heads):
    if heads % 2 == 0:
        return weight
    parted = weight.reshape(weight.shape[0], -1, heads * HD)
    return jnp.pad(parted, ((0, 0), (0, 0), (0, HD))).reshape(weight.shape[0], -1)


def body(
    tokens, history, cotangent, qkv_weight, out_weight, up_weight, down_weight, attn_gain, mlp_gain, depth_mix, lengths,
    positions,
):
    seqs, block, width = tokens.shape
    kept = history.shape[0]
    n = lax.axis_size("seq")
    batches = lax.axis_size("batch")
    place = Place()
    share = n // 2
    heads = H // share
    pairs = (heads + 1) // 2
    rows = seqs * block
    total = n * block

    wide_qkv = whole_pairs(qkv_weight, heads)
    o, att, normed, qp, kp, vp, cosine, sine, normed_t, all_lengths = attend(tokens, positions, lengths, wide_qkv, attn_gain)

    wide_out = jnp.pad(
        out_weight.reshape(share, heads * HD, width), ((0, 0), (0, (2 * pairs - heads) * HD), (0, 0))
    ).reshape(-1, width)
    summing = n == 4 and batches == 8
    hgrad = history_part(depth_mix, lengths, all_lengths, cotangent.reshape(rows, width), kept, block)
    mixed, gmid, grad, small, *parts = middle_part(
        depth_mix, lengths, all_lengths, o, tokens.reshape(rows, width), cotangent.reshape(rows, width), wide_out, mlp_gain, up_weight,
        down_weight, history.reshape(kept, rows, width), summing,
    )
    inner = up_weight.shape[1]
    slabs = width // LANES
    if summing:
        early_sums, half_sum, own_grads, own_out = parts
        sums, osums, qsums, small, input_grad = summing_back(
            qp, kp, vp, grad, att, cosine, sine, normed, normed_t, small, half_sum[None], own_grads, own_out, attn_gain, wide_qkv,
            tokens, gmid.reshape(tokens.shape), early_sums,
        )
        down_grad, up_grad, out_grad, qkv_grad = widen(sums, osums, qsums, width, inner)
    else:
        qkvg, gn, gain_part = plain_back(qp, kp, vp, grad, att, cosine, sine, normed, wide_qkv)
        slots = to_owners(gn.reshape(n, block, width), "exchange_normed_grad", 3)
        normed_grad = slots.astype(F32).sum(1).reshape(seqs, block // TILE, TILE, slabs, LANES).swapaxes(2, 3)
        small = lax.psum(small.at[-1].set(gain_part.sum(0)), ("batch", "seq"))
        mine = qkvg.reshape(width, 3, 1, 2 * pairs * HD)[..., : heads * HD]
        spread = jnp.zeros((width, 3, share, heads * HD), B16)
        spread = lax.dynamic_update_slice(spread, mine, (0, 0, place.u, 0)).reshape(width, -1)
        both, out_grad, qkv_grad = (v.astype(F32) for v in lax.psum((*parts, spread), ("batch", "seq")))
        chunks = jnp.moveaxis(both.reshape(inner // PIECE, 2, PIECE // LANES, width, LANES), 3, 1)
        down_grad = chunks[:, :, 0].swapaxes(0, 1).reshape(width, inner).T
        up_grad = chunks[:, :, 1].swapaxes(0, 1).reshape(width, inner)
        out_grad = out_grad.reshape(share, 2 * pairs * HD, width)[:, : heads * HD].reshape(H * HD, width)
        input_grad = finish(tokens, attn_gain[None, :], gmid.reshape(tokens.shape), normed_grad)
    return (
        mixed.reshape(tokens.shape),
        input_grad,
        hgrad.reshape(history.shape),
        qkv_grad,
        out_grad,
        up_grad,
        down_grad,
        small[-1] / attn_gain,
        small[0],
        small[1 : kept + 2].sum(1),
    )


def solution(mesh):
    placed = (
        P("batch", "seq", None),
        P(None, "batch", "seq", None),
        P("batch", "seq", None),
        P(),
        P(),
        P(),
        P(),
        P(),
        P(),
        P(),
        P("batch"),
        P("batch", "seq"),
    )
    return jax.shard_map(
        body,
        mesh=mesh,
        in_specs=placed,
        out_specs=(
            P("batch", "seq", None),
            P("batch", "seq", None),
            P(None, "batch", "seq", None),
            P(),
            P(),
            P(),
            P(),
            P(),
            P(),
            P(),
        ),
        check_vma=False,
    )
```
